32 devices in a mesh: seq: 8 (over z, y), dp: 4 (over x, core).
Axes of the slice: x: 2, y: 2, z: 4, core: 2. Of those that a mesh axis runs over, the one named last changes fastest.
Arguments:
- patches: bfloat16 [4, 2048, 1280], P('dp', 'seq')
- lengths: int32 [4, 8, 4], P('dp', 'seq'), may hold values from 1 to 32, 64 in all within a row
- token_dest: int32 [4, 512], P('dp', 'seq'), may hold values from 0 to 511, as said below
- gain: float32 [1280], replicated, may hold values from 0.1 to 1.9
- w_qkv: bfloat16 [1280, 3840], replicated
- w_out: bfloat16 [1280, 1280], P('seq'), may hold values from -0.15625 to 0.15625
- cotangent: bfloat16 [4, 512, 5120], P('dp', 'seq'), may hold values from -6 to 6
Outputs:
- merged: bfloat16 [4, 512, 5120], P('dp', 'seq')
- grad_patches: bfloat16 [4, 2048, 1280], P('dp', 'seq')
- grad_out_weight: float32 [1280, 1280], P('seq')
- grad_gain: float32 [1280], P('seq')
The draws below stay inside these ranges and needn't reach their ends.
Inputs may be any that keep to these rules, and one draw needn't show every extreme that they name: The lengths of a shard add up to 64. `token_dest`: A token of shard s that goes to shard d lands at a position from d*64 + s*8 to d*64 + (s+1)*8 - 1, and each of these positions receives exactly one token of shard s.
All inputs are finite; a program needn't handle non-finite values.
Results may differ from the reference program's by a relative error of at most 0.01.
Values may be sent and summed in bfloat16 or wider, within the bound.
No kernel may reach another device: no remote copies, remote signals or barrier semaphores. Data moves between devices by JAX's collectives and lax.ppermute only.
A program may use at most 128 MiB of HBM per device.

```python
import math
import jax
import jax.numpy as jnp
import numpy as np
from jax import lax

D = 1280
HEADS = 16
GROUP = 4
IMGS = 4
ROWS = 256
M_TOK = 64
PEER_TOK = 8
MOST = 32
TOTAL_ROWS = 8192
N_SEQ = 8
N_DP = 4


def draw_patches(key, part):
    key = jax.random.fold_in(key, 11)
    key_base, key_rows, key_cols = jax.random.split(key, 3)
    shape = (N_DP, N_SEQ * ROWS, D)
    row_scale = jnp.exp(jax.random.uniform(key_rows, (N_DP, N_SEQ * ROWS, 1), minval=jnp.log(0.5), maxval=jnp.log(5.0)))
    col_scale = jnp.exp(jax.random.uniform(key_cols, (1, 1, D), minval=jnp.log(0.3), maxval=jnp.log(3.0)))
    base = jnp.clip(jax.random.normal(key_base, shape), -6.0, 6.0)
    scaled = base * row_scale * col_scale
    return scaled.astype(jnp.bfloat16)


def draw_w_qkv(key, part):
    key = jax.random.fold_in(key, 23)
    key_base = jax.random.fold_in(key, 0)
    shape = (D, 3, HEADS, D // HEADS)
    base = jnp.clip(jax.random.normal(key_base, shape), -6.0, 6.0) * D ** (-0.5)
    return base.reshape(D, 3 * D).astype(jnp.bfloat16)


def draw_token_dest(key, part):
    key = jax.random.fold_in(key, 37)
    shard_keys = jax.random.split(key, N_DP * N_SEQ)
    slot_ids = jax.vmap(lambda one_key: jax.random.permutation(one_key, M_TOK))(shard_keys).astype(jnp.int32)
    shard_ids = (jnp.arange(N_DP * N_SEQ, dtype=jnp.int32) % N_SEQ)[:, None]
    targets = slot_ids // PEER_TOK * M_TOK + shard_ids * PEER_TOK + slot_ids % PEER_TOK
    return targets.reshape(N_DP, N_SEQ * M_TOK).astype(jnp.int32)


def level_of(own_key, extent, pieces, smallest, high):
    def one(position, parts):
        heights = jax.random.uniform(jax.random.fold_in(jax.random.fold_in(own_key, 6), position), (parts,), jnp.float32, smallest / len(pieces), high / len(pieces))
        return jnp.repeat(jnp.exp(heights), extent[position] // parts).reshape((-1,) + (1,) * (len(extent) - position - 1))

    level = one(*pieces[0])
    for cut in pieces[1:]:
        level = level * one(*cut)
    return level


def length_profile(count, total, limit, slope):
    portions = [(1 << 20) // math.isqrt(rank ** slope) + 1 for rank in range(2, count + 1)]
    spare, given = total - limit - (count - 1), [1] * (count - 1)
    while spare > 0:
        free = [i for i in range(count - 1) if given[i] < limit]
        pool, remaining = sum([portions[i] for i in free]), spare
        for i in free:
            addition = min(limit - given[i], max(1, remaining * portions[i] // pool), spare)
            given[i] = given[i] + addition
            spare = spare - addition
    return np.array([limit] + given)


def ragged(key, number_of, total, reach, skew):
    if number_of == 2:
        one = jax.random.randint(key, (), max(1, total - reach), min(reach, total - 1) + 1)
        return jnp.stack([one, total - one])
    sizes = jnp.asarray(length_profile(number_of, total, reach, skew), jnp.int32)
    twos = (number_of - 1) // 2
    donor, receiver = sizes[1:1 + 2 * twos:2], sizes[2:2 + 2 * twos:2]
    margin = jnp.minimum(donor - 1, reach - receiver)
    shifted = jax.random.randint(jax.random.fold_in(key, 1), (twos,), 0, 1 << 20) % (margin + 1)
    sizes = sizes.at[1:1 + 2 * twos:2].set(donor - shifted).at[2:2 + 2 * twos:2].set(receiver + shifted)
    return sizes[jax.random.permutation(jax.random.fold_in(key, 2), number_of)]


def gaussian(stream_key, shape, deviation, bound, cuts=(), kind=jnp.bfloat16):
    values = jax.random.normal(stream_key, shape, jnp.float32) * deviation
    if len(cuts) > 0:
        values = level_of(stream_key, shape, cuts, -0.22, 0.18) * values
    return jnp.clip(values, min=-bound, max=bound).astype(kind)


def setup_inputs(seed: int = 0) -> dict:
    splits = jax.random.split(jax.random.key(seed), 8)
    return {
        "patches": draw_patches(jax.random.fold_in(splits[7], 71), 0),
        "lengths": jax.vmap(lambda own: ragged(own, IMGS, M_TOK, MOST, 2))(jax.random.split(splits[1], N_DP * N_SEQ)).reshape((N_DP, N_SEQ, IMGS)).astype(jnp.int32),
        "token_dest": draw_token_dest(jax.random.fold_in(splits[7], 71), 0),
        "gain": jnp.clip(1.0 + 0.18 * jax.random.normal(splits[3], (D,), jnp.float32), 0.1, 1.9),
        "w_qkv": draw_w_qkv(jax.random.fold_in(splits[7], 71), 0),
        "w_out": gaussian(splits[5], (D, D), D ** -0.5, 0.15625, ((0, 8),)),
        "cotangent": gaussian(splits[6], (N_DP, N_SEQ * M_TOK, GROUP * D), 1.0, 6.0, ((0, 4), (1, 8))),
    }


eps = 1e-06

def image_mask(shard_lengths, row_count):
    image_ends = jnp.cumsum(shard_lengths.astype(jnp.int32) * GROUP).astype(jnp.int32)
    row_index = jnp.arange(row_count, dtype=jnp.int32)
    image_ids = lax.optimization_barrier(jnp.sum((row_index[:, None] >= image_ends[None, :]).astype(jnp.int32), axis=1))
    return image_ids[:, None] == image_ids[None, :]

def forward(patch_rows, shard_lengths, gain, w_qkv, w_out):
    row_count, model_width = patch_rows.shape
    head_size = model_width // HEADS
    score_scale = 1.0 / math.sqrt(head_size)
    wide_rows = patch_rows.astype(jnp.float32)
    centred = wide_rows - lax.optimization_barrier(jnp.mean(wide_rows, axis=-1, keepdims=True))
    inv_spread = lax.rsqrt(lax.optimization_barrier(jnp.mean(centred * centred, axis=-1, keepdims=True)) + eps)
    standard = centred * inv_spread
    normed = (standard * gain).astype(jnp.bfloat16)
    projected = jnp.dot(normed, w_qkv, preferred_element_type=jnp.float32).astype(jnp.bfloat16)
    queries = projected[:, :model_width].reshape(row_count, HEADS, head_size)
    key_rows = projected[:, model_width:2 * model_width].reshape(row_count, HEADS, head_size)
    value_rows = projected[:, 2 * model_width:].reshape(row_count, HEADS, head_size)
    scores = jnp.einsum('qhe,khe->hqk', queries.astype(jnp.float32), key_rows.astype(jnp.float32)) * score_scale
    same_image = image_mask(shard_lengths, row_count)
    scores = jnp.where(same_image[None], scores, -jnp.inf)
    row_max = lax.optimization_barrier(jnp.max(scores, axis=-1, keepdims=True))
    weights_exp = jnp.exp(scores - row_max)
    probs = weights_exp / lax.optimization_barrier(jnp.sum(weights_exp, axis=-1, keepdims=True))
    probs_low = probs.astype(jnp.bfloat16)
    attended = jnp.einsum('hqk,khe->qhe', probs_low.astype(jnp.float32), value_rows.astype(jnp.float32))
    attended = attended.astype(jnp.bfloat16).reshape(row_count, model_width)
    branch = jnp.dot(attended, w_out, preferred_element_type=jnp.float32)
    block = (wide_rows + branch).astype(jnp.bfloat16)
    return (block, (standard, inv_spread, queries, key_rows, value_rows, probs, probs_low, attended))

def backward(saved, block_grad, gain, w_qkv, w_out):
    standard, inv_spread, queries, key_rows, value_rows, probs, probs_low, attended = saved
    row_count, model_width = block_grad.shape
    head_size = model_width // HEADS
    score_scale = 1.0 / math.sqrt(head_size)
    incoming = block_grad.astype(jnp.float32)
    weight_grad = lax.dot_general(attended, block_grad, (((0,), (0,)), ((), ())), preferred_element_type=jnp.float32)
    grad_attended = lax.dot_general(block_grad, w_out, (((1,), (1,)), ((), ())), preferred_element_type=jnp.float32)
    grad_attended = grad_attended.astype(jnp.bfloat16).reshape(row_count, HEADS, head_size)
    grad_probs = jnp.einsum('qhe,khe->hqk', grad_attended.astype(jnp.float32), value_rows.astype(jnp.float32))
    grad_values = jnp.einsum('hqk,qhe->khe', probs_low.astype(jnp.float32), grad_attended.astype(jnp.float32)).astype(jnp.bfloat16)
    grad_scores = probs * (grad_probs - lax.optimization_barrier(jnp.sum(grad_probs * probs, axis=-1, keepdims=True))) * score_scale
    grad_scores = grad_scores.astype(jnp.bfloat16)
    grad_queries = jnp.einsum('hqk,khe->qhe', grad_scores.astype(jnp.float32), key_rows.astype(jnp.float32)).astype(jnp.bfloat16)
    grad_keys = jnp.einsum('hqk,qhe->khe', grad_scores.astype(jnp.float32), queries.astype(jnp.float32)).astype(jnp.bfloat16)
    grad_projected = jnp.concatenate([grad_queries.reshape(row_count, model_width), grad_keys.reshape(row_count, model_width), grad_values.reshape(row_count, model_width)], axis=1)
    grad_normed = lax.dot_general(grad_projected, w_qkv, (((1,), (1,)), ((), ())), preferred_element_type=jnp.float32)
    gain_grad = lax.optimization_barrier(jnp.sum(grad_normed * standard, axis=0))
    grad_standard = grad_normed * gain
    grad_branch = inv_spread * (grad_standard - lax.optimization_barrier(jnp.mean(grad_standard, axis=-1, keepdims=True)) - standard * lax.optimization_barrier(jnp.mean(grad_standard * standard, axis=-1, keepdims=True)))
    patch_grad = (incoming + grad_branch).astype(jnp.bfloat16)
    return (patch_grad, weight_grad, gain_grad)

def reference(patches, lengths, token_dest, gain, w_qkv, w_out, cotangent):
    shard_count = N_DP * N_SEQ
    patch_blocks = patches.reshape(shard_count, ROWS, D)
    length_blocks = lengths.reshape(shard_count, IMGS)
    routed = jax.vmap(lambda grads, where: jnp.take(grads, where, axis=0))(cotangent, token_dest)
    grad_blocks = routed.reshape(shard_count, ROWS, D)

    def step(carry, inputs):
        weight_sum, gain_sum = carry
        patch_rows, shard_lengths, block_grad = inputs
        block, saved = forward(patch_rows, shard_lengths, gain, w_qkv, w_out)
        patch_grad, weight_grad, gain_grad = backward(saved, block_grad, gain, w_qkv, w_out)
        return ((weight_sum + weight_grad, gain_sum + gain_grad), (block, patch_grad))
    start = (jnp.zeros((D, D), jnp.float32), jnp.zeros((D,), jnp.float32))
    (weight_sum, gain_sum), (blocks, patch_grads) = lax.scan(step, start, (patch_blocks, length_blocks, grad_blocks))
    tokens = blocks.reshape(N_DP, N_SEQ * M_TOK, GROUP * D)
    merged = jax.vmap(lambda rows_in, where: jnp.zeros_like(rows_in).at[where].set(rows_in))(tokens, token_dest)
    grad_patches = patch_grads.reshape(N_DP, N_SEQ * ROWS, D)
    norm_scale = 1.0 / math.sqrt(TOTAL_ROWS)
    return (merged, grad_patches, weight_sum * norm_scale, gain_sum * norm_scale)
```

```python
import math

import jax
import jax.numpy as jnp
from jax import lax
from jax.sharding import PartitionSpec as P

HEADS = 16
GROUP = 4


eps = 1e-06


def image_mask(shard_lengths, row_count):
    image_ends = jnp.cumsum(shard_lengths * GROUP)
    row_index = jnp.arange(row_count, dtype=jnp.int32)
    image_ids = jnp.sum((row_index[:, None] >= image_ends[None, :]).astype(jnp.int32), axis=1)
    return image_ids[:, None] == image_ids[None, :]


def forward(patch_rows, shard_lengths, gain, w_qkv, w_out):
    row_count, model_width = patch_rows.shape
    head_size = model_width // HEADS
    score_scale = 1.0 / math.sqrt(head_size)
    wide_rows = patch_rows.astype(jnp.float32)
    centred = wide_rows - jnp.mean(wide_rows, axis=-1, keepdims=True)
    inv_spread = lax.rsqrt(jnp.mean(centred * centred, axis=-1, keepdims=True) + eps)
    standard = centred * inv_spread
    normed = (standard * gain).astype(jnp.bfloat16)
    projected = jnp.dot(normed, w_qkv, preferred_element_type=jnp.float32).astype(jnp.bfloat16)
    queries = projected[:, :model_width].reshape(row_count, HEADS, head_size)
    key_rows = projected[:, model_width : 2 * model_width].reshape(row_count, HEADS, head_size)
    value_rows = projected[:, 2 * model_width :].reshape(row_count, HEADS, head_size)
    scores = (
        jnp.einsum("qhe,khe->hqk", queries, key_rows, preferred_element_type=jnp.float32)
        * score_scale
    )
    same_image = image_mask(shard_lengths, row_count)
    scores = jnp.where(same_image[None], scores, -jnp.inf)
    row_max = jnp.max(scores, axis=-1, keepdims=True)
    weights_exp = jnp.exp(scores - row_max)
    probs = weights_exp / jnp.sum(weights_exp, axis=-1, keepdims=True)
    probs_low = probs.astype(jnp.bfloat16)
    attended = jnp.einsum("hqk,khe->qhe", probs_low, value_rows, preferred_element_type=jnp.float32)
    attended = attended.astype(jnp.bfloat16).reshape(row_count, model_width)
    branch = jnp.dot(attended, w_out, preferred_element_type=jnp.float32)
    block = (wide_rows + branch).astype(jnp.bfloat16)
    return (
        block,
        (standard, inv_spread, queries, key_rows, value_rows, probs, probs_low, attended),
    )


def backward(saved, block_grad, gain, w_qkv, w_out):
    standard, inv_spread, queries, key_rows, value_rows, probs, probs_low, attended = saved
    row_count, model_width = block_grad.shape
    head_size = model_width // HEADS
    score_scale = 1.0 / math.sqrt(head_size)
    incoming = block_grad.astype(jnp.float32)
    weight_grad = lax.dot_general(
        attended, block_grad, (((0,), (0,)), ((), ())), preferred_element_type=jnp.float32
    )
    grad_attended = lax.dot_general(
        block_grad, w_out, (((1,), (1,)), ((), ())), preferred_element_type=jnp.float32
    )
    grad_attended = grad_attended.astype(jnp.bfloat16).reshape(row_count, HEADS, head_size)
    grad_probs = jnp.einsum(
        "qhe,khe->hqk", grad_attended, value_rows, preferred_element_type=jnp.float32
    )
    grad_values = jnp.einsum(
        "hqk,qhe->khe", probs_low, grad_attended, preferred_element_type=jnp.float32
    ).astype(jnp.bfloat16)
    grad_scores = (
        probs * (grad_probs - jnp.sum(grad_probs * probs, axis=-1, keepdims=True)) * score_scale
    )
    grad_scores = grad_scores.astype(jnp.bfloat16)
    grad_queries = jnp.einsum(
        "hqk,khe->qhe", grad_scores, key_rows, preferred_element_type=jnp.float32
    ).astype(jnp.bfloat16)
    grad_keys = jnp.einsum(
        "hqk,qhe->khe", grad_scores, queries, preferred_element_type=jnp.float32
    ).astype(jnp.bfloat16)
    grad_projected = jnp.concatenate(
        [
            grad_queries.reshape(row_count, model_width),
            grad_keys.reshape(row_count, model_width),
            grad_values.reshape(row_count, model_width),
        ],
        axis=1,
    )
    grad_normed = lax.dot_general(
        grad_projected, w_qkv, (((1,), (1,)), ((), ())), preferred_element_type=jnp.float32
    )
    gain_grad = jnp.sum(grad_normed * standard, axis=0)
    grad_standard = grad_normed * gain
    grad_branch = inv_spread * (
        grad_standard
        - jnp.mean(grad_standard, axis=-1, keepdims=True)
        - standard * jnp.mean(grad_standard * standard, axis=-1, keepdims=True)
    )
    patch_grad = (incoming + grad_branch).astype(jnp.bfloat16)
    return (patch_grad, weight_grad, gain_grad)


def partner_swap(value, dp_count):
    pairs = [(i, i ^ 1) for i in range(dp_count)]
    return lax.ppermute(value, "dp", pairs)


def gather_out(w_out, seq_count, dp_count, parity):
    share, model_width = w_out.shape
    half = share // 2
    mine = lax.dynamic_slice_in_dim(w_out, parity * half, half, 0)
    spread = jnp.broadcast_to(mine[None], (seq_count, half, model_width))
    held = lax.all_to_all(spread, "seq", split_axis=0, concat_axis=0, tiled=True)
    other = partner_swap(held, dp_count)
    lower = jnp.where(parity == 0, held, other)
    upper = jnp.where(parity == 0, other, held)
    return jnp.concatenate([lower[:, None], upper[:, None]], axis=1).reshape(
        seq_count * share, model_width
    )


def reduce_weight(weight_grad, seq_count, dp_count, parity):
    model_width = weight_grad.shape[1]
    share = model_width // seq_count
    half = share // 2
    parts = weight_grad.reshape(seq_count, 2, half, model_width)
    away = lax.dynamic_index_in_dim(parts, 1 - parity, 1, keepdims=False).astype(jnp.bfloat16)
    own = lax.dynamic_index_in_dim(parts, parity, 1, keepdims=False)
    pair_sum = (own + partner_swap(away, dp_count).astype(jnp.float32)).astype(jnp.bfloat16)
    arrived = lax.all_to_all(pair_sum, "seq", split_axis=0, concat_axis=0, tiled=True)
    chip_sum = jnp.sum(arrived.astype(jnp.float32), axis=0).astype(jnp.bfloat16)
    spread = jnp.broadcast_to(chip_sum[None], (dp_count, half, model_width))
    halves = lax.all_to_all(spread, "dp", split_axis=0, concat_axis=0, tiled=True)
    halves = halves.astype(jnp.float32).reshape(dp_count // 2, 2, half, model_width)
    return jnp.sum(halves, axis=0).reshape(share, model_width)


def reduce_gain(gain_grad, seq_count, dp_count):
    share = gain_grad.shape[0] // seq_count
    spread = jnp.broadcast_to(
        gain_grad.reshape(seq_count, 1, share), (seq_count, dp_count, share)
    ).reshape(seq_count * dp_count, share)
    arrived = lax.all_to_all(spread, ("seq", "dp"), split_axis=0, concat_axis=0, tiled=True)
    return jnp.sum(arrived, axis=0)


def per_device(patches, lengths, token_dest, gain, w_qkv, w_out, cotangent):
    seq_count = lax.axis_size("seq")
    dp_count = lax.axis_size("dp")
    parity = lax.axis_index("dp") % 2
    returned = lax.all_to_all(cotangent[0], "seq", split_axis=0, concat_axis=0, tiled=True)
    full_out = gather_out(w_out, seq_count, dp_count, parity)
    patch_rows = patches[0]
    row_count, model_width = patch_rows.shape
    block, saved = forward(patch_rows, lengths[0, 0], gain, w_qkv, full_out)
    token_count = row_count // GROUP
    peer_count = token_count // seq_count
    tokens = block.reshape(token_count, GROUP * model_width)
    targets = token_dest[0]
    slot_ids = targets // token_count * peer_count + targets % peer_count
    placing = (slot_ids[:, None] == jnp.arange(token_count, dtype=jnp.int32)[None, :]).astype(
        jnp.bfloat16
    )
    outgoing = lax.dot_general(
        placing, tokens, (((0,), (0,)), ((), ())), preferred_element_type=jnp.float32
    ).astype(jnp.bfloat16)
    merged = lax.all_to_all(outgoing, "seq", split_axis=0, concat_axis=0, tiled=True)
    token_grad = jnp.dot(placing, returned, preferred_element_type=jnp.float32).astype(jnp.bfloat16)
    block_grad = token_grad.reshape(row_count, model_width)
    patch_grad, weight_grad, gain_grad = backward(saved, block_grad, gain, w_qkv, full_out)
    own_weight = reduce_weight(weight_grad, seq_count, dp_count, parity)
    own_gain = reduce_gain(gain_grad, seq_count, dp_count)
    norm_scale = 1.0 / math.sqrt(row_count * seq_count * dp_count)
    return (merged[None], patch_grad[None], own_weight * norm_scale, own_gain * norm_scale)


def solution(mesh):
    placed = (
        P("dp", "seq", None),
        P("dp", "seq", None),
        P("dp", "seq"),
        P(),
        P(),
        P("seq", None),
        P("dp", "seq", None),
    )
    return jax.shard_map(
        per_device,
        mesh=mesh,
        in_specs=placed,
        out_specs=(P("dp", "seq", None), P("dp", "seq", None), P("seq", None), P("seq")),
        check_vma=False,
    )
```

```python
import functools
import math

import jax
import jax.numpy as jnp
from jax import lax
from jax.sharding import PartitionSpec as P

HEADS = 16
GROUP = 4


eps = 1e-06


def image_mask(shard_lengths, row_count):
    image_ends = jnp.cumsum(shard_lengths * GROUP)
    row_index = jnp.arange(row_count, dtype=jnp.int32)
    image_ids = jnp.sum((row_index[:, None] >= image_ends[None, :]).astype(jnp.int32), axis=1)
    return image_ids[:, None] == image_ids[None, :]


def forward(patch_rows, shard_lengths, gain, w_qkv, w_out):
    row_count, model_width = patch_rows.shape
    head_size = model_width // HEADS
    score_scale = 1.0 / math.sqrt(head_size)
    wide_rows = patch_rows.astype(jnp.float32)
    centred = wide_rows - jnp.mean(wide_rows, axis=-1, keepdims=True)
    inv_spread = lax.rsqrt(jnp.mean(centred * centred, axis=-1, keepdims=True) + eps)
    standard = centred * inv_spread
    normed = (standard * gain).astype(jnp.bfloat16)
    projected = jnp.dot(normed, w_qkv, preferred_element_type=jnp.float32).astype(jnp.bfloat16)
    queries = projected[:, :model_width].reshape(row_count, HEADS, head_size)
    key_rows = projected[:, model_width : 2 * model_width].reshape(row_count, HEADS, head_size)
    value_rows = projected[:, 2 * model_width :].reshape(row_count, HEADS, head_size)
    scores = (
        jnp.einsum("qhe,khe->hqk", queries, key_rows, preferred_element_type=jnp.float32)
        * score_scale
    )
    same_image = image_mask(shard_lengths, row_count)
    scores = jnp.where(same_image[None], scores, -jnp.inf)
    row_max = jnp.max(scores, axis=-1, keepdims=True)
    weights_exp = jnp.exp(scores - row_max)
    probs = weights_exp / jnp.sum(weights_exp, axis=-1, keepdims=True)
    probs_low = probs.astype(jnp.bfloat16)
    attended = jnp.einsum("hqk,khe->qhe", probs_low, value_rows, preferred_element_type=jnp.float32)
    attended = attended.astype(jnp.bfloat16).reshape(row_count, model_width)
    branch = jnp.dot(attended, w_out, preferred_element_type=jnp.float32)
    block = (wide_rows + branch).astype(jnp.bfloat16)
    return (
        block,
        (standard, inv_spread, queries, key_rows, value_rows, probs, probs_low, attended),
    )


def backward(saved, block_grad, gain, w_qkv, w_out):
    standard, inv_spread, queries, key_rows, value_rows, probs, probs_low, attended = saved
    row_count, model_width = block_grad.shape
    head_size = model_width // HEADS
    score_scale = 1.0 / math.sqrt(head_size)
    incoming = block_grad.astype(jnp.float32)
    weight_grad = lax.dot_general(
        attended, block_grad, (((0,), (0,)), ((), ())), preferred_element_type=jnp.float32
    )
    grad_attended = lax.dot_general(
        block_grad, w_out, (((1,), (1,)), ((), ())), preferred_element_type=jnp.float32
    )
    grad_attended = grad_attended.astype(jnp.bfloat16).reshape(row_count, HEADS, head_size)
    grad_probs = jnp.einsum(
        "qhe,khe->hqk", grad_attended, value_rows, preferred_element_type=jnp.float32
    )
    grad_values = jnp.einsum(
        "hqk,qhe->khe", probs_low, grad_attended, preferred_element_type=jnp.float32
    ).astype(jnp.bfloat16)
    grad_scores = (
        probs * (grad_probs - jnp.sum(grad_probs * probs, axis=-1, keepdims=True)) * score_scale
    )
    grad_scores = grad_scores.astype(jnp.bfloat16)
    grad_queries = jnp.einsum(
        "hqk,khe->qhe", grad_scores, key_rows, preferred_element_type=jnp.float32
    ).astype(jnp.bfloat16)
    grad_keys = jnp.einsum(
        "hqk,qhe->khe", grad_scores, queries, preferred_element_type=jnp.float32
    ).astype(jnp.bfloat16)
    grad_projected = jnp.concatenate(
        [
            grad_queries.reshape(row_count, model_width),
            grad_keys.reshape(row_count, model_width),
            grad_values.reshape(row_count, model_width),
        ],
        axis=1,
    )
    grad_normed = lax.dot_general(
        grad_projected, w_qkv, (((1,), (1,)), ((), ())), preferred_element_type=jnp.float32
    )
    gain_grad = jnp.sum(grad_normed * standard, axis=0)
    grad_standard = grad_normed * gain
    grad_branch = inv_spread * (
        grad_standard
        - jnp.mean(grad_standard, axis=-1, keepdims=True)
        - standard * jnp.mean(grad_standard * standard, axis=-1, keepdims=True)
    )
    patch_grad = (incoming + grad_branch).astype(jnp.bfloat16)
    return (patch_grad, weight_grad, gain_grad)


def joint_permute(value, seq_count, dp_count, target):
    pairs = []
    for s in range(seq_count):
        for d in range(dp_count):
            to_s, to_d = target(s, d)
            pairs.append((s * dp_count + d, to_s * dp_count + to_d))
    return lax.ppermute(value, ("seq", "dp"), pairs)


def core_target(s, d):
    return s, d ^ 1


def first_target(s, d):
    return (s, d ^ 2) if d % 2 == 0 else (s ^ 1, d)


def second_target(s, d):
    return (s ^ 1, d) if d % 2 == 0 else (s, d ^ 2)


def far_target(step):
    return lambda s, d: (s ^ (2 * step), d)


def gather_out(w_out, seq_count, dp_count):
    share, model_width = w_out.shape
    rows, cols = share // 2, model_width // 2
    s, d = lax.axis_index("seq"), lax.axis_index("dp")
    core, x_bit, y_bit, z_index = d % 2, d // 2, s % 2, s // 2
    far_count = seq_count // 2
    send = functools.partial(joint_permute, seq_count=seq_count, dp_count=dp_count)
    own = lax.dynamic_slice(w_out, (x_bit * rows, core * cols), (rows, cols))
    level = jnp.stack(
        [own] + [send(own, target=far_target(step)) for step in range(1, far_count)]
    )
    near = send(level, target=second_target)
    held = [level, near, send(level, target=first_target), send(near, target=first_target)]
    held = [jnp.stack(held), jnp.stack([send(one, target=core_target) for one in held])]
    held = jnp.stack(held)
    columns = []
    for c in range(2):
        side = lax.dynamic_index_in_dim(held, c ^ core, 0, keepdims=False)
        blocks = []
        for z in range(far_count):
            for y in range(2):
                for x in range(2):
                    y_off, x_off = y ^ y_bit, x ^ x_bit
                    place = jnp.where(c == 0, y_off + 2 * x_off, x_off + 2 * y_off)
                    piece = lax.dynamic_slice(
                        side, (place, z ^ z_index, 0, 0), (1, 1, rows, cols)
                    )
                    blocks.append(piece[0, 0])
        columns.append(jnp.concatenate(blocks, axis=0))
    return jnp.concatenate(columns, axis=1)


def reduce_weight(weight_grad, seq_count, dp_count):
    model_width = weight_grad.shape[1]
    share = model_width // seq_count
    rows, cols = share // 2, model_width // 2
    s, d = lax.axis_index("seq"), lax.axis_index("dp")
    core, x_bit, y_bit, z_index = d % 2, d // 2, s % 2, s // 2
    far_count = seq_count // 2
    send = functools.partial(joint_permute, seq_count=seq_count, dp_count=dp_count)
    low = jnp.bfloat16
    away = lax.dynamic_slice(weight_grad, (0, (1 - core) * cols), (model_width, cols))
    own = lax.dynamic_slice(weight_grad, (0, core * cols), (model_width, cols))
    chip = own + send(away.astype(low), target=core_target).astype(jnp.float32)
    chip = chip.astype(low).reshape(far_count, 2, 2, rows, cols)
    ordered = []
    for first in range(2):
        for second in range(2):
            y = y_bit ^ jnp.where(core == 0, second, first)
            x = x_bit ^ jnp.where(core == 0, first, second)
            ordered.append(
                lax.dynamic_slice(chip, (0, y, x, 0, 0), (far_count, 1, 1, rows, cols))[:, 0, 0]
            )
    kept = jnp.stack(ordered[:2])
    arrived = send(jnp.stack(ordered[2:]), target=first_target)
    kept = (kept.astype(jnp.float32) + arrived.astype(jnp.float32)).astype(low)
    arrived = send(kept[1], target=second_target)
    level = (kept[0].astype(jnp.float32) + arrived.astype(jnp.float32)).astype(low)
    total = lax.dynamic_index_in_dim(level, z_index, 0, keepdims=False).astype(jnp.float32)
    for step in range(1, far_count):
        piece = lax.dynamic_index_in_dim(level, z_index ^ step, 0, keepdims=False)
        total = total + send(piece, target=far_target(step)).astype(jnp.float32)
    spread = jnp.broadcast_to(total.astype(low)[None], (dp_count, rows, cols))
    blocks = lax.all_to_all(spread, "dp", split_axis=0, concat_axis=0, tiled=True)
    blocks = blocks.astype(jnp.float32).reshape(2, 2, rows, cols)
    return blocks.transpose(0, 2, 1, 3).reshape(share, model_width)


def reduce_gain(gain_grad, seq_count, dp_count):
    share = gain_grad.shape[0] // seq_count
    spread = jnp.broadcast_to(
        gain_grad.reshape(seq_count, 1, share), (seq_count, dp_count, share)
    ).reshape(seq_count * dp_count, share)
    arrived = lax.all_to_all(spread, ("seq", "dp"), split_axis=0, concat_axis=0, tiled=True)
    return jnp.sum(arrived, axis=0)


def per_device(patches, lengths, token_dest, gain, w_qkv, w_out, cotangent):
    seq_count = lax.axis_size("seq")
    dp_count = lax.axis_size("dp")
    returned = lax.all_to_all(cotangent[0], "seq", split_axis=0, concat_axis=0, tiled=True)
    full_out = gather_out(w_out, seq_count, dp_count)
    patch_rows = patches[0]
    row_count, model_width = patch_rows.shape
    block, saved = forward(patch_rows, lengths[0, 0], gain, w_qkv, full_out)
    token_count = row_count // GROUP
    peer_count = token_count // seq_count
    tokens = block.reshape(token_count, GROUP * model_width)
    targets = token_dest[0]
    slot_ids = targets // token_count * peer_count + targets % peer_count
    placing = (slot_ids[:, None] == jnp.arange(token_count, dtype=jnp.int32)[None, :]).astype(
        jnp.bfloat16
    )
    outgoing = lax.dot_general(
        placing, tokens, (((0,), (0,)), ((), ())), preferred_element_type=jnp.float32
    ).astype(jnp.bfloat16)
    merged = lax.all_to_all(outgoing, "seq", split_axis=0, concat_axis=0, tiled=True)
    token_grad = jnp.dot(placing, returned, preferred_element_type=jnp.float32).astype(jnp.bfloat16)
    block_grad = token_grad.reshape(row_count, model_width)
    patch_grad, weight_grad, gain_grad = backward(saved, block_grad, gain, w_qkv, full_out)
    own_weight = reduce_weight(weight_grad, seq_count, dp_count)
    own_gain = reduce_gain(gain_grad, seq_count, dp_count)
    norm_scale = 1.0 / math.sqrt(row_count * seq_count * dp_count)
    return (merged[None], patch_grad[None], own_weight * norm_scale, own_gain * norm_scale)


def solution(mesh):
    placed = (
        P("dp", "seq", None),
        P("dp", "seq", None),
        P("dp", "seq"),
        P(),
        P(),
        P("seq", None),
        P("dp", "seq", None),
    )
    return jax.shard_map(
        per_device,
        mesh=mesh,
        in_specs=placed,
        out_specs=(P("dp", "seq", None), P("dp", "seq", None), P("seq", None), P("seq")),
        check_vma=False,
    )
```

```python
import functools
import math

import jax
import jax.numpy as jnp
from jax import lax
from jax.experimental import pallas as pl
from jax.experimental.pallas import tpu as pltpu
from jax.sharding import PartitionSpec as P

HEADS = 16
GROUP = 4
HALVES = 2
LANES = 128
VMEM_LIMIT = 56 * 1024 * 1024

eps = 1e-06
low = jnp.bfloat16
wide = jnp.float32


def params():
    return pltpu.CompilerParams(vmem_limit_bytes=VMEM_LIMIT)


def smem():
    return pl.BlockSpec(memory_space=pltpu.SMEM)


def vmem():
    return pl.BlockSpec(memory_space=pltpu.VMEM)


def dot_nt(left, right):
    return lax.dot_general(left, right, (((1,), (1,)), ((), ())), preferred_element_type=wide)


def dot_tn(left, right):
    return lax.dot_general(left, right, (((0,), (0,)), ((), ())), preferred_element_type=wide)


def dot_nn(left, right):
    return jnp.dot(left, right, preferred_element_type=wide)


def head_windows(head_size, width):
    windows = []
    for start in range(0, width, head_size):
        first = start // LANES * LANES
        last = -(-(start + head_size) // LANES) * LANES
        windows.append((first, last, start - first, start - first + head_size))
    return windows


def image_bias(lengths_ref, row_count):
    def image_of(index):
        number = jnp.zeros(index.shape, jnp.int32)
        end = jnp.int32(0)
        for image in range(lengths_ref.shape[0]):
            end = end + lengths_ref[image] * GROUP
            number = number + (index >= end).astype(jnp.int32)
        return number

    rows = lax.broadcasted_iota(jnp.int32, (row_count, row_count), 0)
    cols = lax.broadcasted_iota(jnp.int32, (row_count, row_count), 1)
    return jnp.where(image_of(rows) == image_of(cols), 0.0, -jnp.inf).astype(wide)


def standardise(rows):
    centred = rows - jnp.mean(rows, axis=-1, keepdims=True)
    inv_spread = lax.rsqrt(jnp.mean(centred * centred, axis=-1, keepdims=True) + eps)
    return centred * inv_spread, inv_spread


def only(window, value):
    lane = lax.broadcasted_iota(jnp.int32, value.shape, 1)
    keep = (lane >= window[2]) & (lane < window[3])
    return jnp.where(keep, value, jnp.zeros_like(value))


def forward_kernel(
    score_scale, windows, lengths_ref, x_ref, gain_ref, w_ref,
    proj_ref, att_ref, lse_ref, normed, qkv, bias, acc,
):
    step = pl.program_id(0)
    kind, half = lax.rem(step, 3), lax.div(step, 3)

    @pl.when(step == 0)
    def _():
        standard, _ = standardise(x_ref[...].astype(wide))
        normed[...] = (standard * gain_ref[...]).astype(low)
        bias[...] = image_bias(lengths_ref, x_ref.shape[0])
        lse_ref[...] = jnp.zeros_like(lse_ref)

    block = dot_nn(normed[...], w_ref[...]).astype(low)
    proj_ref[...] = block
    qkv[kind] = block

    @pl.when(kind == 2)
    def _():
        acc[...] = jnp.zeros_like(acc)
        lane = lax.broadcasted_iota(jnp.int32, lse_ref.shape, 1)
        for head, window in enumerate(windows):
            cols = slice(window[0], window[1])
            queries = only(window, qkv[0, :, cols])
            scores = dot_nt(queries, qkv[1, :, cols]) * score_scale + bias[...]
            row_max = jnp.max(scores, axis=-1, keepdims=True)
            weights = jnp.exp(scores - row_max)
            total = jnp.sum(weights, axis=-1, keepdims=True)
            probs = (weights * (1.0 / total)).astype(low)
            values = only(window, qkv[2, :, cols])
            acc[:, cols] += dot_nn(probs, values)
            place = half * len(windows) + head
            lse_ref[...] = jnp.where(lane == place, row_max + jnp.log(total), lse_ref[...])
        att_ref[...] = acc[...].astype(low)


def forward(patch_rows, shard_lengths, gain, w_qkv):
    row_count, model_width = patch_rows.shape
    half_width = model_width // HALVES
    windows = head_windows(model_width // HEADS, half_width)
    kernel = functools.partial(
        forward_kernel, 1.0 / math.sqrt(model_width // HEADS), windows
    )
    block = lambda step: (0, lax.rem(step, 3) * HALVES + lax.div(step, 3))
    whole = lambda step: (0, 0)
    return pl.pallas_call(
        kernel,
        grid=(3 * HALVES,),
        in_specs=[
            smem(),
            pl.BlockSpec((row_count, model_width), whole),
            pl.BlockSpec((1, model_width), whole),
            pl.BlockSpec((model_width, half_width), block),
        ],
        out_specs=[
            pl.BlockSpec((row_count, half_width), block),
            pl.BlockSpec((row_count, half_width), lambda step: (0, lax.div(step, 3))),
            pl.BlockSpec((row_count, LANES), whole),
        ],
        out_shape=[
            jax.ShapeDtypeStruct((row_count, 3 * model_width), low),
            jax.ShapeDtypeStruct((row_count, model_width), low),
            jax.ShapeDtypeStruct((row_count, LANES), wide),
        ],
        scratch_shapes=[
            pltpu.VMEM((row_count, model_width), low),
            pltpu.VMEM((3, row_count, half_width), low),
            pltpu.VMEM((row_count, row_count), wide),
            pltpu.VMEM((row_count, half_width), wide),
        ],
        compiler_params=params(),
        name="forward",
    )(shard_lengths, patch_rows, gain[None], w_qkv)


def backward_kernel(
    score_scale, windows, lengths_ref, x_ref, gain_ref, w_ref, q_ref, k_ref, v_ref,
    ga_ref, lse_ref, bg_ref, patch_ref, gain_out_ref, grads, bias, acc, normed_grad,
):
    step = pl.program_id(0)
    kind, half = lax.rem(step, 3), lax.div(step, 3)

    @pl.when(step == 0)
    def _():
        bias[...] = image_bias(lengths_ref, x_ref.shape[0])
        normed_grad[...] = jnp.zeros_like(normed_grad)

    @pl.when(kind == 0)
    def _():
        acc[...] = jnp.zeros_like(acc)
        lane = lax.broadcasted_iota(jnp.int32, lse_ref.shape, 1)
        for head, window in enumerate(windows):
            cols = slice(window[0], window[1])
            place = half * len(windows) + head
            lse = jnp.sum(jnp.where(lane == place, lse_ref[...], 0.0), axis=-1, keepdims=True)
            queries, keys = only(window, q_ref[:, cols]), only(window, k_ref[:, cols])
            grad_att = only(window, ga_ref[:, cols])
            scores = dot_nt(queries, k_ref[:, cols]) * score_scale + bias[...]
            probs = jnp.exp(scores - lse)
            grad_probs = dot_nt(grad_att, v_ref[:, cols])
            inner = jnp.sum(grad_probs * probs, axis=-1, keepdims=True)
            grad_scores = (probs * (grad_probs - inner) * score_scale).astype(low)
            acc[0, :, cols] += dot_nn(grad_scores, keys)
            acc[1, :, cols] += dot_tn(grad_scores, queries)
            acc[2, :, cols] += dot_tn(probs.astype(low), grad_att)
        grads[...] = acc[...].astype(low)

    normed_grad[...] += dot_nt(grads[kind], w_ref[...])

    @pl.when(step == pl.num_programs(0) - 1)
    def _():
        standard, inv_spread = standardise(x_ref[...].astype(wide))
        grad_normed = normed_grad[...]
        gain_out_ref[...] = jnp.sum(grad_normed * standard, axis=0, keepdims=True)
        grad = grad_normed * gain_ref[...]
        branch = inv_spread * (
            grad
            - jnp.mean(grad, axis=-1, keepdims=True)
            - standard * jnp.mean(grad * standard, axis=-1, keepdims=True)
        )
        patch_ref[...] = (bg_ref[...].astype(wide) + branch).astype(low)


def backward(patch_rows, shard_lengths, gain, w_qkv, projected, grad_attended, lse, block_grad):
    row_count, model_width = patch_rows.shape
    half_width = model_width // HALVES
    windows = head_windows(model_width // HEADS, half_width)
    kernel = functools.partial(
        backward_kernel, 1.0 / math.sqrt(model_width // HEADS), windows
    )
    whole = lambda step: (0, 0)
    part = lambda kind: pl.BlockSpec(
        (row_count, half_width), lambda step: (0, kind * HALVES + lax.div(step, 3))
    )
    return pl.pallas_call(
        kernel,
        grid=(3 * HALVES,),
        in_specs=[
            smem(),
            pl.BlockSpec((row_count, model_width), whole),
            pl.BlockSpec((1, model_width), whole),
            pl.BlockSpec(
                (model_width, half_width),
                lambda step: (0, lax.rem(step, 3) * HALVES + lax.div(step, 3)),
            ),
            part(0),
            part(1),
            part(2),
            part(0),
            pl.BlockSpec((row_count, LANES), whole),
            pl.BlockSpec((row_count, model_width), whole),
        ],
        out_specs=[
            pl.BlockSpec((row_count, model_width), whole),
            pl.BlockSpec((1, model_width), whole),
        ],
        out_shape=[
            jax.ShapeDtypeStruct((row_count, model_width), low),
            jax.ShapeDtypeStruct((1, model_width), wide),
        ],
        scratch_shapes=[
            pltpu.VMEM((3, row_count, half_width), low),
            pltpu.VMEM((row_count, row_count), wide),
            pltpu.VMEM((3, row_count, half_width), wide),
            pltpu.VMEM((row_count, model_width), wide),
        ],
        compiler_params=params(),
        name="backward",
    )(
        shard_lengths, patch_rows, gain[None], w_qkv,
        projected, projected, projected, grad_attended, lse, block_grad,
    )


def place_kernel(place_ref, target_ref, returned_ref, grad_ref, away_ref, stacked):
    token_count = returned_ref.shape[0]
    model_width = returned_ref.shape[1] // GROUP
    for member in range(GROUP):
        stacked[member * token_count : (member + 1) * token_count, :] = returned_ref[
            :, member * model_width : (member + 1) * model_width
        ]
    row_count = grad_ref.shape[0]
    lane = lax.broadcasted_iota(jnp.int32, (row_count, row_count), 1)
    placing = (lane == target_ref[...]).astype(low)
    grad_ref[...] = dot_nn(placing, stacked[...]).astype(low)
    half_width = model_width // HALVES
    other = pl.multiple_of((1 - place_ref[0]) * half_width, LANES)
    away_ref[...] = grad_ref[:, pl.ds(other, half_width)]


def place_rows(place, target, returned):
    token_count, merged_width = returned.shape
    row_count, model_width = token_count * GROUP, merged_width // GROUP
    return pl.pallas_call(
        place_kernel,
        in_specs=[smem(), vmem(), vmem()],
        out_specs=[vmem(), vmem()],
        out_shape=[
            jax.ShapeDtypeStruct((row_count, model_width), low),
            jax.ShapeDtypeStruct((row_count, model_width // HALVES), low),
        ],
        scratch_shapes=[pltpu.VMEM((row_count, model_width), low)],
        compiler_params=params(),
        name="place_rows",
    )(place, target[:, None], returned)


def weight_kernel(rows, place_ref, att_ref, att_other_ref, bg_ref, bg_other_ref, out_ref):
    core, x_bit, y_bit, z_index = (place_ref[i] for i in range(4))
    half_width = bg_other_ref.shape[1]
    own = pl.multiple_of(core * half_width, LANES)
    terms = dot_tn(att_ref[...], bg_ref[:, pl.ds(own, half_width)])
    terms = (terms + dot_tn(att_other_ref[...], bg_other_ref[...])).astype(low)
    if rows is None:
        out_ref[...] = terms
        return
    count = terms.shape[0] // rows
    for index in range(count):
        number = pl.program_id(0) * count + index
        x_off = lax.rem(number, 2) ^ x_bit
        y_off = lax.rem(lax.div(number, 2), 2) ^ y_bit
        z_off = lax.div(number, 4) ^ z_index
        first = jnp.where(core == 0, x_off, y_off)
        second = jnp.where(core == 0, y_off, x_off)
        out_ref[first, second, z_off] = terms[index * rows : (index + 1) * rows]


def weight_terms(place, attended, attended_other, block_grad, grad_other, far_count):
    row_count, model_width = attended.shape
    half_width = model_width // HALVES
    rows = model_width // (4 * far_count)
    direct = rows % 16 == 0 and half_width % rows == 0
    part = pl.BlockSpec((row_count, half_width), lambda step: (0, step))
    if direct:
        shape = (2, 2, far_count, rows, half_width)
        out_spec = pl.BlockSpec(shape, lambda step: (0,) * 5)
    else:
        shape = (model_width, half_width)
        out_spec = pl.BlockSpec((half_width, half_width), lambda step: (step, 0))
    terms = pl.pallas_call(
        functools.partial(weight_kernel, rows if direct else None),
        grid=(HALVES,),
        in_specs=[
            smem(),
            part,
            part,
            pl.BlockSpec((row_count, model_width), lambda step: (0, 0)),
            pl.BlockSpec((row_count, half_width), lambda step: (0, 0)),
        ],
        out_specs=out_spec,
        out_shape=jax.ShapeDtypeStruct(shape, low),
        compiler_params=params(),
        name="weight_terms",
    )(place, attended, attended_other, block_grad, grad_other)
    if direct:
        return terms
    core, x_bit, y_bit, z_index = (place[i] for i in range(4))
    terms = terms.reshape(far_count, 2, 2, rows, half_width)
    terms = terms[jnp.arange(far_count) ^ z_index]
    ordered = []
    for first in range(2):
        for second in range(2):
            y = y_bit ^ jnp.where(core == 0, second, first)
            x = x_bit ^ jnp.where(core == 0, first, second)
            size = (far_count, 1, 1, rows, half_width)
            ordered.append(lax.dynamic_slice(terms, (0, y, x, 0, 0), size)[:, 0, 0])
    return jnp.stack(ordered).reshape(2, 2, far_count, rows, half_width)


def project_kernel(
    piece_count, place_ref, target_ref, x_ref, att_ref, bg_ref, *refs
):
    pieces, (out_ref, ga_ref, weights, sems) = refs[:piece_count], refs[piece_count:]
    core, x_bit, y_bit, z_index = (place_ref[i] for i in range(4))
    copies = []
    for number, piece in enumerate(pieces):
        if piece_count == 1:
            copies.append(pltpu.make_async_copy(piece, weights, sems.at[0, 0]))
            continue
        side, near = number // 4, number % 4
        column = core ^ side
        low_bit, high_bit = near % 2, near // 2
        y = y_bit ^ jnp.where(column == 0, low_bit, high_bit)
        x = x_bit ^ jnp.where(column == 0, high_bit, low_bit)
        for far in range(piece.shape[0]):
            row = ((z_index ^ far) * 2 + y) * 2 + x
            copies.append(
                pltpu.make_async_copy(
                    piece.at[far], weights.at[column, row], sems.at[number, far]
                )
            )
    for copy in copies:
        copy.start()
    row_count, model_width = x_ref.shape
    half_width = model_width // HALVES
    token_count = row_count // GROUP
    sub = lax.broadcasted_iota(jnp.int32, (row_count, row_count), 0)
    placing = (sub == target_ref[...]).astype(low)
    for copy in copies:
        copy.wait()
    grad = None
    for half in range(HALVES):
        cols = slice(half * half_width, (half + 1) * half_width)
        matrix = weights[half].reshape(model_width, half_width)
        branch = dot_nn(att_ref[...], matrix)
        block = (x_ref[:, cols].astype(wide) + branch).astype(low)
        tokens = dot_nn(placing, block).astype(low)
        for member in range(GROUP):
            first = member * model_width + half * half_width
            out_ref[:, first : first + half_width] = tokens[
                member * token_count : (member + 1) * token_count
            ]
        term = dot_nt(bg_ref[:, cols], matrix)
        grad = term if grad is None else grad + term
    ga_ref[...] = grad.astype(low)


def project(place, target, patch_rows, attended, block_grad, pieces):
    row_count, model_width = patch_rows.shape
    half_width = model_width // HALVES
    if len(pieces) == 1:
        scratch = (HALVES, model_width, half_width)
    else:
        far_count, rows, _ = pieces[0].shape
        scratch = (HALVES, 4 * far_count, rows, half_width)
    return pl.pallas_call(
        functools.partial(project_kernel, len(pieces)),
        in_specs=[smem()] + [vmem()] * 4 + [pl.BlockSpec(memory_space=pl.ANY)] * len(pieces),
        out_specs=[vmem(), vmem()],
        out_shape=[
            jax.ShapeDtypeStruct((row_count // GROUP, GROUP * model_width), low),
            jax.ShapeDtypeStruct((row_count, model_width), low),
        ],
        scratch_shapes=[
            pltpu.VMEM(scratch, low),
            pltpu.SemaphoreType.DMA((len(pieces), pieces[0].shape[0])),
        ],
        compiler_params=params(),
        name="project",
    )(place, target[None], patch_rows, attended, block_grad, *pieces)


def joint_permute(value, seq_count, dp_count, target):
    pairs = []
    for s in range(seq_count):
        for d in range(dp_count):
            to_s, to_d = target(s, d)
            pairs.append((s * dp_count + d, to_s * dp_count + to_d))
    return lax.ppermute(value, ("seq", "dp"), pairs)


def core_target(s, d):
    return s, d ^ 1


def first_target(s, d):
    return (s, d ^ 2) if d % 2 == 0 else (s ^ 1, d)


def second_target(s, d):
    return (s ^ 1, d) if d % 2 == 0 else (s, d ^ 2)


def far_target(step):
    return lambda s, d: (s ^ (2 * step), d)


def gather_out(place, w_out, seq_count, send):
    share, model_width = w_out.shape
    rows, cols = share // 2, model_width // 2
    core, x_bit, y_bit, z_index = (place[i] for i in range(4))
    far_count = seq_count // 2
    own = lax.dynamic_slice(w_out, (x_bit * rows, core * cols), (rows, cols))
    level = jnp.stack(
        [own] + [send(own, target=far_target(step)) for step in range(1, far_count)]
    )
    near = send(level, target=second_target)
    held = [level, near, send(level, target=first_target), send(near, target=first_target)]
    held = held + [send(one, target=core_target) for one in held]
    if rows % 16 == 0:
        return held
    held = jnp.stack(held).reshape(2, 4, far_count, rows, cols)
    held = held[:, :, jnp.arange(far_count) ^ z_index]
    columns = []
    for column in range(2):
        side = lax.dynamic_index_in_dim(held, column ^ core, 0, keepdims=False)
        blocks = []
        for y in range(2):
            for x in range(2):
                y_off, x_off = y ^ y_bit, x ^ x_bit
                near_place = y_off + 2 * x_off if column == 0 else x_off + 2 * y_off
                blocks.append(lax.dynamic_index_in_dim(side, near_place, 0, keepdims=False))
        columns.append(jnp.stack(blocks, axis=1).reshape(model_width, cols))
    return [jnp.stack(columns)]


def reduce_weight(terms, dp_count, send):
    kept, away = terms[0], terms[1]
    arrived = send(away, target=first_target)
    kept = (kept.astype(wide) + arrived.astype(wide)).astype(low)
    arrived = send(kept[1], target=second_target)
    level = (kept[0].astype(wide) + arrived.astype(wide)).astype(low)
    far_count, rows, cols = level.shape
    total = level[0].astype(wide)
    for step in range(1, far_count):
        total = total + send(level[step], target=far_target(step)).astype(wide)
    spread = jnp.broadcast_to(total.astype(low)[None], (dp_count, rows, cols))
    blocks = lax.all_to_all(spread, "dp", split_axis=0, concat_axis=0, tiled=True)
    blocks = blocks.astype(wide).reshape(dp_count // 2, 2, rows, cols)
    return blocks.transpose(0, 2, 1, 3).reshape(dp_count // 2 * rows, 2 * cols)


def reduce_gain(gain_grad, seq_count, dp_count):
    share = gain_grad.shape[0] // seq_count
    spread = jnp.broadcast_to(
        gain_grad.reshape(seq_count, 1, share), (seq_count, dp_count, share)
    ).reshape(seq_count * dp_count, share)
    arrived = lax.all_to_all(spread, ("seq", "dp"), split_axis=0, concat_axis=0, tiled=True)
    return jnp.sum(arrived, axis=0)


def per_device(patches, lengths, token_dest, gain, w_qkv, w_out, cotangent):
    seq_count = lax.axis_size("seq")
    dp_count = lax.axis_size("dp")
    send = functools.partial(joint_permute, seq_count=seq_count, dp_count=dp_count)
    s, d = lax.axis_index("seq"), lax.axis_index("dp")
    place = jnp.stack([d % 2, d // 2, s % 2, s // 2]).astype(jnp.int32)
    pieces = gather_out(place, w_out, seq_count, send)
    returned = lax.all_to_all(cotangent[0], "seq", split_axis=0, concat_axis=0, tiled=True)
    patch_rows, shard_lengths = patches[0], lengths[0, 0]
    row_count, model_width = patch_rows.shape
    token_count = row_count // GROUP
    peer_count = token_count // seq_count
    targets = token_dest[0]
    slot_ids = targets // token_count * peer_count + targets % peer_count
    members = jnp.arange(GROUP, dtype=jnp.int32) * token_count
    target = (slot_ids[:, None] + members[None, :]).reshape(row_count)
    projected, attended, lse = forward(patch_rows, shard_lengths, gain, w_qkv)
    attended_other = send(attended, target=core_target)
    block_grad, away = place_rows(place, target, returned)
    grad_other = send(away, target=core_target)
    terms = weight_terms(
        place, attended, attended_other, block_grad, grad_other, seq_count // 2
    )
    outgoing, grad_attended = project(place, target, patch_rows, attended, block_grad, pieces)
    merged = lax.all_to_all(
        outgoing.reshape(seq_count, peer_count, GROUP * model_width),
        "seq", split_axis=0, concat_axis=0, tiled=True,
    ).reshape(token_count, GROUP * model_width)
    patch_grad, gain_grad = backward(
        patch_rows, shard_lengths, gain, w_qkv, projected, grad_attended, lse, block_grad
    )
    own_weight = reduce_weight(terms, dp_count, send)
    own_gain = reduce_gain(gain_grad[0], seq_count, dp_count)
    norm_scale = 1.0 / math.sqrt(row_count * seq_count * dp_count)
    return (merged[None], patch_grad[None], own_weight * norm_scale, own_gain * norm_scale)


def solution(mesh):
    placed = (
        P("dp", "seq", None),
        P("dp", "seq", None),
        P("dp", "seq"),
        P(),
        P(),
        P("seq", None),
        P("dp", "seq", None),
    )
    return jax.shard_map(
        per_device,
        mesh=mesh,
        in_specs=placed,
        out_specs=(P("dp", "seq", None), P("dp", "seq", None), P("seq", None), P("seq")),
        check_vma=False,
    )
```

```python
import functools
import math

import jax
import jax.numpy as jnp
from jax import lax
from jax.experimental import pallas as pl
from jax.experimental.pallas import tpu as pltpu
from jax.sharding import PartitionSpec as P

HEADS = 16
GROUP = 4
HALVES = 2
LANES = 128
VMEM_LIMIT = 56 * 1024 * 1024
HBM_BYTES_PER_US = 3690000

eps = 1e-06
low = jnp.bfloat16
wide = jnp.float32


def params():
    return pltpu.CompilerParams(vmem_limit_bytes=VMEM_LIMIT)


def cost(microseconds, flops):
    nominal = microseconds * HBM_BYTES_PER_US
    return pl.CostEstimate(flops=flops, bytes_accessed=nominal, transcendentals=0)


def smem():
    return pl.BlockSpec(memory_space=pltpu.SMEM)


def vmem():
    return pl.BlockSpec(memory_space=pltpu.VMEM)


def dot_nt(left, right):
    return lax.dot_general(left, right, (((1,), (1,)), ((), ())), preferred_element_type=wide)


def dot_tn(left, right):
    return lax.dot_general(left, right, (((0,), (0,)), ((), ())), preferred_element_type=wide)


def dot_nn(left, right):
    return jnp.dot(left, right, preferred_element_type=wide)


def head_windows(head_size, width):
    windows = []
    for start in range(0, width, head_size):
        first = start // LANES * LANES
        last = -(-(start + head_size) // LANES) * LANES
        windows.append((first, last, start - first, start - first + head_size))
    return windows


def image_bias(lengths_ref, row_count):
    def image_of(index):
        number = jnp.zeros(index.shape, jnp.int32)
        end = jnp.int32(0)
        for image in range(lengths_ref.shape[0]):
            end = end + lengths_ref[image] * GROUP
            number = number + (index >= end).astype(jnp.int32)
        return number

    rows = lax.broadcasted_iota(jnp.int32, (row_count, row_count), 0)
    cols = lax.broadcasted_iota(jnp.int32, (row_count, row_count), 1)
    return jnp.where(image_of(rows) == image_of(cols), 0.0, -jnp.inf).astype(wide)


def standardise(rows):
    centred = rows - jnp.mean(rows, axis=-1, keepdims=True)
    inv_spread = lax.rsqrt(jnp.mean(centred * centred, axis=-1, keepdims=True) + eps)
    return centred * inv_spread, inv_spread


def only(window, value):
    lane = lax.broadcasted_iota(jnp.int32, value.shape, 1)
    keep = (lane >= window[2]) & (lane < window[3])
    return jnp.where(keep, value, jnp.zeros_like(value))


def forward_kernel(
    score_scale, windows, lengths_ref, x_ref, gain_ref, w_ref,
    proj_ref, att_ref, lse_ref, normed, qkv, bias, acc,
):
    step = pl.program_id(0)
    kind, half = lax.rem(step, 3), lax.div(step, 3)

    @pl.when(step == 0)
    def _():
        standard, _ = standardise(x_ref[...].astype(wide))
        normed[...] = (standard * gain_ref[...]).astype(low)
        bias[...] = image_bias(lengths_ref, x_ref.shape[0])
        lse_ref[...] = jnp.zeros_like(lse_ref)

    block = dot_nn(normed[...], w_ref[...]).astype(low)
    proj_ref[...] = block
    qkv[kind] = block

    @pl.when(kind == 2)
    def _():
        acc[...] = jnp.zeros_like(acc)
        lane = lax.broadcasted_iota(jnp.int32, lse_ref.shape, 1)
        for head, window in enumerate(windows):
            cols = slice(window[0], window[1])
            queries = only(window, qkv[0, :, cols])
            scores = dot_nt(queries, qkv[1, :, cols]) * score_scale + bias[...]
            row_max = jnp.max(scores, axis=-1, keepdims=True)
            weights = jnp.exp(scores - row_max)
            total = jnp.sum(weights, axis=-1, keepdims=True)
            probs = (weights * (1.0 / total)).astype(low)
            values = only(window, qkv[2, :, cols])
            acc[:, cols] += dot_nn(probs, values)
            place = half * len(windows) + head
            lse_ref[...] = jnp.where(lane == place, row_max + jnp.log(total), lse_ref[...])
        att_ref[...] = acc[...].astype(low)


def forward(patch_rows, shard_lengths, gain, w_qkv):
    row_count, model_width = patch_rows.shape
    half_width = model_width // HALVES
    windows = head_windows(model_width // HEADS, half_width)
    kernel = functools.partial(
        forward_kernel, 1.0 / math.sqrt(model_width // HEADS), windows
    )
    block = lambda step: (0, lax.rem(step, 3) * HALVES + lax.div(step, 3))
    whole = lambda step: (0, 0)
    return pl.pallas_call(
        kernel,
        grid=(3 * HALVES,),
        in_specs=[
            smem(),
            pl.BlockSpec((row_count, model_width), whole),
            pl.BlockSpec((1, model_width), whole),
            pl.BlockSpec((model_width, half_width), block),
        ],
        out_specs=[
            pl.BlockSpec((row_count, half_width), block),
            pl.BlockSpec((row_count, half_width), lambda step: (0, lax.div(step, 3))),
            pl.BlockSpec((row_count, LANES), whole),
        ],
        out_shape=[
            jax.ShapeDtypeStruct((row_count, 3 * model_width), low),
            jax.ShapeDtypeStruct((row_count, model_width), low),
            jax.ShapeDtypeStruct((row_count, LANES), wide),
        ],
        scratch_shapes=[
            pltpu.VMEM((row_count, model_width), low),
            pltpu.VMEM((3, row_count, half_width), low),
            pltpu.VMEM((row_count, row_count), wide),
            pltpu.VMEM((row_count, half_width), wide),
        ],
        compiler_params=params(),
        cost_estimate=cost(12, 0),
        name="forward",
    )(shard_lengths, patch_rows, gain[None], w_qkv)


def backward_kernel(
    score_scale, windows, lengths_ref, x_ref, gain_ref, w_ref, q_ref, k_ref, v_ref,
    ga_ref, lse_ref, bg_ref, patch_ref, gain_out_ref, grads, bias, acc, normed_grad,
):
    step = pl.program_id(0)
    kind, half = lax.rem(step, 3), lax.div(step, 3)

    @pl.when(step == 0)
    def _():
        bias[...] = image_bias(lengths_ref, x_ref.shape[0])
        normed_grad[...] = jnp.zeros_like(normed_grad)

    @pl.when(kind == 0)
    def _():
        acc[...] = jnp.zeros_like(acc)
        lane = lax.broadcasted_iota(jnp.int32, lse_ref.shape, 1)
        for head, window in enumerate(windows):
            cols = slice(window[0], window[1])
            place = half * len(windows) + head
            lse = jnp.sum(jnp.where(lane == place, lse_ref[...], 0.0), axis=-1, keepdims=True)
            queries, keys = only(window, q_ref[:, cols]), only(window, k_ref[:, cols])
            grad_att = only(window, ga_ref[:, cols])
            scores = dot_nt(queries, k_ref[:, cols]) * score_scale + bias[...]
            probs = jnp.exp(scores - lse)
            grad_probs = dot_nt(grad_att, v_ref[:, cols])
            inner = jnp.sum(grad_probs * probs, axis=-1, keepdims=True)
            grad_scores = (probs * (grad_probs - inner) * score_scale).astype(low)
            acc[0, :, cols] += dot_nn(grad_scores, keys)
            acc[1, :, cols] += dot_tn(grad_scores, queries)
            acc[2, :, cols] += dot_tn(probs.astype(low), grad_att)
        grads[...] = acc[...].astype(low)

    normed_grad[...] += dot_nt(grads[kind], w_ref[...])

    @pl.when(step == pl.num_programs(0) - 1)
    def _():
        standard, inv_spread = standardise(x_ref[...].astype(wide))
        grad_normed = normed_grad[...]
        gain_out_ref[...] = jnp.sum(grad_normed * standard, axis=0, keepdims=True)
        grad = grad_normed * gain_ref[...]
        branch = inv_spread * (
            grad
            - jnp.mean(grad, axis=-1, keepdims=True)
            - standard * jnp.mean(grad * standard, axis=-1, keepdims=True)
        )
        patch_ref[...] = (bg_ref[...].astype(wide) + branch).astype(low)


def backward(patch_rows, shard_lengths, gain, w_qkv, projected, grad_attended, lse, block_grad):
    row_count, model_width = patch_rows.shape
    half_width = model_width // HALVES
    windows = head_windows(model_width // HEADS, half_width)
    kernel = functools.partial(
        backward_kernel, 1.0 / math.sqrt(model_width // HEADS), windows
    )
    whole = lambda step: (0, 0)
    part = lambda kind: pl.BlockSpec(
        (row_count, half_width), lambda step: (0, kind * HALVES + lax.div(step, 3))
    )
    return pl.pallas_call(
        kernel,
        grid=(3 * HALVES,),
        in_specs=[
            smem(),
            pl.BlockSpec((row_count, model_width), whole),
            pl.BlockSpec((1, model_width), whole),
            pl.BlockSpec(
                (model_width, half_width),
                lambda step: (0, lax.rem(step, 3) * HALVES + lax.div(step, 3)),
            ),
            part(0),
            part(1),
            part(2),
            part(0),
            pl.BlockSpec((row_count, LANES), whole),
            pl.BlockSpec((row_count, model_width), whole),
        ],
        out_specs=[
            pl.BlockSpec((row_count, model_width), whole),
            pl.BlockSpec((1, model_width), whole),
        ],
        out_shape=[
            jax.ShapeDtypeStruct((row_count, model_width), low),
            jax.ShapeDtypeStruct((1, model_width), wide),
        ],
        scratch_shapes=[
            pltpu.VMEM((3, row_count, half_width), low),
            pltpu.VMEM((row_count, row_count), wide),
            pltpu.VMEM((3, row_count, half_width), wide),
            pltpu.VMEM((row_count, model_width), wide),
        ],
        compiler_params=params(),
        cost_estimate=cost(17, 0),
        name="backward",
    )(
        shard_lengths, patch_rows, gain[None], w_qkv,
        projected, projected, projected, grad_attended, lse, block_grad,
    )


def place_kernel(place_ref, target_ref, returned_ref, grad_ref, away_ref, stacked):
    token_count = returned_ref.shape[0]
    model_width = returned_ref.shape[1] // GROUP
    for member in range(GROUP):
        stacked[member * token_count : (member + 1) * token_count, :] = returned_ref[
            :, member * model_width : (member + 1) * model_width
        ]
    row_count = grad_ref.shape[0]
    lane = lax.broadcasted_iota(jnp.int32, (row_count, row_count), 1)
    placing = (lane == target_ref[...]).astype(low)
    grad_ref[...] = dot_nn(placing, stacked[...]).astype(low)
    half_width = model_width // HALVES
    other = pl.multiple_of((1 - place_ref[0]) * half_width, LANES)
    away_ref[...] = grad_ref[:, pl.ds(other, half_width)]


def place_rows(place, target, returned):
    token_count, merged_width = returned.shape
    row_count, model_width = token_count * GROUP, merged_width // GROUP
    return pl.pallas_call(
        place_kernel,
        in_specs=[smem(), vmem(), vmem()],
        out_specs=[vmem(), vmem()],
        out_shape=[
            jax.ShapeDtypeStruct((row_count, model_width), low),
            jax.ShapeDtypeStruct((row_count, model_width // HALVES), low),
        ],
        scratch_shapes=[pltpu.VMEM((row_count, model_width), low)],
        compiler_params=params(),
        cost_estimate=cost(3, 0),
        name="place_rows",
    )(place, target[:, None], returned)


def weight_kernel(rows, place_ref, att_ref, att_other_ref, bg_ref, bg_other_ref, out_ref):
    core, x_bit, y_bit, z_index = (place_ref[i] for i in range(4))
    half_width = bg_other_ref.shape[1]
    own = pl.multiple_of(core * half_width, LANES)
    terms = dot_tn(att_ref[...], bg_ref[:, pl.ds(own, half_width)])
    terms = (terms + dot_tn(att_other_ref[...], bg_other_ref[...])).astype(low)
    if rows is None:
        out_ref[...] = terms
        return
    count = terms.shape[0] // rows
    for index in range(count):
        number = pl.program_id(0) * count + index
        x_off = lax.rem(number, 2) ^ x_bit
        y_off = lax.rem(lax.div(number, 2), 2) ^ y_bit
        z_off = lax.div(number, 4) ^ z_index
        first = jnp.where(core == 0, x_off, y_off)
        second = jnp.where(core == 0, y_off, x_off)
        out_ref[first, second, z_off] = terms[index * rows : (index + 1) * rows]


def weight_terms(place, attended, attended_other, block_grad, grad_other, far_count):
    row_count, model_width = attended.shape
    half_width = model_width // HALVES
    rows = model_width // (4 * far_count)
    direct = rows % 16 == 0 and half_width % rows == 0
    part = pl.BlockSpec((row_count, half_width), lambda step: (0, step))
    if direct:
        shape = (2, 2, far_count, rows, half_width)
        out_spec = pl.BlockSpec(shape, lambda step: (0,) * 5)
    else:
        shape = (model_width, half_width)
        out_spec = pl.BlockSpec((half_width, half_width), lambda step: (step, 0))
    terms = pl.pallas_call(
        functools.partial(weight_kernel, rows if direct else None),
        grid=(HALVES,),
        in_specs=[
            smem(),
            part,
            part,
            pl.BlockSpec((row_count, model_width), lambda step: (0, 0)),
            pl.BlockSpec((row_count, half_width), lambda step: (0, 0)),
        ],
        out_specs=out_spec,
        out_shape=jax.ShapeDtypeStruct(shape, low),
        compiler_params=params(),
        cost_estimate=cost(4, 0),
        name="weight_terms",
    )(place, attended, attended_other, block_grad, grad_other)
    if direct:
        return terms
    core, x_bit, y_bit, z_index = (place[i] for i in range(4))
    terms = terms.reshape(far_count, 2, 2, rows, half_width)
    terms = terms[jnp.arange(far_count) ^ z_index]
    ordered = []
    for first in range(2):
        for second in range(2):
            y = y_bit ^ jnp.where(core == 0, second, first)
            x = x_bit ^ jnp.where(core == 0, first, second)
            size = (far_count, 1, 1, rows, half_width)
            ordered.append(lax.dynamic_slice(terms, (0, y, x, 0, 0), size)[:, 0, 0])
    return jnp.stack(ordered).reshape(2, 2, far_count, rows, half_width)


def project_kernel(
    piece_count, place_ref, target_ref, x_ref, att_ref, bg_ref, *refs
):
    pieces, (out_ref, ga_ref, weights, sems) = refs[:piece_count], refs[piece_count:]
    core, x_bit, y_bit, z_index = (place_ref[i] for i in range(4))
    copies = []
    for number, piece in enumerate(pieces):
        if piece_count == 1:
            copies.append(pltpu.make_async_copy(piece, weights, sems.at[0, 0]))
            continue
        side, near = number // 4, number % 4
        column = core ^ side
        low_bit, high_bit = near % 2, near // 2
        y = y_bit ^ jnp.where(column == 0, low_bit, high_bit)
        x = x_bit ^ jnp.where(column == 0, high_bit, low_bit)
        for far in range(piece.shape[0]):
            row = ((z_index ^ far) * 2 + y) * 2 + x
            copies.append(
                pltpu.make_async_copy(
                    piece.at[far], weights.at[column, row], sems.at[number, far]
                )
            )
    for copy in copies:
        copy.start()
    row_count, model_width = x_ref.shape
    half_width = model_width // HALVES
    token_count = row_count // GROUP
    sub = lax.broadcasted_iota(jnp.int32, (row_count, row_count), 0)
    placing = (sub == target_ref[...]).astype(low)
    for copy in copies:
        copy.wait()
    grad = None
    for half in range(HALVES):
        cols = slice(half * half_width, (half + 1) * half_width)
        matrix = weights[half].reshape(model_width, half_width)
        branch = dot_nn(att_ref[...], matrix)
        block = (x_ref[:, cols].astype(wide) + branch).astype(low)
        tokens = dot_nn(placing, block).astype(low)
        for member in range(GROUP):
            first = member * model_width + half * half_width
            out_ref[:, first : first + half_width] = tokens[
                member * token_count : (member + 1) * token_count
            ]
        term = dot_nt(bg_ref[:, cols], matrix)
        grad = term if grad is None else grad + term
    ga_ref[...] = grad.astype(low)


def project(place, target, patch_rows, attended, block_grad, pieces):
    row_count, model_width = patch_rows.shape
    half_width = model_width // HALVES
    if len(pieces) == 1:
        scratch = (HALVES, model_width, half_width)
    else:
        far_count, rows, _ = pieces[0].shape
        scratch = (HALVES, 4 * far_count, rows, half_width)
    return pl.pallas_call(
        functools.partial(project_kernel, len(pieces)),
        in_specs=[smem()] + [vmem()] * 4 + [pl.BlockSpec(memory_space=pl.ANY)] * len(pieces),
        out_specs=[vmem(), vmem()],
        out_shape=[
            jax.ShapeDtypeStruct((row_count // GROUP, GROUP * model_width), low),
            jax.ShapeDtypeStruct((row_count, model_width), low),
        ],
        scratch_shapes=[
            pltpu.VMEM(scratch, low),
            pltpu.SemaphoreType.DMA((len(pieces), pieces[0].shape[0])),
        ],
        compiler_params=params(),
        cost_estimate=cost(7, 0),
        name="project",
    )(place, target[None], patch_rows, attended, block_grad, *pieces)


def joint_permute(value, seq_count, dp_count, target):
    pairs = []
    for s in range(seq_count):
        for d in range(dp_count):
            to_s, to_d = target(s, d)
            pairs.append((s * dp_count + d, to_s * dp_count + to_d))
    return lax.ppermute(value, ("seq", "dp"), pairs)


def core_target(s, d):
    return s, d ^ 1


def first_target(s, d):
    return (s, d ^ 2) if d % 2 == 0 else (s ^ 1, d)


def second_target(s, d):
    return (s ^ 1, d) if d % 2 == 0 else (s, d ^ 2)


def far_target(step):
    return lambda s, d: (s ^ (2 * step), d)


def gather_far(place, w_out, seq_count, send):
    share, model_width = w_out.shape
    rows, cols = share // 2, model_width // 2
    core, x_bit = place[0], place[1]
    own = lax.dynamic_slice(w_out, (x_bit * rows, core * cols), (rows, cols))
    return [own] + [send(own, target=far_target(step)) for step in range(1, seq_count // 2)]


def gather_near(place, level, near, send):
    held = [level, near, send(level, target=first_target), send(near, target=first_target)]
    held = held + [send(one, target=core_target) for one in held]
    core, x_bit, y_bit, z_index = (place[i] for i in range(4))
    far_count, rows, cols = level.shape
    model_width = 2 * cols
    if rows % 16 == 0:
        return held
    held = jnp.stack(held).reshape(2, 4, far_count, rows, cols)
    held = held[:, :, jnp.arange(far_count) ^ z_index]
    columns = []
    for column in range(2):
        side = lax.dynamic_index_in_dim(held, column ^ core, 0, keepdims=False)
        blocks = []
        for y in range(2):
            for x in range(2):
                y_off, x_off = y ^ y_bit, x ^ x_bit
                near_place = y_off + 2 * x_off if column == 0 else x_off + 2 * y_off
                blocks.append(lax.dynamic_index_in_dim(side, near_place, 0, keepdims=False))
        columns.append(jnp.stack(blocks, axis=1).reshape(model_width, cols))
    return [jnp.stack(columns)]


def reduce_weight(terms, dp_count, send):
    kept, away = terms[0], terms[1]
    arrived = send(away, target=first_target)
    kept = (kept.astype(wide) + arrived.astype(wide)).astype(low)
    arrived = send(kept[1], target=second_target)
    level = (kept[0].astype(wide) + arrived.astype(wide)).astype(low)
    far_count, rows, cols = level.shape
    total = level[0].astype(wide)
    for step in range(1, far_count):
        total = total + send(level[step], target=far_target(step)).astype(wide)
    spread = jnp.broadcast_to(total.astype(low)[None], (dp_count, rows, cols))
    blocks = lax.all_to_all(spread, "dp", split_axis=0, concat_axis=0, tiled=True)
    blocks = blocks.astype(wide).reshape(dp_count // 2, 2, rows, cols)
    return blocks.transpose(0, 2, 1, 3).reshape(dp_count // 2 * rows, 2 * cols)


def reduce_gain(gain_grad, seq_count, dp_count):
    share = gain_grad.shape[0] // seq_count
    spread = jnp.broadcast_to(
        gain_grad.reshape(seq_count, 1, share), (seq_count, dp_count, share)
    ).reshape(seq_count * dp_count, share)
    arrived = lax.all_to_all(spread, ("seq", "dp"), split_axis=0, concat_axis=0, tiled=True)
    return jnp.sum(arrived, axis=0)


def per_device(patches, lengths, token_dest, gain, w_qkv, w_out, cotangent):
    seq_count = lax.axis_size("seq")
    dp_count = lax.axis_size("dp")
    send = functools.partial(joint_permute, seq_count=seq_count, dp_count=dp_count)
    s, d = lax.axis_index("seq"), lax.axis_index("dp")
    place = jnp.stack([d % 2, d // 2, s % 2, s // 2]).astype(jnp.int32)
    level = gather_far(place, w_out, seq_count, send)
    returned = lax.all_to_all(cotangent[0], "seq", split_axis=0, concat_axis=0, tiled=True)
    patch_rows, shard_lengths = patches[0], lengths[0, 0]
    row_count, model_width = patch_rows.shape
    token_count = row_count // GROUP
    peer_count = token_count // seq_count
    targets = token_dest[0]
    slot_ids = targets // token_count * peer_count + targets % peer_count
    members = jnp.arange(GROUP, dtype=jnp.int32) * token_count
    target = (slot_ids[:, None] + members[None, :]).reshape(row_count)
    projected, attended, lse = forward(patch_rows, shard_lengths, gain, w_qkv)
    projected, attended, lse, level = lax.optimization_barrier(
        (projected, attended, lse, level)
    )
    level = jnp.stack(level)
    near = send(level, target=second_target)
    attended_other = send(attended, target=core_target)
    block_grad, away = place_rows(place, target, returned)
    block_grad, away, near = lax.optimization_barrier((block_grad, away, near))
    grad_other = send(away, target=core_target)
    pieces = gather_near(place, level, near, send)
    terms = weight_terms(
        place, attended, attended_other, block_grad, grad_other, seq_count // 2
    )
    outgoing, grad_attended = project(place, target, patch_rows, attended, block_grad, pieces)
    merged = lax.all_to_all(
        outgoing.reshape(seq_count, peer_count, GROUP * model_width),
        "seq", split_axis=0, concat_axis=0, tiled=True,
    ).reshape(token_count, GROUP * model_width)
    patch_grad, gain_grad = backward(
        patch_rows, shard_lengths, gain, w_qkv, projected, grad_attended, lse, block_grad
    )
    own_weight = reduce_weight(terms, dp_count, send)
    own_gain = reduce_gain(gain_grad[0], seq_count, dp_count)
    norm_scale = 1.0 / math.sqrt(row_count * seq_count * dp_count)
    return (merged[None], patch_grad[None], own_weight * norm_scale, own_gain * norm_scale)


def solution(mesh):
    placed = (
        P("dp", "seq", None),
        P("dp", "seq", None),
        P("dp", "seq"),
        P(),
        P(),
        P("seq", None),
        P("dp", "seq", None),
    )
    return jax.shard_map(
        per_device,
        mesh=mesh,
        in_specs=placed,
        out_specs=(P("dp", "seq", None), P("dp", "seq", None), P("seq", None), P("seq")),
        check_vma=False,
    )
```

```python
import functools
import math

import jax
import jax.numpy as jnp
from jax import lax
from jax.experimental import pallas as pl
from jax.experimental.pallas import tpu as pltpu
from jax.sharding import PartitionSpec as P

HEADS = 16
GROUP = 4
HALVES = 2
LANES = 128
CHUNK = 64
LOG2_E = math.log2(math.e)
VMEM_LIMIT = 56 * 1024 * 1024
HBM_BYTES_PER_US = 3690000

eps = 1e-06
low = jnp.bfloat16
wide = jnp.float32


def params():
    return pltpu.CompilerParams(vmem_limit_bytes=VMEM_LIMIT)


def cost(microseconds, flops):
    nominal = microseconds * HBM_BYTES_PER_US
    return pl.CostEstimate(flops=flops, bytes_accessed=nominal, transcendentals=0)


def smem():
    return pl.BlockSpec(memory_space=pltpu.SMEM)


def vmem():
    return pl.BlockSpec(memory_space=pltpu.VMEM)


def dot_nt(left, right):
    return lax.dot_general(left, right, (((1,), (1,)), ((), ())), preferred_element_type=wide)


def dot_tn(left, right):
    return lax.dot_general(left, right, (((0,), (0,)), ((), ())), preferred_element_type=wide)


def dot_nn(left, right):
    return jnp.dot(left, right, preferred_element_type=wide)


def head_windows(head_size, width):
    windows = []
    for start in range(0, width, head_size):
        first = start // LANES * LANES
        last = -(-(start + head_size) // LANES) * LANES
        windows.append((start, start + head_size, first, last))
    return windows


def image_bias(lengths_ref, row_count):
    def image_of(index):
        number = jnp.zeros(index.shape, jnp.int32)
        end = jnp.int32(0)
        for image in range(lengths_ref.shape[0]):
            end = end + lengths_ref[image] * GROUP
            number = number + (index >= end).astype(jnp.int32)
        return number

    rows = lax.broadcasted_iota(jnp.int32, (row_count, row_count), 0)
    cols = lax.broadcasted_iota(jnp.int32, (row_count, row_count), 1)
    return jnp.where(image_of(rows) == image_of(cols), 0.0, -jnp.inf).astype(wide)


def standardise(rows):
    centred = rows - jnp.mean(rows, axis=-1, keepdims=True)
    inv_spread = lax.rsqrt(jnp.mean(centred * centred, axis=-1, keepdims=True) + eps)
    return centred * inv_spread, inv_spread


def only(window, first, last, value):
    lane = lax.broadcasted_iota(jnp.int32, value.shape, 1) + first
    keep = (lane >= window[0]) & (lane < window[1])
    return jnp.where(keep, value, jnp.zeros_like(value))


def position():
    s, d = lax.axis_index("seq"), lax.axis_index("dp")
    return d % 2, d // 2, s % 2, s // 2


def row_chunks(row_count):
    return [slice(first, first + CHUNK) for first in range(0, row_count, CHUNK)]


def forward_kernel(
    score_scale, head_size, lengths_ref, x_ref, gain_ref, w_ref,
    proj_ref, att_ref, att_t_ref, lse_ref, normed, qkv, bias, scores, probs,
):
    step = pl.program_id(0)
    kind = lax.rem(step, 3)
    row_count, half_width = att_ref.shape
    windows = head_windows(head_size, half_width)

    @pl.when(step == 0)
    def _():
        standard, _ = standardise(x_ref[...].astype(wide))
        normed[...] = (standard * gain_ref[...]).astype(low)
        bias[...] = image_bias(lengths_ref, row_count)

    block = dot_nn(normed[...], w_ref[...]).astype(low)
    proj_ref[...] = block
    qkv[kind] = block

    @pl.when(kind == 2)
    def _():
        for head, (start, stop, first, last) in enumerate(windows):
            queries = only((start, stop), first, last, qkv[0, :, first:last])
            scores[head] = dot_nt(queries, qkv[1, :, first:last])
        lane = lax.broadcasted_iota(jnp.int32, (CHUNK, LANES), 1)
        for rows in row_chunks(row_count):
            lse = jnp.zeros((CHUNK, LANES), wide)
            for head in range(len(windows)):
                scaled = scores[head, rows] * (score_scale * LOG2_E) + bias[rows]
                row_max = jnp.max(scaled, axis=-1, keepdims=True)
                weights = jnp.exp2(scaled - row_max)
                total = jnp.sum(weights, axis=-1, keepdims=True)
                probs[head, rows] = (weights * (1.0 / total)).astype(low)
                lse = jnp.where(lane == head, row_max + jnp.log2(total), lse)
            lse_ref[0, rows] = lse
        for first in range(0, half_width, LANES):
            last = first + LANES
            tile = None
            for head, (start, stop, _, _) in enumerate(windows):
                if start < last and stop > first:
                    values = only((start, stop), first, last, qkv[2, :, first:last])
                    term = dot_nn(probs[head], values)
                    tile = term if tile is None else tile + term
            tile = tile.astype(low)
            att_ref[:, first:last] = tile
            att_t_ref[first:last, :] = tile.T


def forward(patch_rows, shard_lengths, gain, w_qkv):
    row_count, model_width = patch_rows.shape
    half_width = model_width // HALVES
    head_size = model_width // HEADS
    heads = HEADS // HALVES
    kernel = functools.partial(forward_kernel, 1.0 / math.sqrt(head_size), head_size)
    block = lambda step: (0, lax.rem(step, 3) * HALVES + lax.div(step, 3))
    whole = lambda step: (0, 0)
    return pl.pallas_call(
        kernel,
        grid=(3 * HALVES,),
        in_specs=[
            smem(),
            pl.BlockSpec((row_count, model_width), whole),
            pl.BlockSpec((1, model_width), whole),
            pl.BlockSpec((model_width, half_width), block),
        ],
        out_specs=[
            pl.BlockSpec((row_count, half_width), block),
            pl.BlockSpec((row_count, half_width), lambda step: (0, lax.div(step, 3))),
            pl.BlockSpec((half_width, row_count), lambda step: (lax.div(step, 3), 0)),
            pl.BlockSpec((1, row_count, LANES), lambda step: (lax.div(step, 3), 0, 0)),
        ],
        out_shape=[
            jax.ShapeDtypeStruct((row_count, 3 * model_width), low),
            jax.ShapeDtypeStruct((row_count, model_width), low),
            jax.ShapeDtypeStruct((model_width, row_count), low),
            jax.ShapeDtypeStruct((HALVES, row_count, LANES), wide),
        ],
        scratch_shapes=[
            pltpu.VMEM((row_count, model_width), low),
            pltpu.VMEM((3, row_count, half_width), low),
            pltpu.VMEM((row_count, row_count), wide),
            pltpu.VMEM((heads, row_count, row_count), wide),
            pltpu.VMEM((heads, row_count, row_count), low),
        ],
        compiler_params=params(),
        cost_estimate=cost(9, 0),
        name="forward",
    )(shard_lengths, patch_rows, gain[None], w_qkv)


def attention_grad_kernel(
    score_scale, head_size, lengths_ref, q_ref, k_ref, v_ref, ga_ref, lse_ref,
    out_ref, bias, scores, grad_probs, probs, grad_scores, turned,
):
    row_count, half_width = q_ref.shape
    windows = head_windows(head_size, half_width)

    @pl.when(pl.program_id(0) == 0)
    def _():
        bias[...] = image_bias(lengths_ref, row_count)

    for head, (start, stop, first, last) in enumerate(windows):
        queries = only((start, stop), first, last, q_ref[:, first:last])
        scores[head] = dot_nt(queries, k_ref[:, first:last])
        grad_att = only((start, stop), first, last, ga_ref[:, first:last])
        grad_probs[head] = dot_nt(grad_att, v_ref[:, first:last])
    turned[0] = k_ref[...].T
    turned[1] = q_ref[...].T
    turned[2] = ga_ref[...].T
    for rows in row_chunks(row_count):
        for head in range(len(windows)):
            scaled = scores[head, rows] * (score_scale * LOG2_E) + bias[rows]
            chance = jnp.exp2(scaled - lse_ref[0, rows, head : head + 1])
            incoming = grad_probs[head, rows]
            inner = jnp.sum(incoming * chance, axis=-1, keepdims=True)
            probs[head, rows] = chance.astype(low)
            grad_scores[head, rows] = (chance * (incoming - inner) * score_scale).astype(low)
    for head in range(len(windows)):
        rows = slice(head * head_size, (head + 1) * head_size)
        out_ref[0, 0, rows] = dot_nt(turned[0, rows], grad_scores[head]).astype(low)
        out_ref[1, 0, rows] = dot_nn(turned[1, rows], grad_scores[head]).astype(low)
        out_ref[2, 0, rows] = dot_nn(turned[2, rows], probs[head]).astype(low)


def attention_grad(shard_lengths, projected, grad_attended, lse):
    row_count, model_width = grad_attended.shape
    half_width = model_width // HALVES
    head_size = model_width // HEADS
    heads = HEADS // HALVES
    kernel = functools.partial(attention_grad_kernel, 1.0 / math.sqrt(head_size), head_size)
    part = lambda kind: pl.BlockSpec(
        (row_count, half_width), lambda half: (0, kind * HALVES + half)
    )
    return pl.pallas_call(
        kernel,
        grid=(HALVES,),
        in_specs=[
            smem(),
            part(0),
            part(1),
            part(2),
            part(0),
            pl.BlockSpec((1, row_count, LANES), lambda half: (half, 0, 0)),
        ],
        out_specs=pl.BlockSpec((3, 1, half_width, row_count), lambda half: (0, half, 0, 0)),
        out_shape=jax.ShapeDtypeStruct((3, HALVES, half_width, row_count), low),
        scratch_shapes=[
            pltpu.VMEM((row_count, row_count), wide),
            pltpu.VMEM((heads, row_count, row_count), wide),
            pltpu.VMEM((heads, row_count, row_count), wide),
            pltpu.VMEM((heads, row_count, row_count), low),
            pltpu.VMEM((heads, row_count, row_count), low),
            pltpu.VMEM((3, half_width, row_count), low),
        ],
        compiler_params=params(),
        cost_estimate=cost(9, 0),
        name="attention_grad",
    )(shard_lengths, projected, projected, projected, grad_attended, lse)


def norm_grad_kernel(
    x_ref, gain_ref, w_ref, grad_ref, bg_ref, patch_ref, gain_out_ref, turned
):
    step = pl.program_id(0) * HALVES + pl.program_id(1)

    @pl.when(step == 0)
    def _():
        turned[...] = jnp.zeros_like(turned)

    turned[...] += dot_nn(w_ref[...], grad_ref[0, 0])

    @pl.when(step == 3 * HALVES - 1)
    def _():
        standard, inv_spread = standardise(x_ref[...].astype(wide))
        grad_normed = turned[...].T
        gain_out_ref[...] = jnp.sum(grad_normed * standard, axis=0, keepdims=True)
        grad = grad_normed * gain_ref[...]
        branch = inv_spread * (
            grad
            - jnp.mean(grad, axis=-1, keepdims=True)
            - standard * jnp.mean(grad * standard, axis=-1, keepdims=True)
        )
        patch_ref[...] = (bg_ref[...].astype(wide) + branch).astype(low)


def norm_grad(patch_rows, gain, w_qkv, grads, block_grad):
    row_count, model_width = patch_rows.shape
    half_width = model_width // HALVES
    whole = lambda kind, half: (0, 0)
    return pl.pallas_call(
        norm_grad_kernel,
        grid=(3, HALVES),
        in_specs=[
            pl.BlockSpec((row_count, model_width), whole),
            pl.BlockSpec((1, model_width), whole),
            pl.BlockSpec((model_width, half_width), lambda kind, half: (0, kind * HALVES + half)),
            pl.BlockSpec((1, 1, half_width, row_count), lambda kind, half: (kind, half, 0, 0)),
            pl.BlockSpec((row_count, model_width), whole),
        ],
        out_specs=[
            pl.BlockSpec((row_count, model_width), whole),
            pl.BlockSpec((1, model_width), whole),
        ],
        out_shape=[
            jax.ShapeDtypeStruct((row_count, model_width), low),
            jax.ShapeDtypeStruct((1, model_width), wide),
        ],
        scratch_shapes=[pltpu.VMEM((model_width, row_count), wide)],
        compiler_params=params(),
        cost_estimate=cost(7, 0),
        name="norm_grad",
    )(patch_rows, gain[None], w_qkv, grads, block_grad)


def placing_matrix(dest_ref, row_count):
    token_count = row_count // GROUP
    peer_count = token_count // lax.axis_size("seq")
    token_bits = token_count.bit_length() - 1
    dest = dest_ref[...]
    shard = lax.shift_right_logical(dest, jnp.full_like(dest, token_bits))
    slot = shard * peer_count + (dest & (peer_count - 1))
    square = (token_count, token_count)
    chosen = (lax.broadcasted_iota(jnp.int32, square, 0) == slot).astype(low)
    shape = (token_count, row_count)
    token = lax.broadcasted_iota(jnp.int32, shape, 0) * GROUP
    row = lax.broadcasted_iota(jnp.int32, shape, 1)
    parts = []
    for member in range(GROUP):
        spread = (row == token + member).astype(low)
        parts.append(dot_nn(chosen, spread).astype(low))
    return jnp.concatenate(parts, axis=0)


def place_kernel(dest_ref, returned_ref, grad_ref, away_ref, stacked):
    token_count = returned_ref.shape[0]
    model_width = returned_ref.shape[1] // GROUP
    for member in range(GROUP):
        stacked[member * token_count : (member + 1) * token_count, :] = returned_ref[
            :, member * model_width : (member + 1) * model_width
        ]
    placing = placing_matrix(dest_ref, grad_ref.shape[0])
    grad_ref[...] = dot_tn(placing, stacked[...]).astype(low)
    half_width = model_width // HALVES
    other = pl.multiple_of((1 - position()[0]) * half_width, LANES)
    away_ref[...] = grad_ref[:, pl.ds(other, half_width)]


def place_rows(token_dest, returned):
    token_count, merged_width = returned.shape
    row_count, model_width = token_count * GROUP, merged_width // GROUP
    return pl.pallas_call(
        place_kernel,
        in_specs=[vmem(), vmem()],
        out_specs=[vmem(), vmem()],
        out_shape=[
            jax.ShapeDtypeStruct((row_count, model_width), low),
            jax.ShapeDtypeStruct((row_count, model_width // HALVES), low),
        ],
        scratch_shapes=[pltpu.VMEM((row_count, model_width), low)],
        compiler_params=params(),
        cost_estimate=cost(3, 0),
        name="place_rows",
    )(token_dest, returned)


def weight_kernel(rows, att_ref, att_other_ref, bg_ref, bg_other_ref, kept_ref, away_ref):
    core, x_bit, y_bit, z_index = position()
    half_width = bg_other_ref.shape[1]
    own = pl.multiple_of(core * half_width, LANES)
    terms = dot_nn(att_ref[...], bg_ref[:, pl.ds(own, half_width)])
    terms = (terms + dot_nn(att_other_ref[...], bg_other_ref[...])).astype(low)
    count = terms.shape[0] // rows
    for index in range(count):
        number = pl.program_id(0) * count + index
        x_off = lax.rem(number, 2) ^ x_bit
        y_off = lax.rem(lax.div(number, 2), 2) ^ y_bit
        z_off = lax.div(number, 4) ^ z_index
        first = jnp.where(core == 0, x_off, y_off)
        second = jnp.where(core == 0, y_off, x_off)
        piece = terms[index * rows : (index + 1) * rows]

        @pl.when(first == 0)
        def _():
            kept_ref[second, z_off] = piece

        @pl.when(first == 1)
        def _():
            away_ref[second, z_off] = piece


def plain_weight_kernel(att_ref, att_other_ref, bg_ref, bg_other_ref, out_ref):
    half_width = bg_other_ref.shape[1]
    own = pl.multiple_of(position()[0] * half_width, LANES)
    terms = dot_nn(att_ref[...], bg_ref[:, pl.ds(own, half_width)])
    out_ref[...] = (terms + dot_nn(att_other_ref[...], bg_other_ref[...])).astype(low)


def weight_terms(place, att_turned, att_other, block_grad, grad_other, far_count):
    model_width, row_count = att_turned.shape
    half_width = model_width // HALVES
    rows = model_width // (4 * far_count)
    direct = rows % 16 == 0 and half_width % rows == 0
    part = pl.BlockSpec((half_width, row_count), lambda step: (step, 0))
    if direct:
        shape = (2, far_count, rows, half_width)
        out_specs = [pl.BlockSpec(shape, lambda step: (0,) * 4)] * 2
        out_shape = [jax.ShapeDtypeStruct(shape, low)] * 2
    else:
        out_specs = pl.BlockSpec((half_width, half_width), lambda step: (step, 0))
        out_shape = jax.ShapeDtypeStruct((model_width, half_width), low)
    terms = pl.pallas_call(
        functools.partial(weight_kernel, rows) if direct else plain_weight_kernel,
        grid=(HALVES,),
        in_specs=[
            part,
            part,
            pl.BlockSpec((row_count, model_width), lambda step: (0, 0)),
            pl.BlockSpec((row_count, half_width), lambda step: (0, 0)),
        ],
        out_specs=out_specs,
        out_shape=out_shape,
        compiler_params=params(),
        cost_estimate=cost(3, 0),
        name="weight_terms",
    )(att_turned, att_other, block_grad, grad_other)
    if direct:
        return terms
    core, x_bit, y_bit, z_index = place
    terms = terms.reshape(far_count, 2, 2, rows, half_width)
    terms = terms[jnp.arange(far_count) ^ z_index]
    ordered = []
    for first in range(2):
        for second in range(2):
            y = y_bit ^ jnp.where(core == 0, second, first)
            x = x_bit ^ jnp.where(core == 0, first, second)
            size = (far_count, 1, 1, rows, half_width)
            ordered.append(lax.dynamic_slice(terms, (0, y, x, 0, 0), size)[:, 0, 0])
    return jnp.stack(ordered[:2]), jnp.stack(ordered[2:])


def project_kernel(piece_count, dest_ref, x_ref, att_ref, bg_ref, *refs):
    pieces, (out_ref, ga_ref, weights, grad, sems) = refs[:piece_count], refs[piece_count:]
    core, x_bit, y_bit, z_index = position()
    copies = ([], [])
    for number, piece in enumerate(pieces):
        if piece_count == 2:
            column = core ^ number
            copy = pltpu.make_async_copy(piece, weights.at[column], sems.at[number, 0])
            copies[number].append(copy)
            continue
        side, near = number // 4, number % 4
        column = core ^ side
        low_bit, high_bit = near % 2, near // 2
        y = y_bit ^ jnp.where(column == 0, low_bit, high_bit)
        x = x_bit ^ jnp.where(column == 0, high_bit, low_bit)
        for far in range(piece.shape[0]):
            row = ((z_index ^ far) * 2 + y) * 2 + x
            copies[side].append(
                pltpu.make_async_copy(
                    piece.at[far], weights.at[column, row], sems.at[number, far]
                )
            )
    for copy in copies[0] + copies[1]:
        copy.start()
    row_count, model_width = x_ref.shape
    half_width = model_width // HALVES
    token_count = row_count // GROUP
    placing = placing_matrix(dest_ref, row_count)
    for side in range(HALVES):
        for copy in copies[side]:
            copy.wait()
        column = core ^ side
        first = pl.multiple_of(column * half_width, LANES)
        cols = pl.ds(first, half_width)
        matrix = weights[column].reshape(model_width, half_width)
        branch = dot_nn(att_ref[...], matrix)
        block = (x_ref[:, cols].astype(wide) + branch).astype(low)
        tokens = dot_nn(placing, block).astype(low)
        for member in range(GROUP):
            place = pl.multiple_of(member * model_width + first, LANES)
            out_ref[:, pl.ds(place, half_width)] = tokens[
                member * token_count : (member + 1) * token_count
            ]
        term = dot_nt(bg_ref[:, cols], matrix)
        if side == 0:
            grad[...] = term
        else:
            ga_ref[...] = (grad[...] + term).astype(low)


def project(token_dest, patch_rows, attended, block_grad, pieces):
    row_count, model_width = patch_rows.shape
    half_width = model_width // HALVES
    if len(pieces) == 2:
        scratch = (HALVES, model_width, half_width)
    else:
        far_count, rows, _ = pieces[0].shape
        scratch = (HALVES, 4 * far_count, rows, half_width)
    return pl.pallas_call(
        functools.partial(project_kernel, len(pieces)),
        in_specs=[vmem()] * 4 + [pl.BlockSpec(memory_space=pl.ANY)] * len(pieces),
        out_specs=[vmem(), vmem()],
        out_shape=[
            jax.ShapeDtypeStruct((row_count // GROUP, GROUP * model_width), low),
            jax.ShapeDtypeStruct((row_count, model_width), low),
        ],
        scratch_shapes=[
            pltpu.VMEM(scratch, low),
            pltpu.VMEM((row_count, model_width), wide),
            pltpu.SemaphoreType.DMA((len(pieces), pieces[0].shape[0] if len(pieces) > 2 else 1)),
        ],
        compiler_params=params(),
        cost_estimate=cost(6, 0),
        name="project",
    )(token_dest, patch_rows, attended, block_grad, *pieces)


def joint_permute(value, seq_count, dp_count, target):
    pairs = []
    for s in range(seq_count):
        for d in range(dp_count):
            to_s, to_d = target(s, d)
            pairs.append((s * dp_count + d, to_s * dp_count + to_d))
    return lax.ppermute(value, ("seq", "dp"), pairs)


def core_target(s, d):
    return s, d ^ 1


def first_target(s, d):
    return (s, d ^ 2) if d % 2 == 0 else (s ^ 1, d)


def second_target(s, d):
    return (s ^ 1, d) if d % 2 == 0 else (s, d ^ 2)


def far_target(step):
    return lambda s, d: (s ^ (2 * step), d)


def gather_far(place, w_out, seq_count, send):
    share, model_width = w_out.shape
    rows, cols = share // 2, model_width // 2
    core, x_bit = place[0], place[1]
    own = lax.dynamic_slice(w_out, (x_bit * rows, core * cols), (rows, cols))
    return [own] + [send(own, target=far_target(step)) for step in range(1, seq_count // 2)]


def gathered_pieces(place, held):
    far_count, rows, cols = held[0].shape
    if rows % 16 == 0:
        return held
    core, x_bit, y_bit, z_index = place
    held = jnp.stack(held).reshape(2, 4, far_count, rows, cols)
    held = held[:, :, jnp.arange(far_count) ^ z_index]
    columns = []
    for side in range(2):
        blocks = []
        for y in range(2):
            for x in range(2):
                y_off, x_off = y ^ y_bit, x ^ x_bit
                near_place = jnp.where(core == side, y_off + 2 * x_off, x_off + 2 * y_off)
                blocks.append(
                    lax.dynamic_index_in_dim(held[side], near_place, 0, keepdims=False)
                )
        columns.append(jnp.stack(blocks, axis=1).reshape(2 * cols, cols))
    return columns


def add_low(left, right):
    return (left.astype(wide) + right.astype(wide)).astype(low)


def share_weight(place, total, send):
    rows, cols = total.shape
    core, x_bit = place[0], place[1]
    held = jnp.stack(
        [total, send(total, target=core_target)]
        + [send(total, target=lambda s, d, flip=flip: (s, d ^ flip)) for flip in (2, 3)]
    ).reshape(2, 2, rows, cols)
    held = jnp.where(x_bit == 0, held, held[::-1])
    held = jnp.where(core == 0, held, held[:, ::-1])
    return held.astype(wide).transpose(0, 2, 1, 3).reshape(2 * rows, 2 * cols)


def reduce_gain(gain_grad, seq_count, dp_count):
    share = gain_grad.shape[0] // seq_count
    spread = jnp.broadcast_to(
        gain_grad.reshape(seq_count, 1, share), (seq_count, dp_count, share)
    ).reshape(seq_count * dp_count, share)
    arrived = lax.all_to_all(spread, ("seq", "dp"), split_axis=0, concat_axis=0, tiled=True)
    return jnp.sum(arrived, axis=0)


def together(*values):
    return lax.optimization_barrier(values)


def per_device(patches, lengths, token_dest, gain, w_qkv, w_out, cotangent):
    seq_count = lax.axis_size("seq")
    dp_count = lax.axis_size("dp")
    send = functools.partial(joint_permute, seq_count=seq_count, dp_count=dp_count)
    place = position()
    patch_rows, shard_lengths = patches[0], lengths[0, 0]
    row_count, model_width = patch_rows.shape
    token_count = row_count // GROUP

    far = gather_far(place, w_out, seq_count, send)
    returned = lax.all_to_all(cotangent[0], "seq", split_axis=0, concat_axis=0, tiled=True)
    projected, attended, att_turned, lse = forward(patch_rows, shard_lengths, gain, w_qkv)
    projected, attended, att_turned, lse, far = together(
        projected, attended, att_turned, lse, far
    )
    level = jnp.stack(far)
    near = send(level, target=second_target)
    beyond = send(level, target=first_target)
    att_other = send(att_turned, target=core_target)
    block_grad, away = place_rows(token_dest, returned)
    block_grad, away, near = together(block_grad, away, near)
    grad_other = send(away, target=core_target)
    corner = send(near, target=first_target)
    att_other, grad_other, beyond = together(att_other, grad_other, beyond)
    kept, away = weight_terms(
        place, att_turned, att_other, block_grad, grad_other, seq_count // 2
    )
    kept, away, corner = together(kept, away, corner)
    held = [level, near, beyond, corner]
    held = held + [send(one, target=core_target) for one in held]
    arrived = send(away, target=first_target)
    pieces = gathered_pieces(place, held)
    outgoing, grad_attended = project(token_dest, patch_rows, attended, block_grad, pieces)
    merged = lax.all_to_all(
        outgoing.reshape(seq_count, token_count // seq_count, GROUP * model_width),
        "seq", split_axis=0, concat_axis=0, tiled=True,
    ).reshape(token_count, GROUP * model_width)
    kept, grad_attended = together(add_low(kept, arrived), grad_attended)
    arrived = send(kept[1], target=second_target)
    grads = attention_grad(shard_lengths, projected, grad_attended, lse)
    level, grads = together(add_low(kept[0], arrived), grads)
    terms = [level[0]] + [
        send(level[step], target=far_target(step)) for step in range(1, seq_count // 2)
    ]
    patch_grad, gain_grad = norm_grad(patch_rows, gain, w_qkv, grads, block_grad)
    patch_grad, gain_grad, merged, terms = together(patch_grad, gain_grad, merged, terms)
    total = sum(term.astype(wide) for term in terms).astype(low)
    own_weight = share_weight(place, total, send)
    own_gain = reduce_gain(gain_grad[0], seq_count, dp_count)
    norm_scale = 1.0 / math.sqrt(row_count * seq_count * dp_count)
    return (merged[None], patch_grad[None], own_weight * norm_scale, own_gain * norm_scale)


def solution(mesh):
    placed = (
        P("dp", "seq", None),
        P("dp", "seq", None),
        P("dp", "seq"),
        P(),
        P(),
        P("seq", None),
        P("dp", "seq", None),
    )
    return jax.shard_map(
        per_device,
        mesh=mesh,
        in_specs=placed,
        out_specs=(P("dp", "seq", None), P("dp", "seq", None), P("seq", None), P("seq")),
        check_vma=False,
    )
```

```python
import functools
import math

import jax
import jax.numpy as jnp
from jax import lax
from jax.experimental import pallas as pl
from jax.experimental.pallas import tpu as pltpu
from jax.sharding import PartitionSpec as P

HEADS = 16
GROUP = 4
HALVES = 2
LANES = 128
CHUNK = 64
LOG2_E = math.log2(math.e)
VMEM_LIMIT = 60 * 1024 * 1024
PART = 256
HBM_BYTES_PER_US = 3690000

eps = 1e-06
low = jnp.bfloat16
wide = jnp.float32


def params():
    return pltpu.CompilerParams(vmem_limit_bytes=VMEM_LIMIT)


def cost(microseconds, flops):
    nominal = microseconds * HBM_BYTES_PER_US
    return pl.CostEstimate(flops=flops, bytes_accessed=nominal, transcendentals=0)


def smem():
    return pl.BlockSpec(memory_space=pltpu.SMEM)


def vmem():
    return pl.BlockSpec(memory_space=pltpu.VMEM)


def dot_nt(left, right):
    return lax.dot_general(left, right, (((1,), (1,)), ((), ())), preferred_element_type=wide)


def dot_tn(left, right):
    return lax.dot_general(left, right, (((0,), (0,)), ((), ())), preferred_element_type=wide)


def dot_nn(left, right):
    return jnp.dot(left, right, preferred_element_type=wide)


def head_windows(head_size, width):
    windows = []
    for start in range(0, width, head_size):
        first = start // LANES * LANES
        last = -(-(start + head_size) // LANES) * LANES
        windows.append((start, start + head_size, first, last))
    return windows


def image_bias(lengths_ref, row_count):
    def image_of(index):
        number = jnp.zeros(index.shape, jnp.int32)
        end = jnp.int32(0)
        for image in range(lengths_ref.shape[0]):
            end = end + lengths_ref[image] * GROUP
            number = number + (index >= end).astype(jnp.int32)
        return number

    rows = lax.broadcasted_iota(jnp.int32, (row_count, row_count), 0)
    cols = lax.broadcasted_iota(jnp.int32, (row_count, row_count), 1)
    return jnp.where(image_of(rows) == image_of(cols), 0.0, -jnp.inf).astype(wide)


def standardise(rows):
    centred = rows - jnp.mean(rows, axis=-1, keepdims=True)
    inv_spread = lax.rsqrt(jnp.mean(centred * centred, axis=-1, keepdims=True) + eps)
    return centred * inv_spread, inv_spread


def anywhere():
    return pl.BlockSpec(memory_space=pl.ANY)


def only(window, first, last, value):
    lane = lax.broadcasted_iota(jnp.int32, (1, last - first), 1) + first
    keep = (lane >= window[0]) & (lane < window[1])
    return value * jnp.where(keep, 1.0, 0.0).astype(low)


class Copies:
    def __init__(self, sems):
        self.sems = sems
        self.used = 0

    def start(self, source, target):
        copy = pltpu.make_async_copy(source, target, self.sems.at[self.used])
        self.used += 1
        copy.start()
        return copy


def wait_all(copies):
    for copy in copies:
        copy.wait()


def position():
    s, d = lax.axis_index("seq"), lax.axis_index("dp")
    return d % 2, d // 2, s % 2, s // 2


def row_chunks(row_count):
    return [slice(first, first + CHUNK) for first in range(0, row_count, CHUNK)]


def forward_kernel(
    score_scale, head_size, lengths_ref, x_hbm, gain_ref, w_hbm,
    proj_hbm, att_hbm, att_t_hbm, lse_hbm,
    x_buf, w_buf, normed, qkv, att_buf, att_t_buf, lse_buf, bias, scores, probs, sems,
):
    copies = Copies(sems)
    row_count, model_width = x_buf.shape
    half_width = model_width // HALVES
    windows = head_windows(head_size, half_width)
    x_copy = copies.start(x_hbm, x_buf)
    w_copies = {}
    for half in range(HALVES):
        for kind in range(3):
            first = kind * model_width + half * half_width
            w_copies[half, kind] = [
                copies.start(
                    w_hbm.at[row : row + PART, first : first + half_width],
                    w_buf.at[half, kind, row : row + PART],
                )
                for row in range(0, model_width, PART)
            ]
    bias[...] = image_bias(lengths_ref, row_count)
    x_copy.wait()
    standard, _ = standardise(x_buf[...].astype(wide))
    normed[...] = (standard * gain_ref[...]).astype(low)
    lane = lax.broadcasted_iota(jnp.int32, (CHUNK, LANES), 1)
    sent = []
    for half in range(HALVES):
        base = half * half_width
        for kind in range(3):
            wait_all(w_copies[half, kind])
            qkv[half, kind] = dot_nn(normed[...], w_buf[half, kind]).astype(low)
            first = kind * model_width + base
            sent.append(
                copies.start(qkv.at[half, kind], proj_hbm.at[:, first : first + half_width])
            )
        for head, (start, stop, first, last) in enumerate(windows):
            queries = only((start, stop), first, last, qkv[half, 0, :, first:last])
            scores[head] = dot_nt(queries, qkv[half, 1, :, first:last])
        for rows in row_chunks(row_count):
            lse = jnp.zeros((CHUNK, LANES), wide)
            for head in range(len(windows)):
                scaled = scores[head, rows] * (score_scale * LOG2_E) + bias[rows]
                row_max = jnp.max(scaled, axis=-1, keepdims=True)
                weights = jnp.exp2(scaled - row_max)
                total = jnp.sum(weights, axis=-1, keepdims=True)
                probs[head, rows] = (weights * (1.0 / total)).astype(low)
                lse = jnp.where(lane == head, row_max + jnp.log2(total), lse)
            lse_buf[half, rows] = lse
        sent.append(copies.start(lse_buf.at[half], lse_hbm.at[half]))
        for first in range(0, half_width, LANES):
            last = first + LANES
            tile = None
            for head, (start, stop, _, _) in enumerate(windows):
                if start < last and stop > first:
                    values = only((start, stop), first, last, qkv[half, 2, :, first:last])
                    term = dot_nn(probs[head], values)
                    tile = term if tile is None else tile + term
            tile = tile.astype(low)
            att_buf[half, :, first:last] = tile
            att_t_buf[base + first : base + last, :] = tile.T
        cols = slice(base, base + half_width)
        sent.append(copies.start(att_t_buf.at[cols], att_t_hbm.at[cols]))
        sent.append(copies.start(att_buf.at[half], att_hbm.at[:, cols]))
    wait_all(sent)


def forward(patch_rows, shard_lengths, gain, w_qkv):
    row_count, model_width = patch_rows.shape
    half_width = model_width // HALVES
    head_size = model_width // HEADS
    heads = HEADS // HALVES
    kernel = functools.partial(forward_kernel, 1.0 / math.sqrt(head_size), head_size)
    count = 1 + 3 * HALVES * (model_width // PART) + 6 * HALVES
    return pl.pallas_call(
        kernel,
        in_specs=[smem(), anywhere(), vmem(), anywhere()],
        out_specs=[anywhere()] * 4,
        out_shape=[
            jax.ShapeDtypeStruct((row_count, 3 * model_width), low),
            jax.ShapeDtypeStruct((row_count, model_width), low),
            jax.ShapeDtypeStruct((model_width, row_count), low),
            jax.ShapeDtypeStruct((HALVES, row_count, LANES), wide),
        ],
        scratch_shapes=[
            pltpu.VMEM((row_count, model_width), low),
            pltpu.VMEM((HALVES, 3, model_width, half_width), low),
            pltpu.VMEM((row_count, model_width), low),
            pltpu.VMEM((HALVES, 3, row_count, half_width), low),
            pltpu.VMEM((HALVES, row_count, half_width), low),
            pltpu.VMEM((model_width, row_count), low),
            pltpu.VMEM((HALVES, row_count, LANES), wide),
            pltpu.VMEM((row_count, row_count), wide),
            pltpu.VMEM((heads, row_count, row_count), wide),
            pltpu.VMEM((heads, row_count, row_count), low),
            pltpu.SemaphoreType.DMA((count,)),
        ],
        compiler_params=params(),
        cost_estimate=cost(9, 0),
        name="forward",
    )(shard_lengths, patch_rows, gain, w_qkv)


def attention_grad_kernel(
    score_scale, head_size, lengths_ref, proj_hbm, ga_hbm, lse_ref, out_hbm,
    parts, out_buf, bias, scores, grad_probs, probs, grad_scores, turned, sems,
):
    copies = Copies(sems)
    row_count, model_width = ga_hbm.shape
    half_width = model_width // HALVES
    windows = head_windows(head_size, half_width)
    arriving = {}
    for half in range(HALVES):
        for kind in range(4):
            first = half * half_width + (kind * model_width if kind < 3 else 0)
            source = proj_hbm if kind < 3 else ga_hbm
            arriving[half, kind] = copies.start(
                source.at[:, first : first + half_width], parts.at[half, kind]
            )
    bias[...] = image_bias(lengths_ref, row_count)
    sent = []
    for half in range(HALVES):
        for kind in range(4):
            arriving[half, kind].wait()
        queries, keys, values, grads = (parts.at[half, kind] for kind in range(4))
        for head, (start, stop, first, last) in enumerate(windows):
            query = only((start, stop), first, last, queries[:, first:last])
            scores[head] = dot_nt(query, keys[:, first:last])
            grad_att = only((start, stop), first, last, grads[:, first:last])
            grad_probs[head] = dot_nt(grad_att, values[:, first:last])
        turned[0] = keys[...].T
        turned[1] = queries[...].T
        turned[2] = grads[...].T
        for rows in row_chunks(row_count):
            for head in range(len(windows)):
                scaled = scores[head, rows] * (score_scale * LOG2_E) + bias[rows]
                chance = jnp.exp2(scaled - lse_ref[half, rows, head : head + 1])
                incoming = grad_probs[head, rows]
                inner = jnp.sum(incoming * chance, axis=-1, keepdims=True)
                probs[head, rows] = chance.astype(low)
                grad_scores[head, rows] = (chance * (incoming - inner) * score_scale).astype(low)
        for head in range(len(windows)):
            rows = slice(head * head_size, (head + 1) * head_size)
            out_buf[0, half, rows] = dot_nt(turned[0, rows], grad_scores[head]).astype(low)
            out_buf[1, half, rows] = dot_nn(turned[1, rows], grad_scores[head]).astype(low)
            out_buf[2, half, rows] = dot_nn(turned[2, rows], probs[head]).astype(low)
        for kind in range(3):
            sent.append(copies.start(out_buf.at[kind, half], out_hbm.at[kind, half]))
    wait_all(sent)


def attention_grad(shard_lengths, projected, grad_attended, lse):
    row_count, model_width = grad_attended.shape
    half_width = model_width // HALVES
    head_size = model_width // HEADS
    heads = HEADS // HALVES
    kernel = functools.partial(attention_grad_kernel, 1.0 / math.sqrt(head_size), head_size)
    shape = (3, HALVES, half_width, row_count)
    return pl.pallas_call(
        kernel,
        in_specs=[smem(), anywhere(), anywhere(), vmem()],
        out_specs=anywhere(),
        out_shape=jax.ShapeDtypeStruct(shape, low),
        scratch_shapes=[
            pltpu.VMEM((HALVES, 4, row_count, half_width), low),
            pltpu.VMEM(shape, low),
            pltpu.VMEM((row_count, row_count), wide),
            pltpu.VMEM((heads, row_count, row_count), wide),
            pltpu.VMEM((heads, row_count, row_count), wide),
            pltpu.VMEM((heads, row_count, row_count), low),
            pltpu.VMEM((heads, row_count, row_count), low),
            pltpu.VMEM((3, half_width, row_count), low),
            pltpu.SemaphoreType.DMA((7 * HALVES,)),
        ],
        compiler_params=params(),
        cost_estimate=cost(9, 0),
        name="attention_grad",
    )(shard_lengths, projected, grad_attended, lse)


def norm_grad_kernel(
    x_hbm, gain_ref, w_hbm, grad_hbm, bg_hbm, patch_hbm, gain_out_ref,
    x_buf, w_buf, grad_buf, bg_buf, grad_normed, patch_buf, sems,
):
    copies = Copies(sems)
    row_count, model_width = x_buf.shape
    grad_copies = [
        copies.start(grad_hbm.at[kind, half], grad_buf.at[kind, half])
        for kind in range(3)
        for half in range(HALVES)
    ]
    w_copies = []
    for row in range(0, model_width, PART):
        w_copies.append([
            copies.start(
                w_hbm.at[row : row + PART, first : first + model_width],
                w_buf.at[row : row + PART, first : first + model_width],
            )
            for first in range(0, 3 * model_width, model_width)
        ])
    late = [copies.start(x_hbm, x_buf), copies.start(bg_hbm, bg_buf)]
    wait_all(grad_copies)
    grads = grad_buf[...].reshape(3 * model_width, row_count)
    for number, arriving in enumerate(w_copies):
        wait_all(arriving)
        part = slice(number * PART, (number + 1) * PART)
        grad_normed[:, part] = dot_nn(w_buf[part], grads).T
    wait_all(late)
    sent = []
    total = None
    for row in range(0, row_count, LANES):
        rows = slice(row, row + LANES)
        standard, inv_spread = standardise(x_buf[rows].astype(wide))
        grad = grad_normed[rows]
        term = jnp.sum(grad * standard, axis=0, keepdims=True)
        total = term if total is None else total + term
        grad = grad * gain_ref[...]
        branch = inv_spread * (
            grad
            - jnp.mean(grad, axis=-1, keepdims=True)
            - standard * jnp.mean(grad * standard, axis=-1, keepdims=True)
        )
        patch_buf[rows] = (bg_buf[rows].astype(wide) + branch).astype(low)
        sent.append(copies.start(patch_buf.at[rows], patch_hbm.at[rows]))
    gain_out_ref[...] = total
    wait_all(sent)


def norm_grad(patch_rows, gain, w_qkv, grads, block_grad):
    row_count, model_width = patch_rows.shape
    count = 3 * HALVES + 3 * (model_width // PART) + 2 + row_count // LANES
    return pl.pallas_call(
        norm_grad_kernel,
        in_specs=[anywhere(), vmem(), anywhere(), anywhere(), anywhere()],
        out_specs=[anywhere(), vmem()],
        out_shape=[
            jax.ShapeDtypeStruct((row_count, model_width), low),
            jax.ShapeDtypeStruct((1, model_width), wide),
        ],
        scratch_shapes=[
            pltpu.VMEM((row_count, model_width), low),
            pltpu.VMEM(w_qkv.shape, low),
            pltpu.VMEM(grads.shape, low),
            pltpu.VMEM((row_count, model_width), low),
            pltpu.VMEM((row_count, model_width), wide),
            pltpu.VMEM((row_count, model_width), low),
            pltpu.SemaphoreType.DMA((count,)),
        ],
        compiler_params=params(),
        cost_estimate=cost(7, 0),
        name="norm_grad",
    )(patch_rows, gain, w_qkv, grads, block_grad)


def placing_matrix(dest_ref, row_count):
    token_count = row_count // GROUP
    peer_count = token_count // lax.axis_size("seq")
    token_bits = token_count.bit_length() - 1
    dest = dest_ref[...]
    shard = lax.shift_right_logical(dest, jnp.full_like(dest, token_bits))
    slot = shard * peer_count + (dest & (peer_count - 1))
    square = (token_count, token_count)
    chosen = (lax.broadcasted_iota(jnp.int32, square, 0) == slot).astype(low)
    shape = (token_count, row_count)
    token = lax.broadcasted_iota(jnp.int32, shape, 0) * GROUP
    row = lax.broadcasted_iota(jnp.int32, shape, 1)
    parts = []
    for member in range(GROUP):
        spread = (row == token + member).astype(low)
        parts.append(dot_nn(chosen, spread).astype(low))
    return jnp.concatenate(parts, axis=0)


def place_kernel(dest_ref, returned_hbm, grad_hbm, away_hbm, stacked, grad_buf, sems):
    copies = Copies(sems)
    token_count = returned_hbm.shape[0]
    row_count, model_width = stacked.shape
    half_width = model_width // HALVES
    arriving = [
        copies.start(
            returned_hbm.at[:, member * model_width : (member + 1) * model_width],
            stacked.at[member * token_count : (member + 1) * token_count],
        )
        for member in range(GROUP)
    ]
    placing = placing_matrix(dest_ref, row_count)
    core = position()[0]
    wait_all(arriving)
    sent = []
    for side in range(HALVES):
        cols = pl.ds(pl.multiple_of((core ^ (1 - side)) * half_width, LANES), half_width)
        grad_buf[side] = dot_tn(placing, stacked[:, cols]).astype(low)
        if side == 0:
            sent.append(copies.start(grad_buf.at[side], away_hbm))
        sent.append(copies.start(grad_buf.at[side], grad_hbm.at[:, cols]))
    wait_all(sent)


def place_rows(token_dest, returned):
    token_count, merged_width = returned.shape
    row_count, model_width = token_count * GROUP, merged_width // GROUP
    half_width = model_width // HALVES
    return pl.pallas_call(
        place_kernel,
        in_specs=[vmem(), anywhere()],
        out_specs=[anywhere(), anywhere()],
        out_shape=[
            jax.ShapeDtypeStruct((row_count, model_width), low),
            jax.ShapeDtypeStruct((row_count, half_width), low),
        ],
        scratch_shapes=[
            pltpu.VMEM((row_count, model_width), low),
            pltpu.VMEM((HALVES, row_count, half_width), low),
            pltpu.SemaphoreType.DMA((GROUP + HALVES + 1,)),
        ],
        compiler_params=params(),
        cost_estimate=cost(3, 0),
        name="place_rows",
    )(token_dest, returned)


def weight_kernel(
    rows, att_hbm, att_other_hbm, bg_hbm, bg_other_hbm, kept_hbm, away_hbm,
    att_buf, bg_buf, out_buf, sems,
):
    copies = Copies(sems)
    core, x_bit, y_bit, z_index = position()
    half_width = bg_other_hbm.shape[1]
    model_width = att_hbm.shape[0]
    own = pl.multiple_of(core * half_width, LANES)
    arriving = [
        copies.start(bg_hbm.at[:, pl.ds(own, half_width)], bg_buf.at[0]),
        copies.start(bg_other_hbm, bg_buf.at[1]),
    ]
    group = 4 * rows
    att_copies = []
    for first in range(0, model_width, group):
        part = slice(first, first + group)
        att_copies.append([
            copies.start(source.at[part], att_buf.at[which, part])
            for which, source in enumerate((att_hbm, att_other_hbm))
        ])
    wait_all(arriving)
    sent = []
    for far, waiting in enumerate(att_copies):
        wait_all(waiting)
        part = slice(far * group, (far + 1) * group)
        terms = dot_nn(att_buf[0, part], bg_buf[0]) + dot_nn(att_buf[1, part], bg_buf[1])
        out_buf[far] = terms.astype(low).reshape(4, rows, half_width)
        z_off = far ^ z_index
        for index in range(4):
            x_off, y_off = (index % 2) ^ x_bit, (index // 2) ^ y_bit
            first = jnp.where(core == 0, x_off, y_off)
            second = jnp.where(core == 0, y_off, x_off)
            sem = sems.at[copies.used]
            copies.used += 1
            to_kept = pltpu.make_async_copy(
                out_buf.at[far, index], kept_hbm.at[second, z_off], sem
            )
            to_away = pltpu.make_async_copy(
                out_buf.at[far, index], away_hbm.at[second, z_off], sem
            )

            @pl.when(first == 0)
            def _():
                to_kept.start()

            @pl.when(first == 1)
            def _():
                to_away.start()

            sent.append(to_kept)
    wait_all(sent)


def plain_weight_kernel(att_ref, att_other_ref, bg_ref, bg_other_ref, out_ref):
    half_width = bg_other_ref.shape[1]
    own = pl.multiple_of(position()[0] * half_width, LANES)
    terms = dot_nn(att_ref[...], bg_ref[:, pl.ds(own, half_width)])
    out_ref[...] = (terms + dot_nn(att_other_ref[...], bg_other_ref[...])).astype(low)


def weight_terms(place, att_turned, att_other, block_grad, grad_other, far_count):
    model_width, row_count = att_turned.shape
    half_width = model_width // HALVES
    rows = model_width // (4 * far_count)
    if rows % 16 == 0:
        shape = (2, far_count, rows, half_width)
        return pl.pallas_call(
            functools.partial(weight_kernel, rows),
            in_specs=[anywhere()] * 4,
            out_specs=[anywhere()] * 2,
            out_shape=[jax.ShapeDtypeStruct(shape, low)] * 2,
            scratch_shapes=[
                pltpu.VMEM((2, model_width, row_count), low),
                pltpu.VMEM((2, row_count, half_width), low),
                pltpu.VMEM((far_count, 4, rows, half_width), low),
                pltpu.SemaphoreType.DMA((2 + 6 * far_count,)),
            ],
            compiler_params=params(),
            cost_estimate=cost(3, 0),
            name="weight_terms",
        )(att_turned, att_other, block_grad, grad_other)
    part = pl.BlockSpec((half_width, row_count), lambda step: (step, 0))
    terms = pl.pallas_call(
        plain_weight_kernel,
        grid=(HALVES,),
        in_specs=[
            part,
            part,
            pl.BlockSpec((row_count, model_width), lambda step: (0, 0)),
            pl.BlockSpec((row_count, half_width), lambda step: (0, 0)),
        ],
        out_specs=pl.BlockSpec((half_width, half_width), lambda step: (step, 0)),
        out_shape=jax.ShapeDtypeStruct((model_width, half_width), low),
        compiler_params=params(),
        cost_estimate=cost(3, 0),
        name="weight_terms",
    )(att_turned, att_other, block_grad, grad_other)
    core, x_bit, y_bit, z_index = place
    terms = terms.reshape(far_count, 2, 2, rows, half_width)
    terms = terms[jnp.arange(far_count) ^ z_index]
    ordered = []
    for first in range(2):
        for second in range(2):
            y = y_bit ^ jnp.where(core == 0, second, first)
            x = x_bit ^ jnp.where(core == 0, first, second)
            size = (far_count, 1, 1, rows, half_width)
            ordered.append(lax.dynamic_slice(terms, (0, y, x, 0, 0), size)[:, 0, 0])
    return jnp.stack(ordered[:2]), jnp.stack(ordered[2:])


def project_kernel(piece_count, dest_ref, x_hbm, att_hbm, bg_hbm, *refs):
    pieces = refs[:piece_count]
    out_hbm, ga_hbm, weights, rows_buf, token_buf, ga_buf, sems = refs[piece_count:]
    copies = Copies(sems)
    core, x_bit, y_bit, z_index = position()
    early = [
        copies.start(source, rows_buf.at[number])
        for number, source in enumerate((att_hbm, x_hbm, bg_hbm))
    ]
    arriving = ([], [])
    for number, piece in enumerate(pieces):
        if piece_count == 2:
            arriving[number].append(copies.start(piece, weights.at[core ^ number]))
            continue
        side, near = number // 4, number % 4
        column = core ^ side
        low_bit, high_bit = near % 2, near // 2
        y = y_bit ^ jnp.where(column == 0, low_bit, high_bit)
        x = x_bit ^ jnp.where(column == 0, high_bit, low_bit)
        for far in range(piece.shape[0]):
            row = ((z_index ^ far) * 2 + y) * 2 + x
            arriving[side].append(copies.start(piece.at[far], weights.at[column, row]))
    _, row_count, model_width = rows_buf.shape
    half_width = model_width // HALVES
    token_count = row_count // GROUP
    placing = placing_matrix(dest_ref, row_count)
    wait_all(early)
    sent = []
    for side in range(HALVES):
        wait_all(arriving[side])
        column = core ^ side
        first = pl.multiple_of(column * half_width, LANES)
        cols = pl.ds(first, half_width)
        matrix = weights[column].reshape(model_width, half_width)
        branch = dot_nn(rows_buf[0], matrix)
        block = (rows_buf[1, :, cols].astype(wide) + branch).astype(low)
        token_buf[side] = dot_nn(placing, block).astype(low)
        for member in range(GROUP):
            place = pl.multiple_of(member * model_width + first, LANES)
            rows = slice(member * token_count, (member + 1) * token_count)
            sent.append(
                copies.start(token_buf.at[side, rows], out_hbm.at[:, pl.ds(place, half_width)])
            )
    halves = [weights[half].reshape(model_width, half_width) for half in range(HALVES)]
    for half in range(HALVES):
        rows = slice(half * half_width, (half + 1) * half_width)
        grad = dot_nt(rows_buf[2, :, :half_width], halves[0][rows])
        grad = grad + dot_nt(rows_buf[2, :, half_width:], halves[1][rows])
        ga_buf[half] = grad.astype(low)
        sent.append(copies.start(ga_buf.at[half], ga_hbm.at[:, rows]))
    wait_all(sent)


def project(token_dest, patch_rows, attended, block_grad, pieces):
    row_count, model_width = patch_rows.shape
    half_width = model_width // HALVES
    if len(pieces) == 2:
        scratch, arrivals = (HALVES, model_width, half_width), 2
    else:
        far_count, rows, _ = pieces[0].shape
        scratch, arrivals = (HALVES, 4 * far_count, rows, half_width), 8 * far_count
    return pl.pallas_call(
        functools.partial(project_kernel, len(pieces)),
        in_specs=[vmem()] + [anywhere()] * (3 + len(pieces)),
        out_specs=[anywhere(), anywhere()],
        out_shape=[
            jax.ShapeDtypeStruct((row_count // GROUP, GROUP * model_width), low),
            jax.ShapeDtypeStruct((row_count, model_width), low),
        ],
        scratch_shapes=[
            pltpu.VMEM(scratch, low),
            pltpu.VMEM((3, row_count, model_width), low),
            pltpu.VMEM((HALVES, row_count, half_width), low),
            pltpu.VMEM((HALVES, row_count, half_width), low),
            pltpu.SemaphoreType.DMA((3 + arrivals + HALVES * (GROUP + 1),)),
        ],
        compiler_params=params(),
        cost_estimate=cost(6, 0),
        name="project",
    )(token_dest, patch_rows, attended, block_grad, *pieces)


def joint_permute(value, seq_count, dp_count, target):
    pairs = []
    for s in range(seq_count):
        for d in range(dp_count):
            to_s, to_d = target(s, d)
            pairs.append((s * dp_count + d, to_s * dp_count + to_d))
    return lax.ppermute(value, ("seq", "dp"), pairs)


def core_target(s, d):
    return s, d ^ 1


def first_target(s, d):
    return (s, d ^ 2) if d % 2 == 0 else (s ^ 1, d)


def second_target(s, d):
    return (s ^ 1, d) if d % 2 == 0 else (s, d ^ 2)


def far_target(step):
    return lambda s, d: (s ^ (2 * step), d)


def gather_far(place, w_out, seq_count, send):
    share, model_width = w_out.shape
    rows, cols = share // 2, model_width // 2
    core, x_bit = place[0], place[1]
    own = lax.dynamic_slice(w_out, (x_bit * rows, core * cols), (rows, cols))
    return [own] + [send(own, target=far_target(step)) for step in range(1, seq_count // 2)]


def gathered_pieces(place, held):
    far_count, rows, cols = held[0].shape
    if rows % 16 == 0:
        return held
    core, x_bit, y_bit, z_index = place
    held = jnp.stack(held).reshape(2, 4, far_count, rows, cols)
    held = held[:, :, jnp.arange(far_count) ^ z_index]
    columns = []
    for side in range(2):
        blocks = []
        for y in range(2):
            for x in range(2):
                y_off, x_off = y ^ y_bit, x ^ x_bit
                near_place = jnp.where(core == side, y_off + 2 * x_off, x_off + 2 * y_off)
                blocks.append(
                    lax.dynamic_index_in_dim(held[side], near_place, 0, keepdims=False)
                )
        columns.append(jnp.stack(blocks, axis=1).reshape(2 * cols, cols))
    return columns


def add_low(left, right):
    return (left.astype(wide) + right.astype(wide)).astype(low)


def share_weight(place, total, send):
    rows, cols = total.shape
    core, x_bit = place[0], place[1]
    held = jnp.stack(
        [total, send(total, target=core_target)]
        + [send(total, target=lambda s, d, flip=flip: (s, d ^ flip)) for flip in (2, 3)]
    ).reshape(2, 2, rows, cols)
    held = jnp.where(x_bit == 0, held, held[::-1])
    held = jnp.where(core == 0, held, held[:, ::-1])
    return held.astype(wide).transpose(0, 2, 1, 3).reshape(2 * rows, 2 * cols)


def reduce_gain(gain_grad, seq_count, dp_count):
    share = gain_grad.shape[0] // seq_count
    spread = jnp.broadcast_to(
        gain_grad.reshape(seq_count, 1, share), (seq_count, dp_count, share)
    ).reshape(seq_count * dp_count, share)
    arrived = lax.all_to_all(spread, ("seq", "dp"), split_axis=0, concat_axis=0, tiled=True)
    return jnp.sum(arrived, axis=0)


def together(*values):
    return lax.optimization_barrier(values)


def per_device(patches, lengths, token_dest, gain, w_qkv, w_out, cotangent):
    seq_count = lax.axis_size("seq")
    dp_count = lax.axis_size("dp")
    send = functools.partial(joint_permute, seq_count=seq_count, dp_count=dp_count)
    place = position()
    patch_rows, shard_lengths = patches[0], lengths[0, 0]
    row_count, model_width = patch_rows.shape
    token_count = row_count // GROUP

    far = gather_far(place, w_out, seq_count, send)
    returned = lax.all_to_all(cotangent[0], "seq", split_axis=0, concat_axis=0, tiled=True)
    projected, attended, att_turned, lse = forward(patch_rows, shard_lengths, gain, w_qkv)
    projected, attended, att_turned, lse, far = together(
        projected, attended, att_turned, lse, far
    )
    level = jnp.stack(far)
    near = send(level, target=second_target)
    beyond = send(level, target=first_target)
    att_other = send(att_turned, target=core_target)
    block_grad, away = place_rows(token_dest, returned)
    grad_other = send(away, target=core_target)
    corner = send(near, target=first_target)
    att_other, grad_other, near, beyond = together(att_other, grad_other, near, beyond)
    kept, away = weight_terms(
        place, att_turned, att_other, block_grad, grad_other, seq_count // 2
    )
    kept, away, corner = together(kept, away, corner)
    held = [level, near, beyond, corner]
    held = held + [send(one, target=core_target) for one in held]
    arrived = send(away, target=first_target)
    pieces = gathered_pieces(place, held)
    outgoing, grad_attended = project(token_dest, patch_rows, attended, block_grad, pieces)
    merged = lax.all_to_all(
        outgoing.reshape(seq_count, token_count // seq_count, GROUP * model_width),
        "seq", split_axis=0, concat_axis=0, tiled=True,
    ).reshape(token_count, GROUP * model_width)
    kept, grad_attended = together(add_low(kept, arrived), grad_attended)
    arrived = send(kept[1], target=second_target)
    grads = attention_grad(shard_lengths, projected, grad_attended, lse)
    level, grads = together(add_low(kept[0], arrived), grads)
    terms = [level[0]] + [
        send(level[step], target=far_target(step)) for step in range(1, seq_count // 2)
    ]
    patch_grad, gain_grad = norm_grad(patch_rows, gain, w_qkv, grads, block_grad)
    patch_grad, gain_grad, merged, terms = together(patch_grad, gain_grad, merged, terms)
    total = sum(term.astype(wide) for term in terms).astype(low)
    own_weight = share_weight(place, total, send)
    own_gain = reduce_gain(gain_grad[0], seq_count, dp_count)
    norm_scale = 1.0 / math.sqrt(row_count * seq_count * dp_count)
    return (merged[None], patch_grad[None], own_weight * norm_scale, own_gain * norm_scale)


def solution(mesh):
    placed = (
        P("dp", "seq", None),
        P("dp", "seq", None),
        P("dp", "seq"),
        P(),
        P(),
        P("seq", None),
        P("dp", "seq", None),
    )
    return jax.shard_map(
        per_device,
        mesh=mesh,
        in_specs=placed,
        out_specs=(P("dp", "seq", None), P("dp", "seq", None), P("seq", None), P("seq")),
        check_vma=False,
    )
```

```python
import functools
import math

import jax
import jax.numpy as jnp
from jax import lax
from jax.experimental import pallas as pl
from jax.experimental.pallas import tpu as pltpu
from jax.sharding import PartitionSpec as P

HEADS = 16
GROUP = 4
HALVES = 2
LANES = 128
CHUNK = 64
LOG2_E = math.log2(math.e)
VMEM_LIMIT = 20 * 1024 * 1024
PART = 256
HBM_BYTES_PER_US = 3690000

eps = 1e-06
low = jnp.bfloat16
wide = jnp.float32


def params():
    return pltpu.CompilerParams(vmem_limit_bytes=VMEM_LIMIT)


def cost(microseconds, flops):
    nominal = microseconds * HBM_BYTES_PER_US
    return pl.CostEstimate(flops=flops, bytes_accessed=nominal, transcendentals=0)


def smem():
    return pl.BlockSpec(memory_space=pltpu.SMEM)


def vmem():
    return pl.BlockSpec(memory_space=pltpu.VMEM)


def dot_nt(left, right):
    return lax.dot_general(left, right, (((1,), (1,)), ((), ())), preferred_element_type=wide)


def dot_tn(left, right):
    return lax.dot_general(left, right, (((0,), (0,)), ((), ())), preferred_element_type=wide)


def dot_nn(left, right):
    return jnp.dot(left, right, preferred_element_type=wide)


def head_windows(head_size, width):
    windows = []
    for start in range(0, width, head_size):
        first = start // LANES * LANES
        last = -(-(start + head_size) // LANES) * LANES
        windows.append((start, start + head_size, first, last))
    return windows


def image_bias(lengths_ref, row_count):
    def image_of(index):
        number = jnp.zeros(index.shape, jnp.int32)
        end = jnp.int32(0)
        for image in range(lengths_ref.shape[0]):
            end = end + lengths_ref[image] * GROUP
            number = number + (index >= end).astype(jnp.int32)
        return number

    rows = lax.broadcasted_iota(jnp.int32, (row_count, row_count), 0)
    cols = lax.broadcasted_iota(jnp.int32, (row_count, row_count), 1)
    return jnp.where(image_of(rows) == image_of(cols), 0.0, -jnp.inf).astype(wide)


def standardise(rows):
    centred = rows - jnp.mean(rows, axis=-1, keepdims=True)
    inv_spread = lax.rsqrt(jnp.mean(centred * centred, axis=-1, keepdims=True) + eps)
    return centred * inv_spread, inv_spread


def anywhere():
    return pl.BlockSpec(memory_space=pl.ANY)


def only(window, first, last, value):
    lane = lax.broadcasted_iota(jnp.int32, (1, last - first), 1) + first
    keep = (lane >= window[0]) & (lane < window[1])
    return value * jnp.where(keep, 1.0, 0.0).astype(low)


class Copies:
    def __init__(self, sems):
        self.sems = sems
        self.used = 0

    def start(self, source, target):
        copy = pltpu.make_async_copy(source, target, self.sems.at[self.used])
        self.used += 1
        copy.start()
        return copy


def wait_all(copies):
    for copy in copies:
        copy.wait()


def position():
    s, d = lax.axis_index("seq"), lax.axis_index("dp")
    return d % 2, d // 2, s % 2, s // 2


def row_chunks(row_count):
    return [slice(first, first + CHUNK) for first in range(0, row_count, CHUNK)]


def forward_kernel(
    score_scale, head_size, lengths_ref, x_hbm, gain_ref, w_hbm,
    proj_ref, att_ref, att_t_ref, lse_ref,
    x_buf, w_buf, normed, bias, scores, probs, x_sem, w_sems,
):
    row_count, model_width = x_buf.shape
    half_width = model_width // HALVES
    windows = head_windows(head_size, half_width)

    def w_copies(half, kind):
        first = pl.multiple_of(kind * model_width + half * half_width, LANES)
        return [
            pltpu.make_async_copy(
                w_hbm.at[part * PART : (part + 1) * PART, pl.ds(first, half_width)],
                w_buf.at[half, kind, part * PART : (part + 1) * PART],
                w_sems.at[half, kind, part],
            )
            for part in range(model_width // PART)
        ]

    x_copy = pltpu.make_async_copy(x_hbm, x_buf, x_sem)
    x_copy.start()
    for half in range(HALVES):
        for kind in range(3):
            for copy in w_copies(half, kind):
                copy.start()
    bias[...] = image_bias(lengths_ref, row_count)
    x_copy.wait()
    standard, _ = standardise(x_buf[...].astype(wide))
    normed[...] = (standard * gain_ref[...]).astype(low)

    @pl.loop(0, HALVES)
    def _(half):
        for kind in range(3):
            wait_all(w_copies(half, kind))
            proj_ref[half, kind] = dot_nn(normed[...], w_buf[half, kind]).astype(low)
        for head, (start, stop, first, last) in enumerate(windows):
            queries = only((start, stop), first, last, proj_ref[half, 0, :, first:last])
            scores[head] = dot_nt(queries, proj_ref[half, 1, :, first:last])

        @pl.loop(0, row_count // CHUNK)
        def _(chunk):
            rows = pl.ds(pl.multiple_of(chunk * CHUNK, CHUNK), CHUNK)
            lane = lax.broadcasted_iota(jnp.int32, (CHUNK, LANES), 1)
            lse = jnp.zeros((CHUNK, LANES), wide)
            for head in range(len(windows)):
                scaled = scores[head, rows] * (score_scale * LOG2_E) + bias[rows]
                row_max = jnp.max(scaled, axis=-1, keepdims=True)
                weights = jnp.exp2(scaled - row_max)
                total = jnp.sum(weights, axis=-1, keepdims=True)
                probs[head, rows] = (weights * (1.0 / total)).astype(low)
                lse = jnp.where(lane == head, row_max + jnp.log2(total), lse)
            lse_ref[half, rows] = lse

        for first in range(0, half_width, LANES):
            last = first + LANES
            tile = None
            for head, (start, stop, _, _) in enumerate(windows):
                if start < last and stop > first:
                    values = only((start, stop), first, last, proj_ref[half, 2, :, first:last])
                    term = dot_nn(probs[head], values)
                    tile = term if tile is None else tile + term
            tile = tile.astype(low)
            att_ref[half, :, first:last] = tile
            att_t_ref[half, first:last, :] = tile.T


def forward(patch_rows, shard_lengths, gain, w_qkv):
    row_count, model_width = patch_rows.shape
    half_width = model_width // HALVES
    head_size = model_width // HEADS
    heads = HEADS // HALVES
    kernel = functools.partial(forward_kernel, 1.0 / math.sqrt(head_size), head_size)
    return pl.pallas_call(
        kernel,
        in_specs=[smem(), anywhere(), vmem(), anywhere()],
        out_specs=[vmem()] * 4,
        out_shape=[
            jax.ShapeDtypeStruct((HALVES, 3, row_count, half_width), low),
            jax.ShapeDtypeStruct((HALVES, row_count, half_width), low),
            jax.ShapeDtypeStruct((HALVES, half_width, row_count), low),
            jax.ShapeDtypeStruct((HALVES, row_count, LANES), wide),
        ],
        scratch_shapes=[
            pltpu.VMEM((row_count, model_width), low),
            pltpu.VMEM((HALVES, 3, model_width, half_width), low),
            pltpu.VMEM((row_count, model_width), low),
            pltpu.VMEM((row_count, row_count), wide),
            pltpu.VMEM((heads, row_count, row_count), wide),
            pltpu.VMEM((heads, row_count, row_count), low),
            pltpu.SemaphoreType.DMA,
            pltpu.SemaphoreType.DMA((HALVES, 3, model_width // PART)),
        ],
        compiler_params=params(),
        cost_estimate=cost(9, 0),
        name="forward",
    )(shard_lengths, patch_rows, gain, w_qkv)


def attention_grad_kernel(
    score_scale, head_size, lengths_ref, proj_ref, ga_ref, lse_ref, out_ref,
    bias, scores, grad_probs, probs, grad_scores, turned,
):
    _, row_count, half_width = ga_ref.shape
    windows = head_windows(head_size, half_width)
    bias[...] = image_bias(lengths_ref, row_count)

    @pl.loop(0, HALVES)
    def _(half):
        for head, (start, stop, first, last) in enumerate(windows):
            query = only((start, stop), first, last, proj_ref[half, 0, :, first:last])
            scores[head] = dot_nt(query, proj_ref[half, 1, :, first:last])
            grad_att = only((start, stop), first, last, ga_ref[half, :, first:last])
            grad_probs[head] = dot_nt(grad_att, proj_ref[half, 2, :, first:last])
        turned[0] = proj_ref[half, 1].T
        turned[1] = proj_ref[half, 0].T
        turned[2] = ga_ref[half].T

        @pl.loop(0, row_count // CHUNK)
        def _(chunk):
            rows = pl.ds(pl.multiple_of(chunk * CHUNK, CHUNK), CHUNK)
            lse = lse_ref[half, rows]
            for head in range(len(windows)):
                scaled = scores[head, rows] * (score_scale * LOG2_E) + bias[rows]
                chance = jnp.exp2(scaled - lse[:, head : head + 1])
                incoming = grad_probs[head, rows]
                inner = jnp.sum(incoming * chance, axis=-1, keepdims=True)
                probs[head, rows] = chance.astype(low)
                grad_scores[head, rows] = (chance * (incoming - inner) * score_scale).astype(low)

        for head in range(len(windows)):
            rows = slice(head * head_size, (head + 1) * head_size)
            out_ref[0, half, rows] = dot_nt(turned[0, rows], grad_scores[head]).astype(low)
            out_ref[1, half, rows] = dot_nn(turned[1, rows], grad_scores[head]).astype(low)
            out_ref[2, half, rows] = dot_nn(turned[2, rows], probs[head]).astype(low)


def attention_grad(shard_lengths, projected, grad_attended, lse):
    _, row_count, half_width = grad_attended.shape
    heads = HEADS // HALVES
    head_size = half_width // heads
    kernel = functools.partial(attention_grad_kernel, 1.0 / math.sqrt(head_size), head_size)
    return pl.pallas_call(
        kernel,
        in_specs=[smem(), vmem(), vmem(), vmem()],
        out_specs=vmem(),
        out_shape=jax.ShapeDtypeStruct((3, HALVES, half_width, row_count), low),
        scratch_shapes=[
            pltpu.VMEM((row_count, row_count), wide),
            pltpu.VMEM((heads, row_count, row_count), wide),
            pltpu.VMEM((heads, row_count, row_count), wide),
            pltpu.VMEM((heads, row_count, row_count), low),
            pltpu.VMEM((heads, row_count, row_count), low),
            pltpu.VMEM((3, half_width, row_count), low),
        ],
        compiler_params=params(),
        cost_estimate=cost(9, 0),
        name="attention_grad",
    )(shard_lengths, projected, grad_attended, lse)


def norm_grad_kernel(
    copies_each, x_ref, gain_ref, w_ref, grad_ref, bg_ref, patch_hbm, gain_out_ref,
    grad_normed, patch_buf, sems,
):
    row_count, model_width = x_ref.shape
    half_width = model_width // HALVES
    grads = grad_ref[...].reshape(3 * model_width, row_count)

    @pl.loop(0, model_width // PART)
    def _(part):
        cols = pl.ds(pl.multiple_of(part * PART, PART), PART)
        grad_normed[:, cols] = dot_nn(w_ref[cols, :], grads).T

    copies = Copies(sems)
    sent = []
    total = None
    for row in range(0, row_count, LANES):
        rows = slice(row, row + LANES)
        standard, inv_spread = standardise(x_ref[rows].astype(wide))
        grad = grad_normed[rows]
        term = jnp.sum(grad * standard, axis=0, keepdims=True)
        total = term if total is None else total + term
        grad = grad * gain_ref[...]
        branch = inv_spread * (
            grad
            - jnp.mean(grad, axis=-1, keepdims=True)
            - standard * jnp.mean(grad * standard, axis=-1, keepdims=True)
        )
        for half in range(HALVES):
            cols = slice(half * half_width, (half + 1) * half_width)
            incoming = bg_ref[half, rows].astype(wide)
            patch_buf[rows, cols] = (incoming + branch[:, cols]).astype(low)
        sent.append(copies.start(patch_buf.at[rows], patch_hbm.at[rows]))
    share = gain_out_ref.shape[2]
    for number in range(model_width // share):
        term = total[:, number * share : (number + 1) * share]
        for copy in range(copies_each):
            gain_out_ref[number * copies_each + copy] = term
    wait_all(sent)


def norm_grad(patch_rows, gain, w_qkv, grads, block_grad, seq_count, dp_count):
    row_count, model_width = patch_rows.shape
    share = model_width // seq_count
    return pl.pallas_call(
        functools.partial(norm_grad_kernel, dp_count),
        in_specs=[vmem()] * 5,
        out_specs=[anywhere(), vmem()],
        out_shape=[
            jax.ShapeDtypeStruct((row_count, model_width), low),
            jax.ShapeDtypeStruct((seq_count * dp_count, 1, share), wide),
        ],
        scratch_shapes=[
            pltpu.VMEM((row_count, model_width), wide),
            pltpu.VMEM((row_count, model_width), low),
            pltpu.SemaphoreType.DMA((row_count // LANES,)),
        ],
        compiler_params=params(),
        cost_estimate=cost(7, 0),
        name="norm_grad",
    )(patch_rows, gain, w_qkv, grads, block_grad)


def placing_matrix(dest_ref, row_count):
    token_count = row_count // GROUP
    peer_count = token_count // lax.axis_size("seq")
    token_bits = token_count.bit_length() - 1
    dest = dest_ref[...]
    shard = lax.shift_right_logical(dest, jnp.full_like(dest, token_bits))
    slot = shard * peer_count + (dest & (peer_count - 1))
    square = (token_count, token_count)
    chosen = (lax.broadcasted_iota(jnp.int32, square, 0) == slot).astype(low)
    shape = (token_count, row_count)
    token = lax.broadcasted_iota(jnp.int32, shape, 0) * GROUP
    row = lax.broadcasted_iota(jnp.int32, shape, 1)
    parts = []
    for member in range(GROUP):
        spread = (row == token + member).astype(low)
        parts.append(dot_nn(chosen, spread).astype(low))
    return jnp.concatenate(parts, axis=0)


def place_kernel(dest_ref, returned_ref, grad_ref, away_ref, stacked):
    token_count = returned_ref.shape[0]
    row_count, model_width = stacked.shape
    half_width = model_width // HALVES
    for member in range(GROUP):
        stacked[member * token_count : (member + 1) * token_count] = returned_ref[
            :, member * model_width : (member + 1) * model_width
        ]
    placing = placing_matrix(dest_ref, row_count)
    core = position()[0]
    for half in range(HALVES):
        cols = slice(half * half_width, (half + 1) * half_width)
        grad_ref[half] = dot_tn(placing, stacked[:, cols]).astype(low)
    away_ref[...] = grad_ref[1 - core]


def place_rows(token_dest, returned):
    token_count, merged_width = returned.shape
    row_count, model_width = token_count * GROUP, merged_width // GROUP
    half_width = model_width // HALVES
    return pl.pallas_call(
        place_kernel,
        in_specs=[vmem(), vmem()],
        out_specs=[vmem(), vmem()],
        out_shape=[
            jax.ShapeDtypeStruct((HALVES, row_count, half_width), low),
            jax.ShapeDtypeStruct((row_count, half_width), low),
        ],
        scratch_shapes=[pltpu.VMEM((row_count, model_width), low)],
        compiler_params=params(),
        cost_estimate=cost(3, 0),
        name="place_rows",
    )(token_dest, returned)


def weight_kernel(rows, att_ref, att_other_ref, bg_ref, bg_other_ref, kept_ref, away_ref):
    core, x_bit, y_bit, z_index = position()
    group = 4 * rows
    model_width, row_count = att_ref.shape[0] * att_ref.shape[1], att_ref.shape[2]
    own = att_ref[...].reshape(model_width, row_count)
    other = att_other_ref[...].reshape(model_width, row_count)
    for far in range(model_width // group):
        part = slice(far * group, (far + 1) * group)
        terms = dot_nn(own[part], bg_ref[core]) + dot_nn(other[part], bg_other_ref[...])
        terms = terms.astype(low)
        z_off = far ^ z_index
        for index in range(4):
            x_off, y_off = (index % 2) ^ x_bit, (index // 2) ^ y_bit
            first = jnp.where(core == 0, x_off, y_off)
            second = jnp.where(core == 0, y_off, x_off)
            piece = terms[index * rows : (index + 1) * rows]

            @pl.when(first == 0)
            def _():
                kept_ref[second, z_off] = piece

            @pl.when(first == 1)
            def _():
                away_ref[second, z_off] = piece


def plain_weight_kernel(att_ref, att_other_ref, bg_ref, bg_other_ref, out_ref):
    own = bg_ref[position()[0]]
    terms = dot_nn(att_ref[0], own) + dot_nn(att_other_ref[0], bg_other_ref[...])
    out_ref[...] = terms.astype(low)


def weight_terms(place, att_turned, att_other, block_grad, grad_other, far_count):
    _, half_width, row_count = att_turned.shape
    model_width = half_width * HALVES
    rows = model_width // (4 * far_count)
    if rows % 16 == 0:
        shape = (2, far_count, rows, half_width)
        return pl.pallas_call(
            functools.partial(weight_kernel, rows),
            in_specs=[vmem()] * 4,
            out_specs=[vmem()] * 2,
            out_shape=[jax.ShapeDtypeStruct(shape, low)] * 2,
            compiler_params=params(),
            cost_estimate=cost(3, 0),
            name="weight_terms",
        )(att_turned, att_other, block_grad, grad_other)
    part = pl.BlockSpec((1, half_width, row_count), lambda step: (step, 0, 0))
    terms = pl.pallas_call(
        plain_weight_kernel,
        grid=(HALVES,),
        in_specs=[
            part,
            part,
            pl.BlockSpec((HALVES, row_count, half_width), lambda step: (0, 0, 0)),
            pl.BlockSpec((row_count, half_width), lambda step: (0, 0)),
        ],
        out_specs=pl.BlockSpec((half_width, half_width), lambda step: (step, 0)),
        out_shape=jax.ShapeDtypeStruct((model_width, half_width), low),
        compiler_params=params(),
        cost_estimate=cost(3, 0),
        name="weight_terms",
    )(att_turned, att_other, block_grad, grad_other)
    core, x_bit, y_bit, z_index = place
    terms = terms.reshape(far_count, 2, 2, rows, half_width)
    terms = terms[jnp.arange(far_count) ^ z_index]
    ordered = []
    for first in range(2):
        for second in range(2):
            y = y_bit ^ jnp.where(core == 0, second, first)
            x = x_bit ^ jnp.where(core == 0, first, second)
            size = (far_count, 1, 1, rows, half_width)
            ordered.append(lax.dynamic_slice(terms, (0, y, x, 0, 0), size)[:, 0, 0])
    return jnp.stack(ordered[:2]), jnp.stack(ordered[2:])


def project_kernel(piece_count, dest_ref, x_ref, att_ref, bg_ref, *refs):
    pieces = refs[:piece_count]
    out_ref, ga_ref, weights, sems = refs[piece_count:]
    copies = Copies(sems)
    core, x_bit, y_bit, z_index = position()
    arriving = ([], [])
    for number, piece in enumerate(pieces):
        if piece_count == 2:
            arriving[number].append(copies.start(piece, weights.at[core ^ number]))
            continue
        side, near = number // 4, number % 4
        column = core ^ side
        low_bit, high_bit = near % 2, near // 2
        y = y_bit ^ jnp.where(column == 0, low_bit, high_bit)
        x = x_bit ^ jnp.where(column == 0, high_bit, low_bit)
        for far in range(piece.shape[0]):
            row = ((z_index ^ far) * 2 + y) * 2 + x
            arriving[side].append(copies.start(piece.at[far], weights.at[column, row]))
    row_count, model_width = x_ref.shape
    half_width = model_width // HALVES
    token_count = row_count // GROUP
    placing = placing_matrix(dest_ref, row_count)
    for side in range(HALVES):
        wait_all(arriving[side])
        column = core ^ side
        first = pl.multiple_of(column * half_width, LANES)
        matrix = weights[column].reshape(model_width, half_width)
        branch = dot_nn(att_ref[0], matrix[:half_width])
        branch = branch + dot_nn(att_ref[1], matrix[half_width:])
        block = (x_ref[:, pl.ds(first, half_width)].astype(wide) + branch).astype(low)
        tokens = dot_nn(placing, block).astype(low)
        for member in range(GROUP):
            place = pl.multiple_of(member * model_width + first, LANES)
            rows = slice(member * token_count, (member + 1) * token_count)
            out_ref[:, pl.ds(place, half_width)] = tokens[rows]
    halves = [weights[half].reshape(model_width, half_width) for half in range(HALVES)]
    for half in range(HALVES):
        rows = slice(half * half_width, (half + 1) * half_width)
        grad = dot_nt(bg_ref[0], halves[0][rows]) + dot_nt(bg_ref[1], halves[1][rows])
        ga_ref[half] = grad.astype(low)


def project(token_dest, patch_rows, attended, block_grad, pieces):
    row_count, model_width = patch_rows.shape
    half_width = model_width // HALVES
    if len(pieces) == 2:
        scratch, arrivals = (HALVES, model_width, half_width), 2
    else:
        far_count, rows, _ = pieces[0].shape
        scratch, arrivals = (HALVES, 4 * far_count, rows, half_width), 8 * far_count
    return pl.pallas_call(
        functools.partial(project_kernel, len(pieces)),
        in_specs=[vmem()] * 4 + [anywhere()] * len(pieces),
        out_specs=[vmem(), vmem()],
        out_shape=[
            jax.ShapeDtypeStruct((row_count // GROUP, GROUP * model_width), low),
            jax.ShapeDtypeStruct((HALVES, row_count, half_width), low),
        ],
        scratch_shapes=[
            pltpu.VMEM(scratch, low),
            pltpu.SemaphoreType.DMA((arrivals,)),
        ],
        compiler_params=params(),
        cost_estimate=cost(6, 0),
        name="project",
    )(token_dest, patch_rows, attended, block_grad, *pieces)


def finish_kernel(norm_scale, own_ref, core_ref, x_ref, both_ref, out_ref):
    core, x_bit, _, _ = position()
    rows, cols = own_ref.shape
    for x_off, pair in enumerate(((own_ref, core_ref), (x_ref, both_ref))):
        for core_off, piece in enumerate(pair):
            to_rows = pl.ds(pl.multiple_of((x_bit ^ x_off) * rows, rows), rows)
            to_cols = pl.ds(pl.multiple_of((core ^ core_off) * cols, LANES), cols)
            out_ref[to_rows, to_cols] = piece[...].astype(wide) * norm_scale


def finish_weight(held, norm_scale):
    rows, cols = held[0].shape
    whole = lambda step: (0, 0)
    return pl.pallas_call(
        functools.partial(finish_kernel, norm_scale),
        grid=(1,),
        in_specs=[vmem()] * 4,
        out_specs=pl.BlockSpec((2 * rows, 2 * cols), whole),
        out_shape=jax.ShapeDtypeStruct((2 * rows, 2 * cols), wide),
        compiler_params=params(),
        cost_estimate=cost(1, 0),
        name="finish_weight",
    )(*held)


def joint_permute(value, seq_count, dp_count, target):
    pairs = []
    for s in range(seq_count):
        for d in range(dp_count):
            to_s, to_d = target(s, d)
            pairs.append((s * dp_count + d, to_s * dp_count + to_d))
    return lax.ppermute(value, ("seq", "dp"), pairs)


def core_target(s, d):
    return s, d ^ 1


def first_target(s, d):
    return (s, d ^ 2) if d % 2 == 0 else (s ^ 1, d)


def second_target(s, d):
    return (s ^ 1, d) if d % 2 == 0 else (s, d ^ 2)


def far_target(step):
    return lambda s, d: (s ^ (2 * step), d)


def gather_far(place, w_out, seq_count, send):
    share, model_width = w_out.shape
    rows, cols = share // 2, model_width // 2
    core, x_bit = place[0], place[1]
    own = lax.dynamic_slice(w_out, (x_bit * rows, core * cols), (rows, cols))
    return [own] + [send(own, target=far_target(step)) for step in range(1, seq_count // 2)]


def gathered_pieces(place, held):
    far_count, rows, cols = held[0].shape
    if rows % 16 == 0:
        return held
    core, x_bit, y_bit, z_index = place
    held = jnp.stack(held).reshape(2, 4, far_count, rows, cols)
    held = held[:, :, jnp.arange(far_count) ^ z_index]
    columns = []
    for side in range(2):
        blocks = []
        for y in range(2):
            for x in range(2):
                y_off, x_off = y ^ y_bit, x ^ x_bit
                near_place = jnp.where(core == side, y_off + 2 * x_off, x_off + 2 * y_off)
                blocks.append(
                    lax.dynamic_index_in_dim(held[side], near_place, 0, keepdims=False)
                )
        columns.append(jnp.stack(blocks, axis=1).reshape(2 * cols, cols))
    return columns


def add_low(left, right):
    return (left.astype(wide) + right.astype(wide)).astype(low)


def share_weight(place, total, send, norm_scale):
    rows, cols = total.shape
    core, x_bit = place[0], place[1]
    held = [total, send(total, target=core_target)]
    held += [send(total, target=lambda s, d, flip=flip: (s, d ^ flip)) for flip in (2, 3)]
    if rows % 16 == 0:
        return finish_weight(held, norm_scale)
    held = jnp.stack(held).reshape(2, 2, rows, cols)
    held = jnp.where(x_bit == 0, held, held[::-1])
    held = jnp.where(core == 0, held, held[:, ::-1])
    return held.astype(wide).transpose(0, 2, 1, 3).reshape(2 * rows, 2 * cols) * norm_scale


def together(*values):
    return lax.optimization_barrier(values)


def per_device(patches, lengths, token_dest, gain, w_qkv, w_out, cotangent):
    seq_count = lax.axis_size("seq")
    dp_count = lax.axis_size("dp")
    send = functools.partial(joint_permute, seq_count=seq_count, dp_count=dp_count)
    place = position()
    patch_rows, shard_lengths = patches[0], lengths[0, 0]
    row_count, model_width = patch_rows.shape
    token_count = row_count // GROUP

    far = gather_far(place, w_out, seq_count, send)
    cotangent, patch_rows, far[1] = together(cotangent, patch_rows, far[1])
    returned = lax.all_to_all(cotangent[0], "seq", split_axis=0, concat_axis=0, tiled=True)
    projected, attended, att_turned, lse = forward(patch_rows, shard_lengths, gain, w_qkv)
    projected, attended, att_turned, lse, far = together(
        projected, attended, att_turned, lse, far
    )
    level = jnp.stack(far)
    near = send(level, target=second_target)
    beyond = send(level, target=first_target)
    att_other = send(att_turned, target=core_target)
    block_grad, away = place_rows(token_dest, returned)
    grad_other = send(away, target=core_target)
    near, _ = together(near, block_grad)
    corner = send(near, target=first_target)
    att_other, grad_other, beyond = together(att_other, grad_other, beyond)
    kept, away = weight_terms(
        place, att_turned, att_other, block_grad, grad_other, seq_count // 2
    )
    kept, away, corner = together(kept, away, corner)
    held = [level, near, beyond, corner]
    held = held + [send(one, target=core_target) for one in held]
    arrived = send(away, target=first_target)
    pieces = gathered_pieces(place, held)
    outgoing, grad_attended = project(token_dest, patch_rows, attended, block_grad, pieces)
    merged = lax.all_to_all(
        outgoing.reshape(seq_count, token_count // seq_count, GROUP * model_width),
        "seq", split_axis=0, concat_axis=0, tiled=True,
    ).reshape(token_count, GROUP * model_width)
    kept, grad_attended = together(add_low(kept, arrived), grad_attended)
    arrived = send(kept[1], target=second_target)
    grads = attention_grad(shard_lengths, projected, grad_attended, lse)
    level, grads = together(add_low(kept[0], arrived), grads)
    terms = [level[0]] + [
        send(level[step], target=far_target(step)) for step in range(1, seq_count // 2)
    ]
    patch_grad, gain_grad = norm_grad(
        patch_rows, gain, w_qkv, grads, block_grad, seq_count, dp_count
    )
    patch_grad, gain_grad, merged, terms = together(patch_grad, gain_grad, merged, terms)
    norm_scale = 1.0 / math.sqrt(row_count * seq_count * dp_count)
    arrived = lax.all_to_all(gain_grad, ("seq", "dp"), split_axis=0, concat_axis=0, tiled=True)
    own_gain = jnp.sum(arrived, axis=(0, 1)) * norm_scale
    total = sum(term.astype(wide) for term in terms).astype(low)
    own_weight = share_weight(place, total, send, norm_scale)
    return (merged[None], patch_grad[None], own_weight, own_gain)


def solution(mesh):
    placed = (
        P("dp", "seq", None),
        P("dp", "seq", None),
        P("dp", "seq"),
        P(),
        P(),
        P("seq", None),
        P("dp", "seq", None),
    )
    return jax.shard_map(
        per_device,
        mesh=mesh,
        in_specs=placed,
        out_specs=(P("dp", "seq", None), P("dp", "seq", None), P("seq", None), P("seq")),
        check_vma=False,
    )
```

```python
import functools
import math

import jax
import jax.numpy as jnp
from jax import lax
from jax.experimental import pallas as pl
from jax.experimental.pallas import tpu as pltpu
from jax.sharding import PartitionSpec as P

HEADS = 16
GROUP = 4
HALVES = 2
LANES = 128
CHUNK = 64
LOG2_E = math.log2(math.e)
VMEM_LIMIT = 24 * 1024 * 1024
PART = 256
HBM_BYTES_PER_US = 3690000

eps = 1e-06
low = jnp.bfloat16
wide = jnp.float32


def params():
    return pltpu.CompilerParams(vmem_limit_bytes=VMEM_LIMIT)


def cost(microseconds, flops):
    nominal = microseconds * HBM_BYTES_PER_US
    return pl.CostEstimate(flops=flops, bytes_accessed=nominal, transcendentals=0)


def smem():
    return pl.BlockSpec(memory_space=pltpu.SMEM)


def vmem():
    return pl.BlockSpec(memory_space=pltpu.VMEM)


def dot_nt(left, right):
    return lax.dot_general(left, right, (((1,), (1,)), ((), ())), preferred_element_type=wide)


def dot_tn(left, right):
    return lax.dot_general(left, right, (((0,), (0,)), ((), ())), preferred_element_type=wide)


def dot_nn(left, right):
    return jnp.dot(left, right, preferred_element_type=wide)


def head_windows(head_size, width):
    windows = []
    for start in range(0, width, head_size):
        first = start // LANES * LANES
        last = -(-(start + head_size) // LANES) * LANES
        windows.append((start, start + head_size, first, last))
    return windows


def image_bias(lengths_ref, row_count):
    def image_of(index):
        number = jnp.zeros(index.shape, jnp.int32)
        end = jnp.int32(0)
        for image in range(lengths_ref.shape[0]):
            end = end + lengths_ref[image] * GROUP
            number = number + (index >= end).astype(jnp.int32)
        return number

    rows = lax.broadcasted_iota(jnp.int32, (row_count, row_count), 0)
    cols = lax.broadcasted_iota(jnp.int32, (row_count, row_count), 1)
    return jnp.where(image_of(rows) == image_of(cols), 0.0, -jnp.inf).astype(wide)


def standardise(rows):
    centred = rows - jnp.mean(rows, axis=-1, keepdims=True)
    inv_spread = lax.rsqrt(jnp.mean(centred * centred, axis=-1, keepdims=True) + eps)
    return centred * inv_spread, inv_spread


def anywhere():
    return pl.BlockSpec(memory_space=pl.ANY)


def outside():
    return pl.BlockSpec(memory_space=pltpu.HBM)


def only(window, first, last, value):
    lane = lax.broadcasted_iota(jnp.int32, (1, last - first), 1) + first
    keep = (lane >= window[0]) & (lane < window[1])
    return value * jnp.where(keep, 1.0, 0.0).astype(low)


class Copies:
    def __init__(self, sems):
        self.sems = sems
        self.used = 0

    def start(self, source, target):
        copy = pltpu.make_async_copy(source, target, self.sems.at[self.used])
        self.used += 1
        copy.start()
        return copy


def wait_all(copies):
    for copy in copies:
        copy.wait()


def position():
    s, d = lax.axis_index("seq"), lax.axis_index("dp")
    return d % 2, d // 2, s % 2, s // 2


def relative_block(block):
    core, x_bit, y_bit, z_index = position()
    x_off, y_off = (block % 2) ^ x_bit, (block // 2 % 2) ^ y_bit
    z_off = (block // 4) ^ z_index
    return jnp.where(core == 0, y_off + 2 * x_off, x_off + 2 * y_off), z_off


def forward_kernel(
    score_scale, head_size, relative, lengths_ref, x_hbm, gain_ref, w_hbm,
    proj_ref, keys_t_ref, att_t_ref, lse_ref, w_ref,
    x_buf, normed, turned, bias, scores, probs, x_sem, w_sems,
):
    row_count, model_width = x_buf.shape
    half_width = model_width // HALVES
    heads = half_width // head_size
    windows = head_windows(head_size, half_width)

    def w_copies(half, kind):
        first = pl.multiple_of(kind * model_width + half * half_width, LANES)
        return [
            pltpu.make_async_copy(
                w_hbm.at[part * PART : (part + 1) * PART, pl.ds(first, half_width)],
                w_ref.at[half, kind, part * PART : (part + 1) * PART],
                w_sems.at[half, kind, part],
            )
            for part in range(model_width // PART)
        ]

    x_copy = pltpu.make_async_copy(x_hbm, x_buf, x_sem)
    x_copy.start()
    for half in range(HALVES):
        for kind in range(3):
            for copy in w_copies(half, kind):
                copy.start()
    bias[...] = image_bias(lengths_ref, row_count)
    x_copy.wait()
    standard, _ = standardise(x_buf[...].astype(wide))
    normed[...] = (standard * gain_ref[...]).astype(low)

    @pl.loop(0, HALVES)
    def _(half):
        for kind in range(3):
            wait_all(w_copies(half, kind))
            proj_ref[half, kind] = dot_nn(normed[...], w_ref[half, kind]).astype(low)
            if kind == 1:
                keys_t_ref[half] = proj_ref[half, 1].T
        for head, (start, stop, first, last) in enumerate(windows):
            queries = only((start, stop), first, last, proj_ref[half, 0, :, first:last])
            scores[head] = dot_nn(queries, keys_t_ref[half, first:last, :])

        @pl.loop(0, row_count // CHUNK)
        def _(chunk):
            rows = pl.ds(pl.multiple_of(chunk * CHUNK, CHUNK), CHUNK)
            lane = lax.broadcasted_iota(jnp.int32, (CHUNK, LANES), 1)
            lse = jnp.zeros((CHUNK, LANES), wide)
            for head in range(heads):
                scaled = scores[head, rows] * (score_scale * LOG2_E) + bias[rows]
                row_max = jnp.max(scaled, axis=-1, keepdims=True)
                weights = jnp.exp2(scaled - row_max)
                total = jnp.sum(weights, axis=-1, keepdims=True)
                probs[head, rows] = (weights * (1.0 / total)).astype(low)
                lse = jnp.where(lane == head, row_max + jnp.log2(total), lse)
            lse_ref[half, rows] = lse

        for first in range(0, half_width, LANES):
            last = first + LANES
            tile = None
            for head, (start, stop, _, _) in enumerate(windows):
                if start < last and stop > first:
                    values = only((start, stop), first, last, proj_ref[half, 2, :, first:last])
                    term = dot_nn(probs[head], values)
                    tile = term if tile is None else tile + term
            turned[first:last, :] = tile.astype(low).T
        for head in range(heads):
            block = turned[head * head_size : (head + 1) * head_size, :]
            number = half * heads + head
            if relative:
                near, far = relative_block(number)
                att_t_ref[near, far] = block
            else:
                att_t_ref[number] = block


def forward(patch_rows, shard_lengths, gain, w_qkv, far_count):
    row_count, model_width = patch_rows.shape
    half_width = model_width // HALVES
    head_size = model_width // HEADS
    heads = HEADS // HALVES
    relative = 4 * far_count == HEADS
    shape = (4, far_count) if relative else (HEADS,)
    kernel = functools.partial(
        forward_kernel, 1.0 / math.sqrt(head_size), head_size, relative
    )
    return pl.pallas_call(
        kernel,
        in_specs=[smem(), anywhere(), vmem(), outside()],
        out_specs=[vmem()] * 5,
        out_shape=[
            jax.ShapeDtypeStruct((HALVES, 3, row_count, half_width), low),
            jax.ShapeDtypeStruct((HALVES, half_width, row_count), low),
            jax.ShapeDtypeStruct(shape + (head_size, row_count), low),
            jax.ShapeDtypeStruct((HALVES, row_count, LANES), wide),
            jax.ShapeDtypeStruct((HALVES, 3, model_width, half_width), low),
        ],
        scratch_shapes=[
            pltpu.VMEM((row_count, model_width), low),
            pltpu.VMEM((row_count, model_width), low),
            pltpu.VMEM((half_width, row_count), low),
            pltpu.VMEM((row_count, row_count), wide),
            pltpu.VMEM((heads, row_count, row_count), wide),
            pltpu.VMEM((heads, row_count, row_count), low),
            pltpu.SemaphoreType.DMA,
            pltpu.SemaphoreType.DMA((HALVES, 3, model_width // PART)),
        ],
        compiler_params=params(),
        cost_estimate=cost(10, 0),
        name="forward",
    )(shard_lengths, patch_rows, gain, w_qkv)


def attention_grad_kernel(
    score_scale, head_size, lengths_ref, proj_ref, keys_t_ref, lse_ref, *refs
):
    ga_refs, out_ref = refs[:-9], refs[-9]
    ga_t, ga, turned, bias, scores, grad_probs, probs, grad_scores = refs[-8:]
    row_count, half_width = ga.shape
    heads = half_width // head_size
    windows = head_windows(head_size, half_width)
    bias[...] = image_bias(lengths_ref, row_count)
    relative = len(ga_refs) > 1
    for near, ga_ref in enumerate(ga_refs):
        count = HEADS // len(ga_refs)
        ga_t[near * count : (near + 1) * count] = ga_ref[...].reshape(count, head_size, row_count)

    @pl.loop(0, HALVES)
    def _(half):
        for head in range(heads):
            number = half * heads + head
            if relative:
                near, far = relative_block(number)
                number = near * (HEADS // len(ga_refs)) + far
            turned[2, head * head_size : (head + 1) * head_size] = ga_t[number]
        ga[...] = turned[2].T
        turned[0] = proj_ref[half, 0].T
        turned[1] = proj_ref[half, 2].T
        for head, (start, stop, first, last) in enumerate(windows):
            query = only((start, stop), first, last, proj_ref[half, 0, :, first:last])
            scores[head] = dot_nn(query, keys_t_ref[half, first:last, :])
            grad_att = only((start, stop), first, last, ga[:, first:last])
            grad_probs[head] = dot_nn(grad_att, turned[1, first:last, :])

        @pl.loop(0, row_count // CHUNK)
        def _(chunk):
            rows = pl.ds(pl.multiple_of(chunk * CHUNK, CHUNK), CHUNK)
            lse = lse_ref[half, rows]
            for head in range(heads):
                scaled = scores[head, rows] * (score_scale * LOG2_E) + bias[rows]
                chance = jnp.exp2(scaled - lse[:, head : head + 1])
                incoming = grad_probs[head, rows]
                inner = jnp.sum(incoming * chance, axis=-1, keepdims=True)
                probs[head, rows] = chance.astype(low)
                grad_scores[head, rows] = (chance * (incoming - inner) * score_scale).astype(low)

        for first in range(0, half_width, LANES):
            last = first + LANES
            tile = None
            for head, (start, stop, _, _) in enumerate(windows):
                if start < last and stop > first:
                    keys = only((start, stop), first, last, proj_ref[half, 1, :, first:last])
                    term = dot_nn(grad_scores[head], keys)
                    tile = term if tile is None else tile + term
            out_ref[half, 0, first:last] = tile.astype(low).T
        for head in range(heads):
            rows = slice(head * head_size, (head + 1) * head_size)
            out_ref[half, 1, rows] = dot_nn(turned[0, rows], grad_scores[head]).astype(low)
            out_ref[half, 2, rows] = dot_nn(turned[2, rows], probs[head]).astype(low)


def attention_grad(shard_lengths, projected, keys_t, lse, grads_att):
    _, _, row_count, half_width = projected.shape
    heads = HEADS // HALVES
    head_size = half_width // heads
    kernel = functools.partial(attention_grad_kernel, 1.0 / math.sqrt(head_size), head_size)
    return pl.pallas_call(
        kernel,
        in_specs=[smem()] + [vmem()] * (3 + len(grads_att)),
        out_specs=vmem(),
        out_shape=jax.ShapeDtypeStruct((HALVES, 3, half_width, row_count), low),
        scratch_shapes=[
            pltpu.VMEM((HEADS, head_size, row_count), low),
            pltpu.VMEM((row_count, half_width), low),
            pltpu.VMEM((3, half_width, row_count), low),
            pltpu.VMEM((row_count, row_count), wide),
            pltpu.VMEM((heads, row_count, row_count), wide),
            pltpu.VMEM((heads, row_count, row_count), wide),
            pltpu.VMEM((heads, row_count, row_count), low),
            pltpu.VMEM((heads, row_count, row_count), low),
        ],
        compiler_params=params(),
        cost_estimate=cost(8, 0),
        name="attention_grad",
    )(shard_lengths, projected, keys_t, lse, *grads_att)


def normed_grad_kernel(copies_each, x_ref, w_ref, grad_ref, out_ref, gain_out_ref):
    row_count, model_width = x_ref.shape
    grads = grad_ref[...].reshape(3 * model_width, row_count)

    @pl.loop(0, model_width // PART)
    def _(part):
        cols = pl.ds(pl.multiple_of(part * PART, PART), PART)
        weights = jnp.concatenate(
            [w_ref[half, kind, cols, :] for half in range(HALVES) for kind in range(3)], axis=1
        )
        out_ref[:, cols] = dot_nn(weights, grads).T

    total = None
    for row in range(0, row_count, LANES):
        rows = slice(row, row + LANES)
        standard, _ = standardise(x_ref[rows].astype(wide))
        term = jnp.sum(out_ref[rows] * standard, axis=0, keepdims=True)
        total = term if total is None else total + term
    share = gain_out_ref.shape[2]
    for number in range(model_width // share):
        term = total[:, number * share : (number + 1) * share]
        for copy in range(copies_each):
            gain_out_ref[number * copies_each + copy] = term


def normed_grad(patch_rows, w_kept, grads, seq_count, dp_count):
    row_count, model_width = patch_rows.shape
    share = model_width // seq_count
    return pl.pallas_call(
        functools.partial(normed_grad_kernel, dp_count),
        in_specs=[vmem()] * 3,
        out_specs=[vmem()] * 2,
        out_shape=[
            jax.ShapeDtypeStruct((row_count, model_width), wide),
            jax.ShapeDtypeStruct((seq_count * dp_count, 1, share), wide),
        ],
        compiler_params=params(),
        cost_estimate=cost(5, 0),
        name="normed_grad",
    )(patch_rows, w_kept, grads)


def patch_grad_kernel(
    x_ref, gain_ref, grad_ref, bg_own_ref, bg_away_ref, patch_hbm, patch_buf, sems
):
    row_count, model_width = x_ref.shape
    half_width = model_width // HALVES
    core = position()[0]
    copies = Copies(sems)
    sent = []
    for row in range(0, row_count, LANES):
        rows = slice(row, row + LANES)
        standard, inv_spread = standardise(x_ref[rows].astype(wide))
        grad = grad_ref[rows] * gain_ref[...]
        branch = inv_spread * (
            grad
            - jnp.mean(grad, axis=-1, keepdims=True)
            - standard * jnp.mean(grad * standard, axis=-1, keepdims=True)
        )
        for half in range(HALVES):
            cols = slice(half * half_width, (half + 1) * half_width)
            incoming = jnp.where(core == half, bg_own_ref[rows], bg_away_ref[rows])
            patch_buf[rows, cols] = (incoming.astype(wide) + branch[:, cols]).astype(low)
        sent.append(copies.start(patch_buf.at[rows], patch_hbm.at[rows]))
    wait_all(sent)


def patch_grads(patch_rows, gain, grad_normed, bg_own, bg_away):
    row_count, model_width = patch_rows.shape
    return pl.pallas_call(
        patch_grad_kernel,
        in_specs=[vmem()] * 5,
        out_specs=anywhere(),
        out_shape=jax.ShapeDtypeStruct((row_count, model_width), low),
        scratch_shapes=[
            pltpu.VMEM((row_count, model_width), low),
            pltpu.SemaphoreType.DMA((row_count // LANES,)),
        ],
        compiler_params=params(),
        cost_estimate=cost(2, 0),
        name="patch_grads",
    )(patch_rows, gain, grad_normed, bg_own, bg_away)


def placing_matrix(dest_ref, row_count):
    token_count = row_count // GROUP
    peer_count = token_count // lax.axis_size("seq")
    token_bits = token_count.bit_length() - 1
    dest = dest_ref[...]
    shard = lax.shift_right_logical(dest, jnp.full_like(dest, token_bits))
    slot = shard * peer_count + (dest & (peer_count - 1))
    square = (token_count, token_count)
    chosen = (lax.broadcasted_iota(jnp.int32, square, 0) == slot).astype(low)
    shape = (token_count, row_count)
    token = lax.broadcasted_iota(jnp.int32, shape, 0) * GROUP
    row = lax.broadcasted_iota(jnp.int32, shape, 1)
    parts = []
    for member in range(GROUP):
        spread = (row == token + member).astype(low)
        parts.append(dot_nn(chosen, spread).astype(low))
    return jnp.concatenate(parts, axis=0)


def place_kernel(dest_ref, returned_ref, own_ref, away_ref, stacked):
    token_count = returned_ref.shape[0]
    row_count, model_width = stacked.shape
    half_width = model_width // HALVES
    for member in range(GROUP):
        stacked[member * token_count : (member + 1) * token_count] = returned_ref[
            :, member * model_width : (member + 1) * model_width
        ]
    placing = placing_matrix(dest_ref, row_count)
    core = position()[0]
    for side, out_ref in enumerate((own_ref, away_ref)):
        cols = pl.ds(pl.multiple_of((core ^ side) * half_width, LANES), half_width)
        out_ref[...] = dot_tn(placing, stacked[:, cols]).astype(low)


def place_rows(token_dest, returned):
    token_count, merged_width = returned.shape
    row_count, model_width = token_count * GROUP, merged_width // GROUP
    half_width = model_width // HALVES
    return pl.pallas_call(
        place_kernel,
        in_specs=[vmem(), vmem()],
        out_specs=[vmem(), vmem()],
        out_shape=[jax.ShapeDtypeStruct((row_count, half_width), low)] * 2,
        scratch_shapes=[pltpu.VMEM((row_count, model_width), low)],
        compiler_params=params(),
        cost_estimate=cost(1, 0),
        name="place_rows",
    )(token_dest, returned)


def token_kernel(dest_ref, x_ref, own_ref, away_ref, out_ref):
    row_count, model_width = x_ref.shape
    half_width = model_width // HALVES
    token_count = row_count // GROUP
    placing = placing_matrix(dest_ref, row_count)
    core = position()[0]
    for side, branch_ref in enumerate((own_ref, away_ref)):
        first = pl.multiple_of((core ^ side) * half_width, LANES)
        block = x_ref[:, pl.ds(first, half_width)].astype(wide) + branch_ref[...]
        tokens = dot_nn(placing, block.astype(low)).astype(low)
        for member in range(GROUP):
            place = pl.multiple_of(member * model_width + first, LANES)
            rows = slice(member * token_count, (member + 1) * token_count)
            out_ref[:, pl.ds(place, half_width)] = tokens[rows]


def place_tokens(token_dest, patch_rows, own, away):
    row_count, model_width = patch_rows.shape
    return pl.pallas_call(
        token_kernel,
        in_specs=[vmem()] * 4,
        out_specs=vmem(),
        out_shape=jax.ShapeDtypeStruct((row_count // GROUP, GROUP * model_width), low),
        compiler_params=params(),
        cost_estimate=cost(1, 0),
        name="place_tokens",
    )(token_dest, patch_rows, own, away)


def finish_kernel(
    norm_scale, own_ref, core_ref, x_ref, both_ref, gain_ref, merged_hbm,
    out_ref, gain_out_ref, merged_out, sem,
):
    copy = pltpu.make_async_copy(merged_hbm, merged_out, sem)
    copy.start()
    core, x_bit, _, _ = position()
    rows, cols = own_ref.shape
    for x_off, pair in enumerate(((own_ref, core_ref), (x_ref, both_ref))):
        for core_off, piece in enumerate(pair):
            to_rows = pl.ds(pl.multiple_of((x_bit ^ x_off) * rows, rows), rows)
            to_cols = pl.ds(pl.multiple_of((core ^ core_off) * cols, LANES), cols)
            out_ref[to_rows, to_cols] = piece[...].astype(wide) * norm_scale
    gain_out_ref[...] = jnp.sum(gain_ref[...], axis=0) * norm_scale
    copy.wait()


def finish(held, gain_terms, merged, norm_scale):
    rows, cols = held[0].shape
    share = gain_terms.shape[2]
    return pl.pallas_call(
        functools.partial(finish_kernel, norm_scale),
        grid=(1,),
        in_specs=[vmem()] * 5 + [anywhere()],
        out_specs=[
            pl.BlockSpec((2 * rows, 2 * cols), lambda step: (0, 0)),
            pl.BlockSpec((1, share), lambda step: (0, 0)),
            outside(),
        ],
        out_shape=[
            jax.ShapeDtypeStruct((2 * rows, 2 * cols), wide),
            jax.ShapeDtypeStruct((1, share), wide),
            jax.ShapeDtypeStruct(merged.shape, merged.dtype),
        ],
        scratch_shapes=[pltpu.SemaphoreType.DMA],
        compiler_params=params(),
        cost_estimate=cost(1, 0),
        name="finish",
    )(*held, gain_terms, merged)


def joint_permute(value, seq_count, dp_count, target):
    pairs = []
    for s in range(seq_count):
        for d in range(dp_count):
            to_s, to_d = target(s, d)
            pairs.append((s * dp_count + d, to_s * dp_count + to_d))
    return lax.ppermute(value, ("seq", "dp"), pairs)


def core_target(s, d):
    return s, d ^ 1


def first_target(s, d):
    return (s, d ^ 2) if d % 2 == 0 else (s ^ 1, d)


def second_target(s, d):
    return (s ^ 1, d) if d % 2 == 0 else (s, d ^ 2)


def far_target(step):
    return lambda s, d: (s ^ (2 * step), d)


def gather_far(place, w_out, seq_count, send):
    share, model_width = w_out.shape
    rows, cols = share // 2, model_width // 2
    core, x_bit = place[0], place[1]
    own = lax.dynamic_slice(w_out, (x_bit * rows, core * cols), (rows, cols))
    return [own] + [send(own, target=far_target(step)) for step in range(1, seq_count // 2)]


def to_relative(place, blocks, far_count):
    core, x_bit, y_bit, z_index = place
    width = blocks.shape[-1]
    blocks = blocks.reshape(far_count, 2, 2, -1, width)[jnp.arange(far_count) ^ z_index]
    blocks = jnp.where(y_bit == 0, blocks, blocks[:, ::-1])
    blocks = jnp.where(x_bit == 0, blocks, blocks[:, :, ::-1])
    x_first, y_first = blocks.transpose(2, 1, 0, 3, 4), blocks.transpose(1, 2, 0, 3, 4)
    return jnp.where(core == 0, x_first, y_first).reshape((4, far_count) + x_first.shape[3:])


def from_relative(place, blocks):
    core, x_bit, y_bit, z_index = place
    _, far_count, rows, width = blocks.shape
    blocks = blocks.reshape(2, 2, far_count, rows, width)
    y_first = blocks.transpose(2, 0, 1, 3, 4)
    blocks = jnp.where(core == 0, blocks.transpose(2, 1, 0, 3, 4), y_first)
    blocks = jnp.where(y_bit == 0, blocks, blocks[:, ::-1])
    blocks = jnp.where(x_bit == 0, blocks, blocks[:, :, ::-1])
    return blocks[jnp.arange(far_count) ^ z_index]


def add_low(left, right):
    return (left.astype(wide) + right.astype(wide)).astype(low)


def together(*values):
    return lax.optimization_barrier(values)


def per_device(patches, lengths, token_dest, gain, w_qkv, w_out, cotangent):
    seq_count = lax.axis_size("seq")
    dp_count = lax.axis_size("dp")
    far_count = seq_count // 2
    send = functools.partial(joint_permute, seq_count=seq_count, dp_count=dp_count)
    place = position()
    patch_rows, shard_lengths = patches[0], lengths[0, 0]
    row_count, model_width = patch_rows.shape
    half_width = model_width // HALVES
    token_count = row_count // GROUP
    direct = 4 * far_count == HEADS

    far = gather_far(place, w_out, seq_count, send)
    projected, keys_t, att_t, lse, w_kept = forward(
        patch_rows, shard_lengths, gain, w_qkv, far_count
    )
    projected, keys_t, att_t, lse, w_kept, far, cotangent = together(
        projected, keys_t, att_t, lse, w_kept, far, cotangent
    )
    if not direct:
        att_t = to_relative(place, att_t, far_count)
    level = jnp.stack(far)
    near = send(level, target=second_target)
    beyond = send(level, target=first_target)
    att_other = send(att_t, target=core_target)
    returned = lax.all_to_all(cotangent[0], "seq", split_axis=0, concat_axis=0, tiled=True)
    level_core = send(level, target=core_target)
    corner = send(near, target=first_target)
    near_core = send(near, target=core_target)
    beyond_core = send(beyond, target=core_target)
    corner_core = send(corner, target=core_target)

    merge = lambda piece: piece.reshape(-1, piece.shape[-1])
    att_parts = [merge(att_t[near_index]) for near_index in range(4)]
    own = [merge(piece) for piece in (level, near, beyond, corner)]
    away = [merge(piece) for piece in (level_core, beyond_core, near_core, corner_core)]
    branch_own = sum(dot_tn(part, piece) for part, piece in zip(att_parts, own))
    branch_away = sum(dot_tn(part, piece) for part, piece in zip(att_parts, away))
    outgoing = place_tokens(token_dest, patch_rows, branch_own, branch_away)
    merged = lax.all_to_all(
        outgoing.reshape(seq_count, token_count // seq_count, GROUP * model_width),
        "seq", split_axis=0, concat_axis=0, tiled=True,
    ).reshape(token_count, GROUP * model_width)

    bg_own, bg_away = place_rows(token_dest, returned)
    bg_other = send(bg_away, target=core_target)
    ga_t = [
        (dot_nt(first, bg_own) + dot_nt(second, bg_away)).astype(low)
        for first, second in zip(own, away)
    ]
    other_parts = [merge(att_other[index]) for index in (0, 2, 1, 3)]
    terms = [
        (dot_nn(mine, bg_own) + dot_nn(other, bg_other)).astype(low)
        for mine, other in zip(att_parts, other_parts)
    ]
    shape = (2, far_count, -1, half_width)
    arrived = send(jnp.stack(terms[2:]).reshape(shape), target=first_target)
    kept = jnp.stack(terms[:2]).reshape(shape)
    if not direct:
        blocks = jnp.stack(ga_t).reshape(4, far_count, -1, row_count)
        ga_t = [from_relative(place, blocks).reshape(model_width, row_count)]
    ga_t, kept = together(ga_t, kept)
    grads = attention_grad(shard_lengths, projected, keys_t, lse, ga_t)
    kept, grads = together(add_low(kept, arrived), grads)
    arrived = send(kept[1], target=second_target)
    grad_normed, gain_terms = normed_grad(patch_rows, w_kept, grads, seq_count, dp_count)
    level, grad_normed, gain_terms = together(
        add_low(kept[0], arrived), grad_normed, gain_terms
    )
    weight_terms = [level[0]] + [
        send(level[step], target=far_target(step)) for step in range(1, far_count)
    ]
    gain_terms, merged = together(gain_terms, merged)
    gain_arrived = lax.all_to_all(
        gain_terms, ("seq", "dp"), split_axis=0, concat_axis=0, tiled=True
    )
    patch_grad = patch_grads(patch_rows, gain, grad_normed, bg_own, bg_away)
    patch_grad, weight_terms = together(patch_grad, weight_terms)
    total = sum(term.astype(wide) for term in weight_terms).astype(low)
    held = [total, send(total, target=core_target)]
    held += [send(total, target=lambda s, d, flip=flip: (s, d ^ flip)) for flip in (2, 3)]
    norm_scale = 1.0 / math.sqrt(row_count * seq_count * dp_count)
    if direct:
        own_weight, own_gain, merged = finish(held, gain_arrived, merged, norm_scale)
        own_gain = own_gain[0]
    else:
        rows = total.shape[0]
        held = jnp.stack(held).reshape(2, 2, rows, half_width)
        held = jnp.where(place[1] == 0, held, held[::-1])
        held = jnp.where(place[0] == 0, held, held[:, ::-1])
        held = held.astype(wide).transpose(0, 2, 1, 3)
        own_weight = held.reshape(2 * rows, model_width) * norm_scale
        own_gain = jnp.sum(gain_arrived, axis=(0, 1)) * norm_scale
    return (merged[None], patch_grad[None], own_weight, own_gain)


def solution(mesh):
    placed = (
        P("dp", "seq", None),
        P("dp", "seq", None),
        P("dp", "seq"),
        P(),
        P(),
        P("seq", None),
        P("dp", "seq", None),
    )
    return jax.shard_map(
        per_device,
        mesh=mesh,
        in_specs=placed,
        out_specs=(P("dp", "seq", None), P("dp", "seq", None), P("seq", None), P("seq")),
        check_vma=False,
    )
```

```python
import functools
import math

import jax
import jax.numpy as jnp
from jax import lax
from jax.experimental import pallas as pl
from jax.experimental.pallas import tpu as pltpu
from jax.sharding import PartitionSpec as P

HEADS = 16
GROUP = 4
HALVES = 2
LANES = 128
CHUNK = 64
LOG2_E = math.log2(math.e)
VMEM_LIMIT = 32 * 1024 * 1024
PART = 256
HBM_BYTES_PER_US = 3690000

eps = 1e-06
low = jnp.bfloat16
wide = jnp.float32


def params():
    return pltpu.CompilerParams(vmem_limit_bytes=VMEM_LIMIT)


def cost(microseconds, flops):
    nominal = microseconds * HBM_BYTES_PER_US
    return pl.CostEstimate(flops=flops, bytes_accessed=nominal, transcendentals=0)


def smem():
    return pl.BlockSpec(memory_space=pltpu.SMEM)


def dot_nt(left, right):
    return lax.dot_general(left, right, (((1,), (1,)), ((), ())), preferred_element_type=wide)


def dot_tn(left, right):
    return lax.dot_general(left, right, (((0,), (0,)), ((), ())), preferred_element_type=wide)


def dot_nn(left, right):
    return jnp.dot(left, right, preferred_element_type=wide)


def score_groups(head_size, width):
    groups = []
    for head in range(width // head_size):
        start = head * head_size
        if groups and start + head_size <= groups[-1][0] + PART:
            groups[-1][1].append(head)
        else:
            groups.append((min(start // LANES * LANES, width - PART), [head]))
    return groups


def value_groups(head_size, width):
    groups = []
    for first in range(0, width, PART):
        last = min(first + PART, width)
        groups.append((first, last, range(first // head_size, -(-last // head_size))))
    return groups


def image_bias(lengths_ref, row_count):
    def image_of(index):
        number = jnp.zeros(index.shape, jnp.int32)
        end = jnp.int32(0)
        for image in range(lengths_ref.shape[0]):
            end = end + lengths_ref[image] * GROUP
            number = number + (index >= end).astype(jnp.int32)
        return number

    rows = lax.broadcasted_iota(jnp.int32, (row_count, row_count), 0)
    cols = lax.broadcasted_iota(jnp.int32, (row_count, row_count), 1)
    return jnp.where(image_of(rows) == image_of(cols), 0.0, -jnp.inf).astype(wide)


def standardise(rows):
    centred = rows - jnp.mean(rows, axis=-1, keepdims=True)
    inv_spread = lax.rsqrt(jnp.mean(centred * centred, axis=-1, keepdims=True) + eps)
    return centred * inv_spread, inv_spread


def full(shape):
    return pl.BlockSpec(shape, lambda *steps: (0,) * len(shape))


def only(head, head_size, first, value):
    lane = lax.broadcasted_iota(jnp.int32, (1, value.shape[1]), 1) + first
    keep = (lane >= head * head_size) & (lane < (head + 1) * head_size)
    return value * jnp.where(keep, 1.0, 0.0).astype(low)


def head_products(out_ref, left_ref, right_t, head_size):
    row_count, width = left_ref.shape
    for first, heads in score_groups(head_size, width):
        window = left_ref[:, first : first + PART]
        stacked = jnp.concatenate(
            [only(head, head_size, first, window) for head in heads], axis=0
        )
        product = dot_nn(stacked, right_t[first : first + PART])
        for place, head in enumerate(heads):
            out_ref[head] = product[place * row_count : (place + 1) * row_count]


def head_sums(out_t_ref, weights_ref, value_ref, head_size):
    row_count, width = value_ref.shape
    for first, last, heads in value_groups(head_size, width):
        stacked = jnp.concatenate(
            [only(head, head_size, first, value_ref[:, first:last]) for head in heads], axis=0
        )
        lanes = slice(heads[0] * row_count, (heads[-1] + 1) * row_count)
        out_t_ref[first:last] = dot_nn(weights_ref[:, lanes], stacked).astype(low).T


def position():
    s, d = lax.axis_index("seq"), lax.axis_index("dp")
    return d % 2, d // 2, s % 2, s // 2


def relative_block(block):
    core, x_bit, y_bit, z_index = position()
    x_off, y_off = (block % 2) ^ x_bit, (block // 2 % 2) ^ y_bit
    z_off = (block // 4) ^ z_index
    return jnp.where(core == 0, y_off + 2 * x_off, x_off + 2 * y_off), z_off


def project_rows(patch_rows, gain, w_qkv):
    standard, _ = standardise(patch_rows.astype(wide))
    return dot_nn((standard * gain).astype(low), w_qkv).astype(low)


def attention_kernel(
    score_scale, head_size, relative, lengths_ref, q_ref, k_ref, v_ref,
    att_t_ref, lse_ref, keys_t, turned, bias, scores, probs,
):
    row_count, half_width = q_ref.shape
    heads = half_width // head_size
    half = pl.program_id(0)

    @pl.when(half == 0)
    def _():
        bias[...] = image_bias(lengths_ref, row_count)

    keys_t[...] = k_ref[...].T
    head_products(scores, q_ref, keys_t, head_size)
    lane = lax.broadcasted_iota(jnp.int32, (CHUNK, LANES), 1)
    for row in range(0, row_count, CHUNK):
        rows = slice(row, row + CHUNK)
        lse = jnp.zeros((CHUNK, LANES), wide)
        for head in range(heads):
            scaled = scores[head, rows] * (score_scale * LOG2_E) + bias[rows]
            row_max = jnp.max(scaled, axis=-1, keepdims=True)
            weights = jnp.exp2(scaled - row_max)
            total = jnp.sum(weights, axis=-1, keepdims=True)
            lanes = slice(head * row_count, (head + 1) * row_count)
            probs[rows, lanes] = (weights * (1.0 / total)).astype(low)
            lse = jnp.where(lane == head, row_max + jnp.log2(total), lse)
        lse_ref[0, rows] = lse
    head_sums(turned, probs, v_ref, head_size)
    for head in range(heads):
        block = turned[head * head_size : (head + 1) * head_size, :]
        number = half * heads + head
        if relative:
            near, far = relative_block(number)
            att_t_ref[near, far] = block
        else:
            att_t_ref[number] = block


def attention(shard_lengths, projected, far_count):
    row_count, model_width = projected.shape[0], projected.shape[1] // 3
    half_width = model_width // HALVES
    head_size = model_width // HEADS
    heads = HEADS // HALVES
    relative = 4 * far_count == HEADS
    shape = ((4, far_count) if relative else (HEADS,)) + (head_size, row_count)
    part = lambda kind: pl.BlockSpec(
        (row_count, half_width), lambda half: (0, kind * HALVES + half)
    )
    return pl.pallas_call(
        functools.partial(attention_kernel, 1.0 / math.sqrt(head_size), head_size, relative),
        grid=(HALVES,),
        in_specs=[smem(), part(0), part(1), part(2)],
        out_specs=[
            full(shape),
            pl.BlockSpec((1, row_count, LANES), lambda half: (half, 0, 0)),
        ],
        out_shape=[
            jax.ShapeDtypeStruct(shape, low),
            jax.ShapeDtypeStruct((HALVES, row_count, LANES), wide),
        ],
        scratch_shapes=[
            pltpu.VMEM((half_width, row_count), low),
            pltpu.VMEM((half_width, row_count), low),
            pltpu.VMEM((row_count, row_count), wide),
            pltpu.VMEM((heads, row_count, row_count), wide),
            pltpu.VMEM((row_count, heads * row_count), low),
        ],
        compiler_params=params(),
        cost_estimate=cost(6, 0),
        name="attention",
    )(shard_lengths, projected, projected, projected)


def attention_grad_kernel(
    score_scale, head_size, lengths_ref, q_ref, k_ref, v_ref, lse_ref, *refs
):
    ga_refs, out_ref = refs[:-8], refs[-8]
    ga, turned, bias, scores, grad_probs, probs, grad_scores = refs[-7:]
    row_count, half_width = ga.shape
    heads = half_width // head_size
    half = pl.program_id(0)

    @pl.when(half == 0)
    def _():
        bias[...] = image_bias(lengths_ref, row_count)

    count = HEADS // len(ga_refs)
    for head in range(heads):
        number = half * heads + head
        rows = slice(head * head_size, (head + 1) * head_size)
        if len(ga_refs) == 1:
            turned[2, rows] = ga_refs[0][number]
            continue
        near, far = relative_block(number)
        block = ga_refs[0][far]
        for index in range(1, len(ga_refs)):
            block = jnp.where(near == index, ga_refs[index][far], block)
        turned[2, rows] = block
    ga[...] = turned[2].T
    turned[0] = k_ref[...].T
    turned[1] = v_ref[...].T
    head_products(scores, q_ref, turned.at[0], head_size)
    head_products(grad_probs, ga, turned.at[1], head_size)
    for row in range(0, row_count, CHUNK):
        rows = slice(row, row + CHUNK)
        lse = lse_ref[0, rows]
        for head in range(heads):
            scaled = scores[head, rows] * (score_scale * LOG2_E) + bias[rows]
            chance = jnp.exp2(scaled - lse[:, head : head + 1])
            incoming = grad_probs[head, rows]
            inner = jnp.sum(incoming * chance, axis=-1, keepdims=True)
            lanes = slice(head * row_count, (head + 1) * row_count)
            probs[rows, lanes] = chance.astype(low)
            grad_scores[rows, lanes] = (chance * (incoming - inner) * score_scale).astype(low)
    head_sums(out_ref.at[0, 0], grad_scores, k_ref, head_size)
    turned[0] = q_ref[...].T
    for head in range(heads):
        rows = slice(head * head_size, (head + 1) * head_size)
        lanes = slice(head * row_count, (head + 1) * row_count)
        out_ref[0, 1, rows] = dot_nn(turned[0, rows], grad_scores[:, lanes]).astype(low)
        out_ref[0, 2, rows] = dot_nn(turned[2, rows], probs[:, lanes]).astype(low)


def attention_grad(shard_lengths, projected, lse, grads_att):
    row_count, model_width = projected.shape[0], projected.shape[1] // 3
    half_width = model_width // HALVES
    head_size = model_width // HEADS
    heads = HEADS // HALVES
    part = lambda kind: pl.BlockSpec(
        (row_count, half_width), lambda half: (0, kind * HALVES + half)
    )
    shape = (HEADS // len(grads_att), head_size, row_count)
    return pl.pallas_call(
        functools.partial(attention_grad_kernel, 1.0 / math.sqrt(head_size), head_size),
        grid=(HALVES,),
        in_specs=[smem(), part(0), part(1), part(2)]
        + [pl.BlockSpec((1, row_count, LANES), lambda half: (half, 0, 0))]
        + [full(shape)] * len(grads_att),
        out_specs=pl.BlockSpec((1, 3, half_width, row_count), lambda half: (half, 0, 0, 0)),
        out_shape=jax.ShapeDtypeStruct((HALVES, 3, half_width, row_count), low),
        scratch_shapes=[
            pltpu.VMEM((row_count, half_width), low),
            pltpu.VMEM((3, half_width, row_count), low),
            pltpu.VMEM((row_count, row_count), wide),
            pltpu.VMEM((heads, row_count, row_count), wide),
            pltpu.VMEM((heads, row_count, row_count), wide),
            pltpu.VMEM((row_count, heads * row_count), low),
            pltpu.VMEM((row_count, heads * row_count), low),
        ],
        compiler_params=params(),
        cost_estimate=cost(9, 0),
        name="attention_grad",
    )(
        shard_lengths, projected, projected, projected, lse,
        *[grad.reshape(shape) for grad in grads_att],
    )


def normed_grad_kernel(copies_each, x_ref, w_ref, grad_ref, out_ref, gain_out_ref):
    row_count, model_width = x_ref.shape
    half_width = model_width // HALVES
    step = pl.program_id(0)
    cols = pl.ds(pl.multiple_of(step * PART, PART), PART)
    parts = [(kind, half) for half in range(HALVES) for kind in range(3)]
    weights = jnp.concatenate(
        [
            w_ref[:, (kind * HALVES + half) * half_width : (kind * HALVES + half + 1) * half_width]
            for kind, half in parts
        ],
        axis=1,
    )
    out_ref[:, cols] = dot_nn(weights, grad_ref[...].reshape(3 * model_width, row_count)).T

    @pl.when(step == pl.num_programs(0) - 1)
    def _():
        total = None
        for row in range(0, row_count, LANES):
            rows = slice(row, row + LANES)
            standard, _ = standardise(x_ref[rows].astype(wide))
            term = jnp.sum(out_ref[rows] * standard, axis=0, keepdims=True)
            total = term if total is None else total + term
        share = gain_out_ref.shape[2]
        for number in range(model_width // share):
            term = total[:, number * share : (number + 1) * share]
            for copy in range(copies_each):
                gain_out_ref[number * copies_each + copy] = term


def normed_grad(patch_rows, w_qkv, grads, seq_count, dp_count):
    row_count, model_width = patch_rows.shape
    share = model_width // seq_count
    spread = (seq_count * dp_count, 1, share)
    return pl.pallas_call(
        functools.partial(normed_grad_kernel, dp_count),
        grid=(model_width // PART,),
        in_specs=[
            full(patch_rows.shape),
            pl.BlockSpec((PART, 3 * model_width), lambda step: (step, 0)),
            full(grads.shape),
        ],
        out_specs=[full(patch_rows.shape), full(spread)],
        out_shape=[
            jax.ShapeDtypeStruct((row_count, model_width), wide),
            jax.ShapeDtypeStruct(spread, wide),
        ],
        compiler_params=params(),
        cost_estimate=cost(7, 0),
        name="normed_grad",
    )(patch_rows, w_qkv, grads)


def patch_grad_kernel(
    x_ref, gain_ref, grad_ref, bg_own_ref, bg_away_ref, merged_ref, patch_ref, merged_out_ref
):
    row_count, model_width = x_ref.shape
    half_width = model_width // HALVES
    core = position()[0]
    merged_out_ref[...] = merged_ref[...]
    for row in range(0, row_count, LANES):
        rows = slice(row, row + LANES)
        standard, inv_spread = standardise(x_ref[rows].astype(wide))
        grad = grad_ref[rows] * gain_ref[...]
        branch = inv_spread * (
            grad
            - jnp.mean(grad, axis=-1, keepdims=True)
            - standard * jnp.mean(grad * standard, axis=-1, keepdims=True)
        )
        for half in range(HALVES):
            cols = slice(half * half_width, (half + 1) * half_width)
            incoming = jnp.where(core == half, bg_own_ref[rows], bg_away_ref[rows])
            patch_ref[rows, cols] = (incoming.astype(wide) + branch[:, cols]).astype(low)


def patch_grads(patch_rows, gain, grad_normed, bg_own, bg_away, merged):
    args = (patch_rows, gain, grad_normed, bg_own, bg_away, merged)
    return pl.pallas_call(
        patch_grad_kernel,
        grid=(1,),
        in_specs=[full(arg.shape) for arg in args],
        out_specs=[full(patch_rows.shape), full(merged.shape)],
        out_shape=[
            jax.ShapeDtypeStruct(patch_rows.shape, low),
            jax.ShapeDtypeStruct(merged.shape, low),
        ],
        compiler_params=params(),
        cost_estimate=cost(3, 0),
        name="patch_grads",
    )(*args)


def placing_matrix(dest_ref, row_count):
    token_count = row_count // GROUP
    peer_count = token_count // lax.axis_size("seq")
    token_bits = token_count.bit_length() - 1
    dest = dest_ref[...]
    shard = lax.shift_right_logical(dest, jnp.full_like(dest, token_bits))
    slot = shard * peer_count + (dest & (peer_count - 1))
    square = (token_count, token_count)
    chosen = (lax.broadcasted_iota(jnp.int32, square, 0) == slot).astype(low)
    shape = (token_count, row_count)
    token = lax.broadcasted_iota(jnp.int32, shape, 0) * GROUP
    row = lax.broadcasted_iota(jnp.int32, shape, 1)
    parts = []
    for member in range(GROUP):
        spread = (row == token + member).astype(low)
        parts.append(dot_nn(chosen, spread).astype(low))
    return jnp.concatenate(parts, axis=0)


def place_kernel(dest_ref, returned_ref, own_ref, away_ref, stacked):
    token_count = returned_ref.shape[0]
    row_count, model_width = stacked.shape
    half_width = model_width // HALVES
    for member in range(GROUP):
        stacked[member * token_count : (member + 1) * token_count] = returned_ref[
            :, member * model_width : (member + 1) * model_width
        ]
    placing = placing_matrix(dest_ref, row_count)
    core = position()[0]
    for side, out_ref in enumerate((own_ref, away_ref)):
        cols = pl.ds(pl.multiple_of((core ^ side) * half_width, LANES), half_width)
        out_ref[...] = dot_tn(placing, stacked[:, cols]).astype(low)


def place_rows(token_dest, returned):
    token_count, merged_width = returned.shape
    row_count, model_width = token_count * GROUP, merged_width // GROUP
    half_width = model_width // HALVES
    return pl.pallas_call(
        place_kernel,
        grid=(1,),
        in_specs=[full(token_dest.shape), full(returned.shape)],
        out_specs=[full((row_count, half_width))] * 2,
        out_shape=[jax.ShapeDtypeStruct((row_count, half_width), low)] * 2,
        scratch_shapes=[pltpu.VMEM((row_count, model_width), low)],
        compiler_params=params(),
        cost_estimate=cost(2, 0),
        name="place_rows",
    )(token_dest, returned)


def token_kernel(dest_ref, x_ref, own_ref, away_ref, out_ref):
    row_count, model_width = x_ref.shape
    half_width = model_width // HALVES
    token_count = row_count // GROUP
    placing = placing_matrix(dest_ref, row_count)
    core = position()[0]
    for side, branch_ref in enumerate((own_ref, away_ref)):
        first = pl.multiple_of((core ^ side) * half_width, LANES)
        block = x_ref[:, pl.ds(first, half_width)].astype(wide) + branch_ref[...]
        tokens = dot_nn(placing, block.astype(low)).astype(low)
        for member in range(GROUP):
            place = pl.multiple_of(member * model_width + first, LANES)
            rows = slice(member * token_count, (member + 1) * token_count)
            out_ref[:, pl.ds(place, half_width)] = tokens[rows]


def place_tokens(token_dest, patch_rows, own, away):
    row_count, model_width = patch_rows.shape
    args = (token_dest, patch_rows, own, away)
    shape = (row_count // GROUP, GROUP * model_width)
    return pl.pallas_call(
        token_kernel,
        grid=(1,),
        in_specs=[full(arg.shape) for arg in args],
        out_specs=full(shape),
        out_shape=jax.ShapeDtypeStruct(shape, low),
        compiler_params=params(),
        cost_estimate=cost(2, 0),
        name="place_tokens",
    )(*args)


def finish_kernel(
    norm_scale, own_ref, core_ref, x_ref, both_ref, gain_ref, out_ref, gain_out_ref
):
    core, x_bit, _, _ = position()
    rows, cols = own_ref.shape
    for x_off, pair in enumerate(((own_ref, core_ref), (x_ref, both_ref))):
        for core_off, piece in enumerate(pair):
            to_rows = pl.ds(pl.multiple_of((x_bit ^ x_off) * rows, rows), rows)
            to_cols = pl.ds(pl.multiple_of((core ^ core_off) * cols, LANES), cols)
            out_ref[to_rows, to_cols] = piece[...].astype(wide) * norm_scale
    gain_out_ref[...] = jnp.sum(gain_ref[...], axis=0) * norm_scale


def finish(held, gain_terms, norm_scale):
    rows, cols = held[0].shape
    share = gain_terms.shape[2]
    return pl.pallas_call(
        functools.partial(finish_kernel, norm_scale),
        grid=(1,),
        in_specs=[full(piece.shape) for piece in held] + [full(gain_terms.shape)],
        out_specs=[full((2 * rows, 2 * cols)), full((1, share))],
        out_shape=[
            jax.ShapeDtypeStruct((2 * rows, 2 * cols), wide),
            jax.ShapeDtypeStruct((1, share), wide),
        ],
        compiler_params=params(),
        cost_estimate=cost(1, 0),
        name="finish",
    )(*held, gain_terms)


def joint_permute(value, seq_count, dp_count, target):
    pairs = []
    for s in range(seq_count):
        for d in range(dp_count):
            to_s, to_d = target(s, d)
            pairs.append((s * dp_count + d, to_s * dp_count + to_d))
    return lax.ppermute(value, ("seq", "dp"), pairs)


def core_target(s, d):
    return s, d ^ 1


def first_target(s, d):
    return (s, d ^ 2) if d % 2 == 0 else (s ^ 1, d)


def second_target(s, d):
    return (s ^ 1, d) if d % 2 == 0 else (s, d ^ 2)


def far_target(step):
    return lambda s, d: (s ^ (2 * step), d)


def gather_far(place, w_out, seq_count, send):
    share, model_width = w_out.shape
    rows, cols = share // 2, model_width // 2
    core, x_bit = place[0], place[1]
    own = lax.dynamic_slice(w_out, (x_bit * rows, core * cols), (rows, cols))
    return [own] + [send(own, target=far_target(step)) for step in range(1, seq_count // 2)]


def to_relative(place, blocks, far_count):
    core, x_bit, y_bit, z_index = place
    width = blocks.shape[-1]
    blocks = blocks.reshape(far_count, 2, 2, -1, width)[jnp.arange(far_count) ^ z_index]
    blocks = jnp.where(y_bit == 0, blocks, blocks[:, ::-1])
    blocks = jnp.where(x_bit == 0, blocks, blocks[:, :, ::-1])
    x_first, y_first = blocks.transpose(2, 1, 0, 3, 4), blocks.transpose(1, 2, 0, 3, 4)
    return jnp.where(core == 0, x_first, y_first).reshape((4, far_count) + x_first.shape[3:])


def from_relative(place, blocks):
    core, x_bit, y_bit, z_index = place
    _, far_count, rows, width = blocks.shape
    blocks = blocks.reshape(2, 2, far_count, rows, width)
    y_first = blocks.transpose(2, 0, 1, 3, 4)
    blocks = jnp.where(core == 0, blocks.transpose(2, 1, 0, 3, 4), y_first)
    blocks = jnp.where(y_bit == 0, blocks, blocks[:, ::-1])
    blocks = jnp.where(x_bit == 0, blocks, blocks[:, :, ::-1])
    return blocks[jnp.arange(far_count) ^ z_index]


def add_low(left, right):
    return (left.astype(wide) + right.astype(wide)).astype(low)


def together(*values):
    return lax.optimization_barrier(values)


def per_device(patches, lengths, token_dest, gain, w_qkv, w_out, cotangent):
    seq_count = lax.axis_size("seq")
    dp_count = lax.axis_size("dp")
    far_count = seq_count // 2
    send = functools.partial(joint_permute, seq_count=seq_count, dp_count=dp_count)
    place = position()
    patch_rows, shard_lengths = patches[0], lengths[0, 0]
    row_count, model_width = patch_rows.shape
    half_width = model_width // HALVES
    token_count = row_count // GROUP
    direct = 4 * far_count == HEADS

    far = gather_far(place, w_out, seq_count, send)
    projected = project_rows(patch_rows, gain, w_qkv)
    projected, cotangent = together(projected, cotangent)
    returned = lax.all_to_all(cotangent[0], "seq", split_axis=0, concat_axis=0, tiled=True)
    att_t, lse = attention(shard_lengths, projected, far_count)
    att_t, lse, far = together(att_t, lse, far)
    if not direct:
        att_t = to_relative(place, att_t, far_count)
    level = jnp.stack(far)
    near = send(level, target=second_target)
    beyond = send(level, target=first_target)
    att_other = send(att_t, target=core_target)
    returned, near = together(returned, near)
    level_core = send(level, target=core_target)
    corner = send(near, target=first_target)
    near_core = send(near, target=core_target)
    beyond_core = send(beyond, target=core_target)
    corner_core = send(corner, target=core_target)

    merge = lambda piece: piece.reshape(-1, piece.shape[-1])
    att_parts = [merge(att_t[near_index]) for near_index in range(4)]
    own = [merge(piece) for piece in (level, near, beyond, corner)]
    away = [merge(piece) for piece in (level_core, beyond_core, near_core, corner_core)]
    branch_own = sum(dot_tn(part, piece) for part, piece in zip(att_parts, own))
    branch_away = sum(dot_tn(part, piece) for part, piece in zip(att_parts, away))
    outgoing = place_tokens(token_dest, patch_rows, branch_own, branch_away)
    merged = lax.all_to_all(
        outgoing.reshape(seq_count, token_count // seq_count, GROUP * model_width),
        "seq", split_axis=0, concat_axis=0, tiled=True,
    ).reshape(token_count, GROUP * model_width)

    bg_own, bg_away = place_rows(token_dest, returned)
    bg_other = send(bg_away, target=core_target)
    ga_t = [
        (dot_nt(first, bg_own) + dot_nt(second, bg_away)).astype(low)
        for first, second in zip(own, away)
    ]
    other_parts = [merge(att_other[index]) for index in (0, 2, 1, 3)]
    terms = [
        (dot_nn(mine, bg_own) + dot_nn(other, bg_other)).astype(low)
        for mine, other in zip(att_parts, other_parts)
    ]
    shape = (2, far_count, -1, half_width)
    arrived = send(jnp.stack(terms[2:]).reshape(shape), target=first_target)
    kept = jnp.stack(terms[:2]).reshape(shape)
    if not direct:
        blocks = jnp.stack(ga_t).reshape(4, far_count, -1, row_count)
        ga_t = [from_relative(place, blocks).reshape(model_width, row_count)]
    ga_t, kept, _ = together(ga_t, add_low(kept, arrived), outgoing)
    arrived = send(kept[1], target=second_target)
    grads = attention_grad(shard_lengths, projected, lse, ga_t)
    level, grads = together(add_low(kept[0], arrived), grads)
    weight_terms = [level[0]] + [
        send(level[step], target=far_target(step)) for step in range(1, far_count)
    ]
    grad_normed, gain_terms = normed_grad(patch_rows, w_qkv, grads, seq_count, dp_count)
    gain_terms, merged, grad_normed = together(gain_terms, merged, grad_normed)
    gain_arrived = lax.all_to_all(
        gain_terms, ("seq", "dp"), split_axis=0, concat_axis=0, tiled=True
    )
    patch_grad, merged = patch_grads(patch_rows, gain, grad_normed, bg_own, bg_away, merged)
    patch_grad, merged, weight_terms = together(patch_grad, merged, weight_terms)
    total = sum(term.astype(wide) for term in weight_terms).astype(low)
    held = [total, send(total, target=core_target)]
    held += [send(total, target=lambda s, d, flip=flip: (s, d ^ flip)) for flip in (2, 3)]
    norm_scale = 1.0 / math.sqrt(row_count * seq_count * dp_count)
    if direct:
        own_weight, own_gain = finish(held, gain_arrived, norm_scale)
        own_gain = own_gain[0]
    else:
        rows = total.shape[0]
        held = jnp.stack(held).reshape(2, 2, rows, half_width)
        held = jnp.where(place[1] == 0, held, held[::-1])
        held = jnp.where(place[0] == 0, held, held[:, ::-1])
        held = held.astype(wide).transpose(0, 2, 1, 3)
        own_weight = held.reshape(2 * rows, model_width) * norm_scale
        own_gain = jnp.sum(gain_arrived, axis=(0, 1)) * norm_scale
    return (merged[None], patch_grad[None], own_weight, own_gain)


def solution(mesh):
    placed = (
        P("dp", "seq", None),
        P("dp", "seq", None),
        P("dp", "seq"),
        P(),
        P(),
        P("seq", None),
        P("dp", "seq", None),
    )
    return jax.shard_map(
        per_device,
        mesh=mesh,
        in_specs=placed,
        out_specs=(P("dp", "seq", None), P("dp", "seq", None), P("seq", None), P("seq")),
        check_vma=False,
    )
```

```python
import functools
import math

import jax
import jax.numpy as jnp
from jax import lax
from jax.experimental import pallas as pl
from jax.experimental.pallas import tpu as pltpu
from jax.sharding import PartitionSpec as P

HEADS = 16
GROUP = 4
HALVES = 2
LANES = 128
CHUNK = 64
LOG2_E = math.log2(math.e)
VMEM_LIMIT = 32 * 1024 * 1024
PART = 256
HBM_BYTES_PER_US = 3690000

eps = 1e-06
low = jnp.bfloat16
wide = jnp.float32


def params(limit=VMEM_LIMIT):
    return pltpu.CompilerParams(vmem_limit_bytes=limit)


def cost(microseconds, flops):
    nominal = microseconds * HBM_BYTES_PER_US
    return pl.CostEstimate(flops=flops, bytes_accessed=nominal, transcendentals=0)


def smem():
    return pl.BlockSpec(memory_space=pltpu.SMEM)


def dot_nt(left, right):
    return lax.dot_general(left, right, (((1,), (1,)), ((), ())), preferred_element_type=wide)


def dot_tn(left, right):
    return lax.dot_general(left, right, (((0,), (0,)), ((), ())), preferred_element_type=wide)


def dot_nn(left, right):
    return jnp.dot(left, right, preferred_element_type=wide)


def score_groups(head_size, width):
    groups = []
    for head in range(width // head_size):
        start = head * head_size
        if groups and start + head_size <= groups[-1][0] + PART:
            groups[-1][1].append(head)
        else:
            groups.append((min(start // LANES * LANES, width - PART), [head]))
    return groups


def value_groups(head_size, width):
    groups = []
    for first in range(0, width, PART):
        last = min(first + PART, width)
        groups.append((first, last, range(first // head_size, -(-last // head_size))))
    return groups


def image_bias(lengths_ref, row_count):
    def image_of(index):
        number = jnp.zeros(index.shape, jnp.int32)
        end = jnp.int32(0)
        for image in range(lengths_ref.shape[0]):
            end = end + lengths_ref[image] * GROUP
            number = number + (index >= end).astype(jnp.int32)
        return number

    rows = lax.broadcasted_iota(jnp.int32, (row_count, row_count), 0)
    cols = lax.broadcasted_iota(jnp.int32, (row_count, row_count), 1)
    return jnp.where(image_of(rows) == image_of(cols), 0.0, -jnp.inf).astype(wide)


def standardise(rows):
    centred = rows - jnp.mean(rows, axis=-1, keepdims=True)
    inv_spread = lax.rsqrt(jnp.mean(centred * centred, axis=-1, keepdims=True) + eps)
    return centred * inv_spread, inv_spread


def full(shape):
    return pl.BlockSpec(shape, lambda *steps: (0,) * len(shape))


def only(head, head_size, first, value):
    lane = lax.broadcasted_iota(jnp.int32, (1, value.shape[1]), 1) + first
    keep = (lane >= head * head_size) & (lane < (head + 1) * head_size)
    return value * jnp.where(keep, 1.0, 0.0).astype(low)


def head_products(out_ref, left_ref, right_t, head_size):
    row_count, width = left_ref.shape
    for first, heads in score_groups(head_size, width):
        window = left_ref[:, first : first + PART]
        stacked = jnp.concatenate(
            [only(head, head_size, first, window) for head in heads], axis=0
        )
        product = dot_nn(stacked, right_t[first : first + PART])
        for place, head in enumerate(heads):
            out_ref[head] = product[place * row_count : (place + 1) * row_count]


def head_sums(out_t_ref, weights_ref, value_ref, head_size):
    row_count, width = value_ref.shape
    for first, last, heads in value_groups(head_size, width):
        stacked = jnp.concatenate(
            [only(head, head_size, first, value_ref[:, first:last]) for head in heads], axis=0
        )
        lanes = slice(heads[0] * row_count, (heads[-1] + 1) * row_count)
        out_t_ref[first:last] = dot_nn(weights_ref[:, lanes], stacked).astype(low).T


def position():
    s, d = lax.axis_index("seq"), lax.axis_index("dp")
    return d % 2, d // 2, s % 2, s // 2


def relative_block(block):
    core, x_bit, y_bit, z_index = position()
    x_off, y_off = (block % 2) ^ x_bit, (block // 2 % 2) ^ y_bit
    z_off = (block // 4) ^ z_index
    return jnp.where(core == 0, y_off + 2 * x_off, x_off + 2 * y_off), z_off


def project_rows(patch_rows, gain, w_qkv):
    standard, _ = standardise(patch_rows.astype(wide))
    return dot_nn((standard * gain).astype(low), w_qkv).astype(low)


def attention_kernel(
    score_scale, head_size, relative, lengths_ref, q_ref, k_ref, v_ref,
    att_t_ref, lse_ref, keys_t, turned, bias, scores, probs,
):
    row_count, half_width = q_ref.shape
    heads = half_width // head_size
    half = pl.program_id(0)

    @pl.when(half == 0)
    def _():
        bias[...] = image_bias(lengths_ref, row_count)

    keys_t[...] = k_ref[...].T
    head_products(scores, q_ref, keys_t, head_size)
    lane = lax.broadcasted_iota(jnp.int32, (CHUNK, LANES), 1)
    for row in range(0, row_count, CHUNK):
        rows = slice(row, row + CHUNK)
        lse = jnp.zeros((CHUNK, LANES), wide)
        for head in range(heads):
            scaled = scores[head, rows] * (score_scale * LOG2_E) + bias[rows]
            row_max = jnp.max(scaled, axis=-1, keepdims=True)
            weights = jnp.exp2(scaled - row_max)
            total = jnp.sum(weights, axis=-1, keepdims=True)
            lanes = slice(head * row_count, (head + 1) * row_count)
            probs[rows, lanes] = (weights * (1.0 / total)).astype(low)
            lse = jnp.where(lane == head, row_max + jnp.log2(total), lse)
        lse_ref[0, rows] = lse
    head_sums(turned, probs, v_ref, head_size)
    for head in range(heads):
        block = turned[head * head_size : (head + 1) * head_size, :]
        number = half * heads + head
        if relative:
            near, far = relative_block(number)
            att_t_ref[near, far] = block
        else:
            att_t_ref[number] = block


def attention(shard_lengths, projected, far_count):
    row_count, model_width = projected.shape[0], projected.shape[1] // 3
    half_width = model_width // HALVES
    head_size = model_width // HEADS
    heads = HEADS // HALVES
    relative = 4 * far_count == HEADS
    shape = ((4, far_count) if relative else (HEADS,)) + (head_size, row_count)
    part = lambda kind: pl.BlockSpec(
        (row_count, half_width), lambda half: (0, kind * HALVES + half)
    )
    return pl.pallas_call(
        functools.partial(attention_kernel, 1.0 / math.sqrt(head_size), head_size, relative),
        grid=(HALVES,),
        in_specs=[smem(), part(0), part(1), part(2)],
        out_specs=[
            full(shape),
            pl.BlockSpec((1, row_count, LANES), lambda half: (half, 0, 0)),
        ],
        out_shape=[
            jax.ShapeDtypeStruct(shape, low),
            jax.ShapeDtypeStruct((HALVES, row_count, LANES), wide),
        ],
        scratch_shapes=[
            pltpu.VMEM((half_width, row_count), low),
            pltpu.VMEM((half_width, row_count), low),
            pltpu.VMEM((row_count, row_count), wide),
            pltpu.VMEM((heads, row_count, row_count), wide),
            pltpu.VMEM((row_count, heads * row_count), low),
        ],
        compiler_params=params(),
        cost_estimate=cost(6, 0),
        name="attention",
    )(shard_lengths, projected, projected, projected)


def attention_grad_kernel(
    score_scale, head_size, relative, lengths_ref, q_ref, k_ref, v_ref, lse_ref, ga_ref,
    out_ref, ga, turned, bias, scores, grad_probs, probs, grad_scores,
):
    row_count, half_width = ga.shape
    heads = half_width // head_size
    half = pl.program_id(0)

    @pl.when(half == 0)
    def _():
        bias[...] = image_bias(lengths_ref, row_count)

    for head in range(heads):
        number = half * heads + head
        if relative:
            near, far = relative_block(number)
            number = near * (HEADS // 4) + far
        turned[2, head * head_size : (head + 1) * head_size] = ga_ref[number]
    ga[...] = turned[2].T
    turned[0] = k_ref[...].T
    turned[1] = v_ref[...].T
    head_products(scores, q_ref, turned.at[0], head_size)
    head_products(grad_probs, ga, turned.at[1], head_size)
    for row in range(0, row_count, CHUNK):
        rows = slice(row, row + CHUNK)
        lse = lse_ref[0, rows]
        for head in range(heads):
            scaled = scores[head, rows] * (score_scale * LOG2_E) + bias[rows]
            chance = jnp.exp2(scaled - lse[:, head : head + 1])
            incoming = grad_probs[head, rows]
            inner = jnp.sum(incoming * chance, axis=-1, keepdims=True)
            lanes = slice(head * row_count, (head + 1) * row_count)
            probs[rows, lanes] = chance.astype(low)
            grad_scores[rows, lanes] = (chance * (incoming - inner) * score_scale).astype(low)
    head_sums(out_ref.at[0, 0], grad_scores, k_ref, head_size)
    turned[0] = q_ref[...].T
    for head in range(heads):
        rows = slice(head * head_size, (head + 1) * head_size)
        lanes = slice(head * row_count, (head + 1) * row_count)
        out_ref[0, 1, rows] = dot_nn(turned[0, rows], grad_scores[:, lanes]).astype(low)
        out_ref[0, 2, rows] = dot_nn(turned[2, rows], probs[:, lanes]).astype(low)


def attention_grad(shard_lengths, projected, lse, ga_t, relative):
    row_count, model_width = projected.shape[0], projected.shape[1] // 3
    half_width = model_width // HALVES
    head_size = model_width // HEADS
    heads = HEADS // HALVES
    part = lambda kind: pl.BlockSpec(
        (row_count, half_width), lambda half: (0, kind * HALVES + half)
    )
    shape = (HEADS, head_size, row_count)
    return pl.pallas_call(
        functools.partial(
            attention_grad_kernel, 1.0 / math.sqrt(head_size), head_size, relative
        ),
        grid=(HALVES,),
        in_specs=[smem(), part(0), part(1), part(2)]
        + [pl.BlockSpec((1, row_count, LANES), lambda half: (half, 0, 0))]
        + [full(shape)],
        out_specs=pl.BlockSpec((1, 3, half_width, row_count), lambda half: (half, 0, 0, 0)),
        out_shape=jax.ShapeDtypeStruct((HALVES, 3, half_width, row_count), low),
        scratch_shapes=[
            pltpu.VMEM((row_count, half_width), low),
            pltpu.VMEM((3, half_width, row_count), low),
            pltpu.VMEM((row_count, row_count), wide),
            pltpu.VMEM((heads, row_count, row_count), wide),
            pltpu.VMEM((heads, row_count, row_count), wide),
            pltpu.VMEM((row_count, heads * row_count), low),
            pltpu.VMEM((row_count, heads * row_count), low),
        ],
        compiler_params=params(),
        cost_estimate=cost(9, 0),
        name="attention_grad",
    )(shard_lengths, projected, projected, projected, lse, ga_t.reshape(shape))


def normed_grad_kernel(copies_each, x_ref, w_ref, grad_ref, out_ref, gain_out_ref):
    row_count, model_width = x_ref.shape
    half_width = model_width // HALVES
    step = pl.program_id(0)
    cols = pl.ds(pl.multiple_of(step * PART, PART), PART)
    parts = [(kind, half) for half in range(HALVES) for kind in range(3)]
    weights = jnp.concatenate(
        [
            w_ref[:, (kind * HALVES + half) * half_width : (kind * HALVES + half + 1) * half_width]
            for kind, half in parts
        ],
        axis=1,
    )
    out_ref[:, cols] = dot_nn(weights, grad_ref[...].reshape(3 * model_width, row_count)).T

    @pl.when(step == pl.num_programs(0) - 1)
    def _():
        total = None
        for row in range(0, row_count, LANES):
            rows = slice(row, row + LANES)
            standard, _ = standardise(x_ref[rows].astype(wide))
            term = jnp.sum(out_ref[rows] * standard, axis=0, keepdims=True)
            total = term if total is None else total + term
        share = gain_out_ref.shape[2]
        for number in range(model_width // share):
            term = total[:, number * share : (number + 1) * share]
            for copy in range(copies_each):
                gain_out_ref[number * copies_each + copy] = term


def normed_grad(patch_rows, w_qkv, grads, seq_count, dp_count):
    row_count, model_width = patch_rows.shape
    share = model_width // seq_count
    spread = (seq_count * dp_count, 1, share)
    return pl.pallas_call(
        functools.partial(normed_grad_kernel, dp_count),
        grid=(model_width // PART,),
        in_specs=[
            full(patch_rows.shape),
            pl.BlockSpec((PART, 3 * model_width), lambda step: (step, 0)),
            full(grads.shape),
        ],
        out_specs=[full(patch_rows.shape), full(spread)],
        out_shape=[
            jax.ShapeDtypeStruct((row_count, model_width), wide),
            jax.ShapeDtypeStruct(spread, wide),
        ],
        compiler_params=params(2 * VMEM_LIMIT - VMEM_LIMIT // 8),
        cost_estimate=cost(7, 0),
        name="normed_grad",
    )(patch_rows, w_qkv, grads)


def patch_grad_kernel(
    x_ref, gain_ref, grad_ref, bg_own_ref, bg_away_ref, merged_ref, patch_ref, merged_out_ref
):
    row_count, model_width = x_ref.shape
    half_width = model_width // HALVES
    core = position()[0]
    merged_out_ref[...] = merged_ref[...]
    for row in range(0, row_count, LANES):
        rows = slice(row, row + LANES)
        standard, inv_spread = standardise(x_ref[rows].astype(wide))
        grad = grad_ref[rows] * gain_ref[...]
        branch = inv_spread * (
            grad
            - jnp.mean(grad, axis=-1, keepdims=True)
            - standard * jnp.mean(grad * standard, axis=-1, keepdims=True)
        )
        for half in range(HALVES):
            cols = slice(half * half_width, (half + 1) * half_width)
            incoming = jnp.where(core == half, bg_own_ref[rows], bg_away_ref[rows])
            patch_ref[rows, cols] = (incoming.astype(wide) + branch[:, cols]).astype(low)


def patch_grads(patch_rows, gain, grad_normed, bg_own, bg_away, merged):
    args = (patch_rows, gain, grad_normed, bg_own, bg_away, merged)
    return pl.pallas_call(
        patch_grad_kernel,
        grid=(1,),
        in_specs=[full(arg.shape) for arg in args],
        out_specs=[full(patch_rows.shape), full(merged.shape)],
        out_shape=[
            jax.ShapeDtypeStruct(patch_rows.shape, low),
            jax.ShapeDtypeStruct(merged.shape, low),
        ],
        compiler_params=params(),
        cost_estimate=cost(3, 0),
        name="patch_grads",
    )(*args)


def placing_matrix(dest_ref, row_count):
    token_count = row_count // GROUP
    peer_count = token_count // lax.axis_size("seq")
    token_bits = token_count.bit_length() - 1
    dest = dest_ref[...]
    shard = lax.shift_right_logical(dest, jnp.full_like(dest, token_bits))
    slot = shard * peer_count + (dest & (peer_count - 1))
    square = (token_count, token_count)
    chosen = (lax.broadcasted_iota(jnp.int32, square, 0) == slot).astype(low)
    shape = (token_count, row_count)
    token = lax.broadcasted_iota(jnp.int32, shape, 0) * GROUP
    row = lax.broadcasted_iota(jnp.int32, shape, 1)
    parts = []
    for member in range(GROUP):
        spread = (row == token + member).astype(low)
        parts.append(dot_nn(chosen, spread).astype(low))
    return jnp.concatenate(parts, axis=0)


def place_kernel(dest_ref, returned_ref, own_ref, away_ref, stacked):
    token_count = returned_ref.shape[0]
    row_count, model_width = stacked.shape
    half_width = model_width // HALVES
    for member in range(GROUP):
        stacked[member * token_count : (member + 1) * token_count] = returned_ref[
            :, member * model_width : (member + 1) * model_width
        ]
    placing = placing_matrix(dest_ref, row_count)
    core = position()[0]
    for side, out_ref in enumerate((own_ref, away_ref)):
        cols = pl.ds(pl.multiple_of((core ^ side) * half_width, LANES), half_width)
        out_ref[...] = dot_tn(placing, stacked[:, cols]).astype(low)


def place_rows(token_dest, returned):
    token_count, merged_width = returned.shape
    row_count, model_width = token_count * GROUP, merged_width // GROUP
    half_width = model_width // HALVES
    return pl.pallas_call(
        place_kernel,
        grid=(1,),
        in_specs=[full(token_dest.shape), full(returned.shape)],
        out_specs=[full((row_count, half_width))] * 2,
        out_shape=[jax.ShapeDtypeStruct((row_count, half_width), low)] * 2,
        scratch_shapes=[pltpu.VMEM((row_count, model_width), low)],
        compiler_params=params(),
        cost_estimate=cost(2, 0),
        name="place_rows",
    )(token_dest, returned)


def project_kernel(dest_ref, x_ref, att_t_ref, bg_own_ref, bg_away_ref, *refs):
    own, away, (out_ref, ga_t_ref, attended) = refs[:4], refs[4:8], refs[8:]
    row_count, model_width = x_ref.shape
    half_width = model_width // HALVES
    token_count = row_count // GROUP
    placing = placing_matrix(dest_ref, row_count)
    core = position()[0]
    attended[...] = att_t_ref[...].T
    grad = None
    for side, (pieces, bg_ref) in enumerate(((own, bg_own_ref), (away, bg_away_ref))):
        matrix = jnp.concatenate([piece[...] for piece in pieces], axis=0)
        first = pl.multiple_of((core ^ side) * half_width, LANES)
        branch = dot_nn(attended[...], matrix)
        block = x_ref[:, pl.ds(first, half_width)].astype(wide) + branch
        tokens = dot_nn(placing, block.astype(low)).astype(low)
        for member in range(GROUP):
            place = pl.multiple_of(member * model_width + first, LANES)
            rows = slice(member * token_count, (member + 1) * token_count)
            out_ref[:, pl.ds(place, half_width)] = tokens[rows]
        term = dot_nt(matrix, bg_ref[...])
        grad = term if grad is None else grad + term
    ga_t_ref[...] = grad.astype(low)


def project(token_dest, patch_rows, att_t, bg_own, bg_away, own, away):
    row_count, model_width = patch_rows.shape
    args = (token_dest, patch_rows, att_t, bg_own, bg_away, *own, *away)
    shapes = [(row_count // GROUP, GROUP * model_width), (model_width, row_count)]
    return pl.pallas_call(
        project_kernel,
        grid=(1,),
        in_specs=[full(arg.shape) for arg in args],
        out_specs=[full(shape) for shape in shapes],
        out_shape=[jax.ShapeDtypeStruct(shape, low) for shape in shapes],
        scratch_shapes=[pltpu.VMEM((row_count, model_width), low)],
        compiler_params=params(),
        cost_estimate=cost(6, 0),
        name="project",
    )(*args)


def finish_kernel(
    norm_scale, own_ref, core_ref, x_ref, both_ref, gain_ref, out_ref, gain_out_ref
):
    core, x_bit, _, _ = position()
    rows, cols = own_ref.shape
    for x_off, pair in enumerate(((own_ref, core_ref), (x_ref, both_ref))):
        for core_off, piece in enumerate(pair):
            to_rows = pl.ds(pl.multiple_of((x_bit ^ x_off) * rows, rows), rows)
            to_cols = pl.ds(pl.multiple_of((core ^ core_off) * cols, LANES), cols)
            out_ref[to_rows, to_cols] = piece[...].astype(wide) * norm_scale
    gain_out_ref[...] = jnp.sum(gain_ref[...], axis=0) * norm_scale


def finish(held, gain_terms, norm_scale):
    rows, cols = held[0].shape
    share = gain_terms.shape[2]
    return pl.pallas_call(
        functools.partial(finish_kernel, norm_scale),
        grid=(1,),
        in_specs=[full(piece.shape) for piece in held] + [full(gain_terms.shape)],
        out_specs=[full((2 * rows, 2 * cols)), full((1, share))],
        out_shape=[
            jax.ShapeDtypeStruct((2 * rows, 2 * cols), wide),
            jax.ShapeDtypeStruct((1, share), wide),
        ],
        compiler_params=params(),
        cost_estimate=cost(1, 0),
        name="finish",
    )(*held, gain_terms)


def joint_permute(value, seq_count, dp_count, target):
    pairs = []
    for s in range(seq_count):
        for d in range(dp_count):
            to_s, to_d = target(s, d)
            pairs.append((s * dp_count + d, to_s * dp_count + to_d))
    return lax.ppermute(value, ("seq", "dp"), pairs)


def core_target(s, d):
    return s, d ^ 1


def first_target(s, d):
    return (s, d ^ 2) if d % 2 == 0 else (s ^ 1, d)


def second_target(s, d):
    return (s ^ 1, d) if d % 2 == 0 else (s, d ^ 2)


def far_target(step):
    return lambda s, d: (s ^ (2 * step), d)


def gather_far(place, w_out, seq_count, send):
    share, model_width = w_out.shape
    rows, cols = share // 2, model_width // 2
    core, x_bit = place[0], place[1]
    own = lax.dynamic_slice(w_out, (x_bit * rows, core * cols), (rows, cols))
    return [own] + [send(own, target=far_target(step)) for step in range(1, seq_count // 2)]


def to_relative(place, blocks, far_count):
    core, x_bit, y_bit, z_index = place
    width = blocks.shape[-1]
    blocks = blocks.reshape(far_count, 2, 2, -1, width)[jnp.arange(far_count) ^ z_index]
    blocks = jnp.where(y_bit == 0, blocks, blocks[:, ::-1])
    blocks = jnp.where(x_bit == 0, blocks, blocks[:, :, ::-1])
    x_first, y_first = blocks.transpose(2, 1, 0, 3, 4), blocks.transpose(1, 2, 0, 3, 4)
    return jnp.where(core == 0, x_first, y_first).reshape((4, far_count) + x_first.shape[3:])


def from_relative(place, blocks):
    core, x_bit, y_bit, z_index = place
    _, far_count, rows, width = blocks.shape
    blocks = blocks.reshape(2, 2, far_count, rows, width)
    y_first = blocks.transpose(2, 0, 1, 3, 4)
    blocks = jnp.where(core == 0, blocks.transpose(2, 1, 0, 3, 4), y_first)
    blocks = jnp.where(y_bit == 0, blocks, blocks[:, ::-1])
    blocks = jnp.where(x_bit == 0, blocks, blocks[:, :, ::-1])
    return blocks[jnp.arange(far_count) ^ z_index]


def add_low(left, right):
    return (left.astype(wide) + right.astype(wide)).astype(low)


def together(*values):
    return lax.optimization_barrier(values)


def per_device(patches, lengths, token_dest, gain, w_qkv, w_out, cotangent):
    seq_count = lax.axis_size("seq")
    dp_count = lax.axis_size("dp")
    far_count = seq_count // 2
    send = functools.partial(joint_permute, seq_count=seq_count, dp_count=dp_count)
    place = position()
    patch_rows, shard_lengths = patches[0], lengths[0, 0]
    row_count, model_width = patch_rows.shape
    half_width = model_width // HALVES
    token_count = row_count // GROUP
    direct = 4 * far_count == HEADS

    far = gather_far(place, w_out, seq_count, send)
    projected = project_rows(patch_rows, gain, w_qkv)
    projected, cotangent = together(projected, cotangent)
    returned = lax.all_to_all(cotangent[0], "seq", split_axis=0, concat_axis=0, tiled=True)
    projected, far = together(projected, far)
    level = jnp.stack(far)
    near = send(level, target=second_target)
    beyond = send(level, target=first_target)
    att_t, lse = attention(shard_lengths, projected, far_count)
    if not direct:
        att_t = to_relative(place, att_t, far_count)
    att_other = send(att_t, target=core_target)
    returned, near = together(returned, near)
    level_core = send(level, target=core_target)
    corner = send(near, target=first_target)
    near_core = send(near, target=core_target)
    beyond_core = send(beyond, target=core_target)
    bg_own, bg_away = place_rows(token_dest, returned)
    bg_other = send(bg_away, target=core_target)
    bg_other, corner, beyond_core = together(bg_other, corner, beyond_core)
    corner_core = send(corner, target=core_target)

    merge = lambda piece: piece.reshape(-1, piece.shape[-1])
    shape = (2, far_count, -1, half_width)
    terms = []
    for first in (1, 0):
        mine = merge(att_t[2 * first : 2 * first + 2])
        other = jnp.concatenate([merge(att_other[first]), merge(att_other[first + 2])])
        term = dot_nn(mine, bg_own) + dot_nn(other, bg_other)
        terms.append(term.astype(low).reshape(shape))
    away_terms, kept = terms
    arrived = send(away_terms, target=first_target)
    own = [merge(piece) for piece in (level, near, beyond, corner)]
    away = [merge(piece) for piece in (level_core, beyond_core, near_core, corner_core)]
    outgoing, ga_t = project(
        token_dest, patch_rows, merge(att_t), bg_own, bg_away, own, away
    )
    merged = lax.all_to_all(
        outgoing.reshape(seq_count, token_count // seq_count, GROUP * model_width),
        "seq", split_axis=0, concat_axis=0, tiled=True,
    ).reshape(token_count, GROUP * model_width)
    if not direct:
        ga_t = from_relative(place, ga_t.reshape(4, far_count, -1, row_count))
    ga_t, kept = together(ga_t, add_low(kept, arrived))
    arrived = send(kept[1], target=second_target)
    grads = attention_grad(shard_lengths, projected, lse, ga_t, direct)
    level, grads = together(add_low(kept[0], arrived), grads)
    weight_terms = [level[0]] + [
        send(level[step], target=far_target(step)) for step in range(1, far_count)
    ]
    grad_normed, gain_terms = normed_grad(patch_rows, w_qkv, grads, seq_count, dp_count)
    gain_terms, merged, grad_normed = together(gain_terms, merged, grad_normed)
    gain_arrived = lax.all_to_all(
        gain_terms, ("seq", "dp"), split_axis=0, concat_axis=0, tiled=True
    )
    patch_grad, merged = patch_grads(patch_rows, gain, grad_normed, bg_own, bg_away, merged)
    total = sum(term.astype(wide) for term in weight_terms).astype(low)
    held = [total, send(total, target=core_target)]
    held += [send(total, target=lambda s, d, flip=flip: (s, d ^ flip)) for flip in (2, 3)]
    norm_scale = 1.0 / math.sqrt(row_count * seq_count * dp_count)
    if direct:
        own_weight, own_gain = finish(held, gain_arrived, norm_scale)
        own_gain = own_gain[0]
    else:
        rows = total.shape[0]
        held = jnp.stack(held).reshape(2, 2, rows, half_width)
        held = jnp.where(place[1] == 0, held, held[::-1])
        held = jnp.where(place[0] == 0, held, held[:, ::-1])
        held = held.astype(wide).transpose(0, 2, 1, 3)
        own_weight = held.reshape(2 * rows, model_width) * norm_scale
        own_gain = jnp.sum(gain_arrived, axis=(0, 1)) * norm_scale
    return (merged[None], patch_grad[None], own_weight, own_gain)


def solution(mesh):
    placed = (
        P("dp", "seq", None),
        P("dp", "seq", None),
        P("dp", "seq"),
        P(),
        P(),
        P("seq", None),
        P("dp", "seq", None),
    )
    return jax.shard_map(
        per_device,
        mesh=mesh,
        in_specs=placed,
        out_specs=(P("dp", "seq", None), P("dp", "seq", None), P("seq", None), P("seq")),
        check_vma=False,
    )
```

```python
import functools
import math

import jax
import jax.numpy as jnp
from jax import lax
from jax.experimental import pallas as pl
from jax.experimental.pallas import tpu as pltpu
from jax.sharding import PartitionSpec as P

HEADS = 16
GROUP = 4
HALVES = 2
LANES = 128
CHUNK = 64
LOG2_E = math.log2(math.e)
VMEM_LIMIT = 32 * 1024 * 1024
PART = 256
HBM_BYTES_PER_US = 3690000

eps = 1e-06
low = jnp.bfloat16
wide = jnp.float32


def params():
    return pltpu.CompilerParams(vmem_limit_bytes=VMEM_LIMIT)


def cost(microseconds, flops):
    nominal = microseconds * HBM_BYTES_PER_US
    return pl.CostEstimate(flops=flops, bytes_accessed=nominal, transcendentals=0)


def smem():
    return pl.BlockSpec(memory_space=pltpu.SMEM)


def dot_nt(left, right):
    return lax.dot_general(left, right, (((1,), (1,)), ((), ())), preferred_element_type=wide)


def dot_tn(left, right):
    return lax.dot_general(left, right, (((0,), (0,)), ((), ())), preferred_element_type=wide)


def dot_nn(left, right):
    return jnp.dot(left, right, preferred_element_type=wide)


def score_groups(head_size, width):
    groups = []
    for head in range(width // head_size):
        start = head * head_size
        if groups and start + head_size <= groups[-1][0] + PART:
            groups[-1][1].append(head)
        else:
            groups.append((min(start // LANES * LANES, width - PART), [head]))
    return groups


def value_groups(head_size, width):
    groups = []
    for first in range(0, width, PART):
        last = min(first + PART, width)
        groups.append((first, last, range(first // head_size, -(-last // head_size))))
    return groups


def image_bias(lengths_ref, row_count):
    def image_of(index):
        number = jnp.zeros(index.shape, jnp.int32)
        end = jnp.int32(0)
        for image in range(lengths_ref.shape[0]):
            end = end + lengths_ref[image] * GROUP
            number = number + (index >= end).astype(jnp.int32)
        return number

    rows = lax.broadcasted_iota(jnp.int32, (row_count, row_count), 0)
    cols = lax.broadcasted_iota(jnp.int32, (row_count, row_count), 1)
    return jnp.where(image_of(rows) == image_of(cols), 0.0, -jnp.inf).astype(wide)


def standardise(rows):
    centred = rows - jnp.mean(rows, axis=-1, keepdims=True)
    inv_spread = lax.rsqrt(jnp.mean(centred * centred, axis=-1, keepdims=True) + eps)
    return centred * inv_spread, inv_spread


def full(shape):
    return pl.BlockSpec(shape, lambda *steps: (0,) * len(shape))


def only(head, head_size, first, value):
    lane = lax.broadcasted_iota(jnp.int32, (1, value.shape[1]), 1) + first
    keep = (lane >= head * head_size) & (lane < (head + 1) * head_size)
    return value * jnp.where(keep, 1.0, 0.0).astype(low)


def head_products(out_ref, left_ref, right_t, head_size):
    row_count, width = left_ref.shape
    for first, heads in score_groups(head_size, width):
        window = left_ref[:, first : first + PART]
        stacked = jnp.concatenate(
            [only(head, head_size, first, window) for head in heads], axis=0
        )
        product = dot_nn(stacked, right_t[first : first + PART])
        for place, head in enumerate(heads):
            out_ref[head] = product[place * row_count : (place + 1) * row_count]


def head_sums(out_t_ref, weights_ref, value_ref, head_size):
    row_count, width = value_ref.shape
    for first, last, heads in value_groups(head_size, width):
        stacked = jnp.concatenate(
            [only(head, head_size, first, value_ref[:, first:last]) for head in heads], axis=0
        )
        lanes = slice(heads[0] * row_count, (heads[-1] + 1) * row_count)
        out_t_ref[first:last] = dot_nn(weights_ref[:, lanes], stacked).astype(low).T


def position():
    s, d = lax.axis_index("seq"), lax.axis_index("dp")
    return d % 2, d // 2, s % 2, s // 2


def relative_block(block):
    core, x_bit, y_bit, z_index = position()
    x_off, y_off = (block % 2) ^ x_bit, (block // 2 % 2) ^ y_bit
    z_off = (block // 4) ^ z_index
    return jnp.where(core == 0, y_off + 2 * x_off, x_off + 2 * y_off), z_off


def project_rows(patch_rows, gain, w_qkv):
    standard, _ = standardise(patch_rows.astype(wide))
    return dot_nn((standard * gain).astype(low), w_qkv).astype(low)


def attention_kernel(
    score_scale, head_size, relative, lengths_ref, q_ref, k_ref, v_ref,
    att_t_ref, lse_ref, keys_t, turned, bias, scores, probs,
):
    row_count, half_width = q_ref.shape
    heads = half_width // head_size
    half = pl.program_id(0)

    @pl.when(half == 0)
    def _():
        bias[...] = image_bias(lengths_ref, row_count)

    keys_t[...] = k_ref[...].T
    head_products(scores, q_ref, keys_t, head_size)
    lane = lax.broadcasted_iota(jnp.int32, (CHUNK, LANES), 1)
    for row in range(0, row_count, CHUNK):
        rows = slice(row, row + CHUNK)
        lse = jnp.zeros((CHUNK, LANES), wide)
        for head in range(heads):
            scaled = scores[head, rows] * (score_scale * LOG2_E) + bias[rows]
            row_max = jnp.max(scaled, axis=-1, keepdims=True)
            weights = jnp.exp2(scaled - row_max)
            total = jnp.sum(weights, axis=-1, keepdims=True)
            lanes = slice(head * row_count, (head + 1) * row_count)
            probs[rows, lanes] = (weights * (1.0 / total)).astype(low)
            lse = jnp.where(lane == head, row_max + jnp.log2(total), lse)
        lse_ref[0, rows] = lse
    head_sums(turned, probs, v_ref, head_size)
    for head in range(heads):
        block = turned[head * head_size : (head + 1) * head_size, :]
        number = half * heads + head
        if relative:
            near, far = relative_block(number)
            att_t_ref[near, far] = block
        else:
            att_t_ref[number] = block


def attention(shard_lengths, projected, far_count):
    row_count, model_width = projected.shape[0], projected.shape[1] // 3
    half_width = model_width // HALVES
    head_size = model_width // HEADS
    heads = HEADS // HALVES
    relative = 4 * far_count == HEADS
    shape = ((4, far_count) if relative else (HEADS,)) + (head_size, row_count)
    part = lambda kind: pl.BlockSpec(
        (row_count, half_width), lambda half: (0, kind * HALVES + half)
    )
    return pl.pallas_call(
        functools.partial(attention_kernel, 1.0 / math.sqrt(head_size), head_size, relative),
        grid=(HALVES,),
        in_specs=[smem(), part(0), part(1), part(2)],
        out_specs=[
            full(shape),
            pl.BlockSpec((1, row_count, LANES), lambda half: (half, 0, 0)),
        ],
        out_shape=[
            jax.ShapeDtypeStruct(shape, low),
            jax.ShapeDtypeStruct((HALVES, row_count, LANES), wide),
        ],
        scratch_shapes=[
            pltpu.VMEM((half_width, row_count), low),
            pltpu.VMEM((half_width, row_count), low),
            pltpu.VMEM((row_count, row_count), wide),
            pltpu.VMEM((heads, row_count, row_count), wide),
            pltpu.VMEM((row_count, heads * row_count), low),
        ],
        compiler_params=params(),
        cost_estimate=cost(6, 0),
        name="attention",
    )(shard_lengths, projected, projected, projected)


def attention_grad_kernel(
    score_scale, head_size, relative, lengths_ref, q_ref, k_ref, v_ref, lse_ref, ga_ref,
    out_ref, ga, turned, bias, scores, grad_probs, probs, grad_scores,
):
    row_count, half_width = ga.shape
    heads = half_width // head_size
    half = pl.program_id(0)

    @pl.when(half == 0)
    def _():
        bias[...] = image_bias(lengths_ref, row_count)

    for head in range(heads):
        number = half * heads + head
        if relative:
            near, far = relative_block(number)
            number = near * (HEADS // 4) + far
        turned[2, head * head_size : (head + 1) * head_size] = ga_ref[number]
    ga[...] = turned[2].T
    turned[0] = k_ref[...].T
    turned[1] = v_ref[...].T
    head_products(scores, q_ref, turned.at[0], head_size)
    head_products(grad_probs, ga, turned.at[1], head_size)
    for row in range(0, row_count, CHUNK):
        rows = slice(row, row + CHUNK)
        lse = lse_ref[0, rows]
        for head in range(heads):
            scaled = scores[head, rows] * (score_scale * LOG2_E) + bias[rows]
            chance = jnp.exp2(scaled - lse[:, head : head + 1])
            incoming = grad_probs[head, rows]
            inner = jnp.sum(incoming * chance, axis=-1, keepdims=True)
            lanes = slice(head * row_count, (head + 1) * row_count)
            probs[rows, lanes] = chance.astype(low)
            grad_scores[rows, lanes] = (chance * (incoming - inner) * score_scale).astype(low)
    head_sums(out_ref.at[0, 0], grad_scores, k_ref, head_size)
    turned[0] = q_ref[...].T
    for head in range(heads):
        rows = slice(head * head_size, (head + 1) * head_size)
        lanes = slice(head * row_count, (head + 1) * row_count)
        out_ref[0, 1, rows] = dot_nn(turned[0, rows], grad_scores[:, lanes]).astype(low)
        out_ref[0, 2, rows] = dot_nn(turned[2, rows], probs[:, lanes]).astype(low)


def attention_grad(shard_lengths, projected, lse, ga_t, relative):
    row_count, model_width = projected.shape[0], projected.shape[1] // 3
    half_width = model_width // HALVES
    head_size = model_width // HEADS
    heads = HEADS // HALVES
    part = lambda kind: pl.BlockSpec(
        (row_count, half_width), lambda half: (0, kind * HALVES + half)
    )
    shape = (HEADS, head_size, row_count)
    return pl.pallas_call(
        functools.partial(
            attention_grad_kernel, 1.0 / math.sqrt(head_size), head_size, relative
        ),
        grid=(HALVES,),
        in_specs=[smem(), part(0), part(1), part(2)]
        + [pl.BlockSpec((1, row_count, LANES), lambda half: (half, 0, 0))]
        + [full(shape)],
        out_specs=pl.BlockSpec((1, 3, half_width, row_count), lambda half: (half, 0, 0, 0)),
        out_shape=jax.ShapeDtypeStruct((HALVES, 3, half_width, row_count), low),
        scratch_shapes=[
            pltpu.VMEM((row_count, half_width), low),
            pltpu.VMEM((3, half_width, row_count), low),
            pltpu.VMEM((row_count, row_count), wide),
            pltpu.VMEM((heads, row_count, row_count), wide),
            pltpu.VMEM((heads, row_count, row_count), wide),
            pltpu.VMEM((row_count, heads * row_count), low),
            pltpu.VMEM((row_count, heads * row_count), low),
        ],
        compiler_params=params(),
        cost_estimate=cost(9, 0),
        name="attention_grad",
    )(shard_lengths, projected, projected, projected, lse, ga_t.reshape(shape))


def normed_grad_kernel(copies_each, x_ref, w_ref, grad_ref, out_ref, gain_out_ref):
    row_count, model_width = x_ref.shape
    half_width = model_width // HALVES
    step = pl.program_id(0)
    cols = pl.ds(pl.multiple_of(step * PART, PART), PART)
    parts = [(kind, half) for half in range(HALVES) for kind in range(3)]
    weights = jnp.concatenate(
        [
            w_ref[:, (kind * HALVES + half) * half_width : (kind * HALVES + half + 1) * half_width]
            for kind, half in parts
        ],
        axis=1,
    )
    out_ref[:, cols] = dot_nn(weights, grad_ref[...].reshape(3 * model_width, row_count)).T

    @pl.when(step == pl.num_programs(0) - 1)
    def _():
        total = None
        for row in range(0, row_count, LANES):
            rows = slice(row, row + LANES)
            standard, _ = standardise(x_ref[rows].astype(wide))
            term = jnp.sum(out_ref[rows] * standard, axis=0, keepdims=True)
            total = term if total is None else total + term
        share = gain_out_ref.shape[2]
        for number in range(model_width // share):
            term = total[:, number * share : (number + 1) * share]
            for copy in range(copies_each):
                gain_out_ref[number * copies_each + copy] = term


def normed_grad(patch_rows, w_qkv, grads, seq_count, dp_count):
    row_count, model_width = patch_rows.shape
    share = model_width // seq_count
    spread = (seq_count * dp_count, 1, share)
    return pl.pallas_call(
        functools.partial(normed_grad_kernel, dp_count),
        grid=(model_width // PART,),
        in_specs=[
            full(patch_rows.shape),
            pl.BlockSpec((PART, 3 * model_width), lambda step: (step, 0)),
            full(grads.shape),
        ],
        out_specs=[full(patch_rows.shape), full(spread)],
        out_shape=[
            jax.ShapeDtypeStruct((row_count, model_width), wide),
            jax.ShapeDtypeStruct(spread, wide),
        ],
        compiler_params=params(),
        cost_estimate=cost(7, 0),
        name="normed_grad",
    )(patch_rows, w_qkv, grads)


def patch_grad_kernel(
    x_ref, gain_ref, grad_ref, bg_own_ref, bg_away_ref, merged_ref, patch_ref, merged_out_ref
):
    row_count, model_width = x_ref.shape
    half_width = model_width // HALVES
    core = position()[0]
    merged_out_ref[...] = merged_ref[...]
    for row in range(0, row_count, LANES):
        rows = slice(row, row + LANES)
        standard, inv_spread = standardise(x_ref[rows].astype(wide))
        grad = grad_ref[rows] * gain_ref[...]
        branch = inv_spread * (
            grad
            - jnp.mean(grad, axis=-1, keepdims=True)
            - standard * jnp.mean(grad * standard, axis=-1, keepdims=True)
        )
        for half in range(HALVES):
            cols = slice(half * half_width, (half + 1) * half_width)
            incoming = jnp.where(core == half, bg_own_ref[rows], bg_away_ref[rows])
            patch_ref[rows, cols] = (incoming.astype(wide) + branch[:, cols]).astype(low)


def patch_grads(patch_rows, gain, grad_normed, bg_own, bg_away, merged):
    args = (patch_rows, gain, grad_normed, bg_own, bg_away, merged)
    return pl.pallas_call(
        patch_grad_kernel,
        grid=(1,),
        in_specs=[full(arg.shape) for arg in args],
        out_specs=[full(patch_rows.shape), full(merged.shape)],
        out_shape=[
            jax.ShapeDtypeStruct(patch_rows.shape, low),
            jax.ShapeDtypeStruct(merged.shape, low),
        ],
        compiler_params=params(),
        cost_estimate=cost(3, 0),
        name="patch_grads",
    )(*args)


def placing_matrix(dest_ref, row_count):
    token_count = row_count // GROUP
    peer_count = token_count // lax.axis_size("seq")
    token_bits = token_count.bit_length() - 1
    dest = dest_ref[...]
    shard = lax.shift_right_logical(dest, jnp.full_like(dest, token_bits))
    slot = shard * peer_count + (dest & (peer_count - 1))
    square = (token_count, token_count)
    chosen = (lax.broadcasted_iota(jnp.int32, square, 0) == slot).astype(low)
    shape = (token_count, row_count)
    token = lax.broadcasted_iota(jnp.int32, shape, 0) * GROUP
    row = lax.broadcasted_iota(jnp.int32, shape, 1)
    parts = []
    for member in range(GROUP):
        spread = (row == token + member).astype(low)
        parts.append(dot_nn(chosen, spread).astype(low))
    return jnp.concatenate(parts, axis=0)


def place_kernel(dest_ref, returned_ref, own_ref, away_ref, stacked):
    token_count = returned_ref.shape[0]
    row_count, model_width = stacked.shape
    half_width = model_width // HALVES
    for member in range(GROUP):
        stacked[member * token_count : (member + 1) * token_count] = returned_ref[
            :, member * model_width : (member + 1) * model_width
        ]
    placing = placing_matrix(dest_ref, row_count)
    core = position()[0]
    for side, out_ref in enumerate((own_ref, away_ref)):
        cols = pl.ds(pl.multiple_of((core ^ side) * half_width, LANES), half_width)
        out_ref[...] = dot_tn(placing, stacked[:, cols]).astype(low)


def place_rows(token_dest, returned):
    token_count, merged_width = returned.shape
    row_count, model_width = token_count * GROUP, merged_width // GROUP
    half_width = model_width // HALVES
    return pl.pallas_call(
        place_kernel,
        grid=(1,),
        in_specs=[full(token_dest.shape), full(returned.shape)],
        out_specs=[full((row_count, half_width))] * 2,
        out_shape=[jax.ShapeDtypeStruct((row_count, half_width), low)] * 2,
        scratch_shapes=[pltpu.VMEM((row_count, model_width), low)],
        compiler_params=params(),
        cost_estimate=cost(2, 0),
        name="place_rows",
    )(token_dest, returned)


def project_kernel(dest_ref, x_ref, att_t_ref, bg_own_ref, bg_away_ref, *refs):
    own, away, (out_ref, ga_t_ref, attended) = refs[:4], refs[4:8], refs[8:]
    row_count, model_width = x_ref.shape
    half_width = model_width // HALVES
    token_count = row_count // GROUP
    placing = placing_matrix(dest_ref, row_count)
    core = position()[0]
    attended[...] = att_t_ref[...].T
    grad = None
    for side, (pieces, bg_ref) in enumerate(((own, bg_own_ref), (away, bg_away_ref))):
        matrix = jnp.concatenate([piece[...] for piece in pieces], axis=0)
        first = pl.multiple_of((core ^ side) * half_width, LANES)
        branch = dot_nn(attended[...], matrix)
        block = x_ref[:, pl.ds(first, half_width)].astype(wide) + branch
        tokens = dot_nn(placing, block.astype(low)).astype(low)
        for member in range(GROUP):
            place = pl.multiple_of(member * model_width + first, LANES)
            rows = slice(member * token_count, (member + 1) * token_count)
            out_ref[:, pl.ds(place, half_width)] = tokens[rows]
        term = dot_nt(matrix, bg_ref[...])
        grad = term if grad is None else grad + term
    ga_t_ref[...] = grad.astype(low)


def project(token_dest, patch_rows, att_t, bg_own, bg_away, own, away):
    row_count, model_width = patch_rows.shape
    args = (token_dest, patch_rows, att_t, bg_own, bg_away, *own, *away)
    shapes = [(row_count // GROUP, GROUP * model_width), (model_width, row_count)]
    return pl.pallas_call(
        project_kernel,
        grid=(1,),
        in_specs=[full(arg.shape) for arg in args],
        out_specs=[full(shape) for shape in shapes],
        out_shape=[jax.ShapeDtypeStruct(shape, low) for shape in shapes],
        scratch_shapes=[pltpu.VMEM((row_count, model_width), low)],
        compiler_params=params(),
        cost_estimate=cost(6, 0),
        name="project",
    )(*args)


def finish_kernel(
    norm_scale, own_ref, core_ref, x_ref, both_ref, gain_ref, out_ref, gain_out_ref
):
    core, x_bit, _, _ = position()
    rows, cols = own_ref.shape
    for x_off, pair in enumerate(((own_ref, core_ref), (x_ref, both_ref))):
        for core_off, piece in enumerate(pair):
            to_rows = pl.ds(pl.multiple_of((x_bit ^ x_off) * rows, rows), rows)
            to_cols = pl.ds(pl.multiple_of((core ^ core_off) * cols, LANES), cols)
            out_ref[to_rows, to_cols] = piece[...].astype(wide) * norm_scale
    gain_out_ref[...] = jnp.sum(gain_ref[...], axis=0) * norm_scale


def finish(held, gain_terms, norm_scale):
    rows, cols = held[0].shape
    share = gain_terms.shape[2]
    return pl.pallas_call(
        functools.partial(finish_kernel, norm_scale),
        grid=(1,),
        in_specs=[full(piece.shape) for piece in held] + [full(gain_terms.shape)],
        out_specs=[full((2 * rows, 2 * cols)), full((1, share))],
        out_shape=[
            jax.ShapeDtypeStruct((2 * rows, 2 * cols), wide),
            jax.ShapeDtypeStruct((1, share), wide),
        ],
        compiler_params=params(),
        cost_estimate=cost(1, 0),
        name="finish",
    )(*held, gain_terms)


def joint_permute(value, seq_count, dp_count, target):
    pairs = []
    for s in range(seq_count):
        for d in range(dp_count):
            to_s, to_d = target(s, d)
            pairs.append((s * dp_count + d, to_s * dp_count + to_d))
    return lax.ppermute(value, ("seq", "dp"), pairs)


def core_target(s, d):
    return s, d ^ 1


def first_target(s, d):
    return (s, d ^ 2) if d % 2 == 0 else (s ^ 1, d)


def second_target(s, d):
    return (s ^ 1, d) if d % 2 == 0 else (s, d ^ 2)


def both_target(s, d):
    return s ^ 1, d ^ 2


def far_target(step):
    return lambda s, d: (s ^ (2 * step), d)


def gather_far(place, w_out, seq_count, send):
    share, model_width = w_out.shape
    rows, cols = share // 2, model_width // 2
    core, x_bit = place[0], place[1]
    own = lax.dynamic_slice(w_out, (x_bit * rows, core * cols), (rows, cols))
    return [own] + [send(own, target=far_target(step)) for step in range(1, seq_count // 2)]


def to_relative(place, blocks, far_count):
    core, x_bit, y_bit, z_index = place
    width = blocks.shape[-1]
    blocks = blocks.reshape(far_count, 2, 2, -1, width)[jnp.arange(far_count) ^ z_index]
    blocks = jnp.where(y_bit == 0, blocks, blocks[:, ::-1])
    blocks = jnp.where(x_bit == 0, blocks, blocks[:, :, ::-1])
    x_first, y_first = blocks.transpose(2, 1, 0, 3, 4), blocks.transpose(1, 2, 0, 3, 4)
    return jnp.where(core == 0, x_first, y_first).reshape((4, far_count) + x_first.shape[3:])


def from_relative(place, blocks):
    core, x_bit, y_bit, z_index = place
    _, far_count, rows, width = blocks.shape
    blocks = blocks.reshape(2, 2, far_count, rows, width)
    y_first = blocks.transpose(2, 0, 1, 3, 4)
    blocks = jnp.where(core == 0, blocks.transpose(2, 1, 0, 3, 4), y_first)
    blocks = jnp.where(y_bit == 0, blocks, blocks[:, ::-1])
    blocks = jnp.where(x_bit == 0, blocks, blocks[:, :, ::-1])
    return blocks[jnp.arange(far_count) ^ z_index]


def together(*values):
    return lax.optimization_barrier(values)


def per_device(patches, lengths, token_dest, gain, w_qkv, w_out, cotangent):
    seq_count = lax.axis_size("seq")
    dp_count = lax.axis_size("dp")
    far_count = seq_count // 2
    send = functools.partial(joint_permute, seq_count=seq_count, dp_count=dp_count)
    place = position()
    patch_rows, shard_lengths = patches[0], lengths[0, 0]
    row_count, model_width = patch_rows.shape
    half_width = model_width // HALVES
    token_count = row_count // GROUP
    direct = 4 * far_count == HEADS

    far = gather_far(place, w_out, seq_count, send)
    projected = project_rows(patch_rows, gain, w_qkv)
    projected, cotangent = together(projected, cotangent)
    returned = lax.all_to_all(cotangent[0], "seq", split_axis=0, concat_axis=0, tiled=True)
    att_t, lse = attention(shard_lengths, projected, far_count)
    att_t, lse, far = together(att_t, lse, far)
    if not direct:
        att_t = to_relative(place, att_t, far_count)
    level = jnp.stack(far)
    near = send(level, target=second_target)
    beyond = send(level, target=first_target)
    corner = send(level, target=both_target)
    att_other = send(att_t, target=core_target)
    bg_own, bg_away = place_rows(token_dest, returned)
    bg_other = send(bg_away, target=core_target)
    bg_other, att_other, near, beyond, corner = together(
        bg_other, att_other, near, beyond, corner
    )
    level_core = send(level, target=core_target)
    near_core = send(near, target=core_target)
    beyond_core = send(beyond, target=core_target)
    corner_core = send(corner, target=core_target)

    merge = lambda piece: piece.reshape(-1, piece.shape[-1])
    terms = []
    for first in (1, 0):
        mine = merge(att_t[2 * first : 2 * first + 2])
        other = jnp.concatenate([merge(att_other[first]), merge(att_other[first + 2])])
        term = dot_nn(mine, bg_own) + dot_nn(other, bg_other)
        terms.append(term.astype(low).reshape(2, far_count, -1, half_width))
    arrived = [
        send(terms[1][1], target=second_target),
        send(terms[0][0], target=first_target),
        send(terms[0][1], target=both_target),
    ]
    kept = terms[1][0]
    own = [merge(piece) for piece in (level, near, beyond, corner)]
    away = [merge(piece) for piece in (level_core, beyond_core, near_core, corner_core)]
    outgoing, ga_t = project(
        token_dest, patch_rows, merge(att_t), bg_own, bg_away, own, away
    )
    merged = lax.all_to_all(
        outgoing.reshape(seq_count, token_count // seq_count, GROUP * model_width),
        "seq", split_axis=0, concat_axis=0, tiled=True,
    ).reshape(token_count, GROUP * model_width)
    if not direct:
        ga_t = from_relative(place, ga_t.reshape(4, far_count, -1, row_count))
    grads = attention_grad(shard_lengths, projected, lse, ga_t, direct)
    grads, arrived = together(grads, arrived)
    level = sum(term.astype(wide) for term in [kept, *arrived]).astype(low)
    weight_terms = [level[0]] + [
        send(level[step], target=far_target(step)) for step in range(1, far_count)
    ]
    grad_normed, gain_terms = normed_grad(patch_rows, w_qkv, grads, seq_count, dp_count)
    gain_terms, merged, grad_normed, weight_terms = together(
        gain_terms, merged, grad_normed, weight_terms
    )
    gain_arrived = lax.all_to_all(
        gain_terms, ("seq", "dp"), split_axis=0, concat_axis=0, tiled=True
    )
    patch_grad, merged = patch_grads(patch_rows, gain, grad_normed, bg_own, bg_away, merged)
    total = sum(term.astype(wide) for term in weight_terms).astype(low)
    held = [total, send(total, target=core_target)]
    held += [send(total, target=lambda s, d, flip=flip: (s, d ^ flip)) for flip in (2, 3)]
    norm_scale = 1.0 / math.sqrt(row_count * seq_count * dp_count)
    if direct:
        own_weight, own_gain = finish(held, gain_arrived, norm_scale)
        own_gain = own_gain[0]
    else:
        rows = total.shape[0]
        held = jnp.stack(held).reshape(2, 2, rows, half_width)
        held = jnp.where(place[1] == 0, held, held[::-1])
        held = jnp.where(place[0] == 0, held, held[:, ::-1])
        held = held.astype(wide).transpose(0, 2, 1, 3)
        own_weight = held.reshape(2 * rows, model_width) * norm_scale
        own_gain = jnp.sum(gain_arrived, axis=(0, 1)) * norm_scale
    return (merged[None], patch_grad[None], own_weight, own_gain)


def solution(mesh):
    placed = (
        P("dp", "seq", None),
        P("dp", "seq", None),
        P("dp", "seq"),
        P(),
        P(),
        P("seq", None),
        P("dp", "seq", None),
    )
    return jax.shard_map(
        per_device,
        mesh=mesh,
        in_specs=placed,
        out_specs=(P("dp", "seq", None), P("dp", "seq", None), P("seq", None), P("seq")),
        check_vma=False,
    )
```

```python
import functools
import math

import jax
import jax.numpy as jnp
from jax import lax
from jax.experimental import pallas as pl
from jax.experimental.pallas import tpu as pltpu
from jax.sharding import PartitionSpec as P

HEADS = 16
GROUP = 4
HALVES = 2
LANES = 128
CHUNK = 64
LOG2_E = math.log2(math.e)
VMEM_LIMIT = 32 * 1024 * 1024
PART = 256
HBM_BYTES_PER_US = 3690000

eps = 1e-06
low = jnp.bfloat16
wide = jnp.float32


def params(limit=VMEM_LIMIT):
    return pltpu.CompilerParams(vmem_limit_bytes=limit)


def cost(microseconds, flops):
    nominal = microseconds * HBM_BYTES_PER_US
    return pl.CostEstimate(flops=flops, bytes_accessed=nominal, transcendentals=0)


def smem():
    return pl.BlockSpec(memory_space=pltpu.SMEM)


def dot_nt(left, right):
    return lax.dot_general(left, right, (((1,), (1,)), ((), ())), preferred_element_type=wide)


def dot_tn(left, right):
    return lax.dot_general(left, right, (((0,), (0,)), ((), ())), preferred_element_type=wide)


def dot_nn(left, right):
    return jnp.dot(left, right, preferred_element_type=wide)


def score_groups(head_size, width):
    groups = []
    for head in range(width // head_size):
        start = head * head_size
        if groups and start + head_size <= groups[-1][0] + PART:
            groups[-1][1].append(head)
        else:
            groups.append((min(start // LANES * LANES, width - PART), [head]))
    return groups


def value_groups(head_size, width):
    groups = []
    for first in range(0, width, PART):
        last = min(first + PART, width)
        groups.append((first, last, range(first // head_size, -(-last // head_size))))
    return groups


def image_bias(lengths_ref, row_count):
    def image_of(index):
        number = jnp.zeros(index.shape, jnp.int32)
        end = jnp.int32(0)
        for image in range(lengths_ref.shape[0]):
            end = end + lengths_ref[image] * GROUP
            number = number + (index >= end).astype(jnp.int32)
        return number

    rows = lax.broadcasted_iota(jnp.int32, (row_count, row_count), 0)
    cols = lax.broadcasted_iota(jnp.int32, (row_count, row_count), 1)
    return jnp.where(image_of(rows) == image_of(cols), 0.0, -jnp.inf).astype(wide)


def standardise(rows):
    centred = rows - jnp.mean(rows, axis=-1, keepdims=True)
    inv_spread = lax.rsqrt(jnp.mean(centred * centred, axis=-1, keepdims=True) + eps)
    return centred * inv_spread, inv_spread


def full(shape):
    return pl.BlockSpec(shape, lambda *steps: (0,) * len(shape))


def only(head, head_size, first, value):
    lane = lax.broadcasted_iota(jnp.int32, (1, value.shape[1]), 1) + first
    keep = (lane >= head * head_size) & (lane < (head + 1) * head_size)
    return value * jnp.where(keep, 1.0, 0.0).astype(low)


def head_products(out_ref, left_ref, right_t, head_size):
    row_count, width = left_ref.shape
    for first, heads in score_groups(head_size, width):
        window = left_ref[:, first : first + PART]
        stacked = jnp.concatenate(
            [only(head, head_size, first, window) for head in heads], axis=0
        )
        product = dot_nn(stacked, right_t[first : first + PART])
        for place, head in enumerate(heads):
            out_ref[head] = product[place * row_count : (place + 1) * row_count]


def head_sums(out_t_ref, weights_ref, value_ref, head_size):
    row_count, width = value_ref.shape
    for first, last, heads in value_groups(head_size, width):
        stacked = jnp.concatenate(
            [only(head, head_size, first, value_ref[:, first:last]) for head in heads], axis=0
        )
        lanes = slice(heads[0] * row_count, (heads[-1] + 1) * row_count)
        out_t_ref[first:last] = dot_nn(weights_ref[:, lanes], stacked).astype(low).T


def position():
    s, d = lax.axis_index("seq"), lax.axis_index("dp")
    return d % 2, d // 2, s % 2, s // 2


def relative_block(block):
    core, x_bit, y_bit, z_index = position()
    x_off, y_off = (block % 2) ^ x_bit, (block // 2 % 2) ^ y_bit
    z_off = (block // 4) ^ z_index
    return jnp.where(core == 0, y_off + 2 * x_off, x_off + 2 * y_off), z_off


def project_rows(patch_rows, gain, w_qkv):
    standard, _ = standardise(patch_rows.astype(wide))
    return dot_nn((standard * gain).astype(low), w_qkv).astype(low)


def attention_kernel(
    score_scale, head_size, relative, lengths_ref, q_ref, k_ref, v_ref,
    att_t_ref, lse_ref, keys_t, turned, bias, scores, probs,
):
    row_count, half_width = q_ref.shape
    heads = half_width // head_size
    half = pl.program_id(0)

    @pl.when(half == 0)
    def _():
        bias[...] = image_bias(lengths_ref, row_count)

    keys_t[...] = k_ref[...].T
    head_products(scores, q_ref, keys_t, head_size)
    lane = lax.broadcasted_iota(jnp.int32, (CHUNK, LANES), 1)
    for row in range(0, row_count, CHUNK):
        rows = slice(row, row + CHUNK)
        lse = jnp.zeros((CHUNK, LANES), wide)
        for head in range(heads):
            scaled = scores[head, rows] * (score_scale * LOG2_E) + bias[rows]
            row_max = jnp.max(scaled, axis=-1, keepdims=True)
            weights = jnp.exp2(scaled - row_max)
            total = jnp.sum(weights, axis=-1, keepdims=True)
            lanes = slice(head * row_count, (head + 1) * row_count)
            probs[rows, lanes] = (weights * (1.0 / total)).astype(low)
            lse = jnp.where(lane == head, row_max + jnp.log2(total), lse)
        lse_ref[0, rows] = lse
    head_sums(turned, probs, v_ref, head_size)
    for head in range(heads):
        block = turned[head * head_size : (head + 1) * head_size, :]
        number = half * heads + head
        if relative:
            near, far = relative_block(number)
            att_t_ref[near, far] = block
        else:
            att_t_ref[number] = block


def attention(shard_lengths, projected, far_count):
    row_count, model_width = projected.shape[0], projected.shape[1] // 3
    half_width = model_width // HALVES
    head_size = model_width // HEADS
    heads = HEADS // HALVES
    relative = 4 * far_count == HEADS
    shape = ((4, far_count) if relative else (HEADS,)) + (head_size, row_count)
    part = lambda kind: pl.BlockSpec(
        (row_count, half_width), lambda half: (0, kind * HALVES + half)
    )
    return pl.pallas_call(
        functools.partial(attention_kernel, 1.0 / math.sqrt(head_size), head_size, relative),
        grid=(HALVES,),
        in_specs=[smem(), part(0), part(1), part(2)],
        out_specs=[
            full(shape),
            pl.BlockSpec((1, row_count, LANES), lambda half: (half, 0, 0)),
        ],
        out_shape=[
            jax.ShapeDtypeStruct(shape, low),
            jax.ShapeDtypeStruct((HALVES, row_count, LANES), wide),
        ],
        scratch_shapes=[
            pltpu.VMEM((half_width, row_count), low),
            pltpu.VMEM((half_width, row_count), low),
            pltpu.VMEM((row_count, row_count), wide),
            pltpu.VMEM((heads, row_count, row_count), wide),
            pltpu.VMEM((row_count, heads * row_count), low),
        ],
        compiler_params=params(),
        cost_estimate=cost(1, 0),
        name="attention",
    )(shard_lengths, projected, projected, projected)


def attention_grad_kernel(
    score_scale, head_size, relative, copies_each,
    lengths_ref, x_ref, q_ref, k_ref, v_ref, lse_ref, ga_ref, w_hbm,
    normed_ref, gain_out_ref,
    ga, turned, bias, scores, grad_probs, probs, grad_scores, grads, w_buf, w_sems,
):
    row_count, half_width = ga.shape
    model_width = x_ref.shape[1]
    heads = half_width // head_size
    half = pl.program_id(0)
    w_copies = [
        pltpu.make_async_copy(
            w_hbm.at[part * PART : (part + 1) * PART],
            w_buf.at[part * PART : (part + 1) * PART],
            w_sems.at[part],
        )
        for part in range(model_width // PART)
    ]

    @pl.when(half == 0)
    def _():
        for copy in w_copies:
            copy.start()
        bias[...] = image_bias(lengths_ref, row_count)

    for head in range(heads):
        number = half * heads + head
        if relative:
            near, far = relative_block(number)
            number = near * (HEADS // 4) + far
        turned[2, head * head_size : (head + 1) * head_size] = ga_ref[number]
    ga[...] = turned[2].T
    turned[0] = k_ref[...].T
    turned[1] = v_ref[...].T
    head_products(scores, q_ref, turned.at[0], head_size)
    head_products(grad_probs, ga, turned.at[1], head_size)
    for row in range(0, row_count, CHUNK):
        rows = slice(row, row + CHUNK)
        lse = lse_ref[0, rows]
        for head in range(heads):
            scaled = scores[head, rows] * (score_scale * LOG2_E) + bias[rows]
            chance = jnp.exp2(scaled - lse[:, head : head + 1])
            incoming = grad_probs[head, rows]
            inner = jnp.sum(incoming * chance, axis=-1, keepdims=True)
            lanes = slice(head * row_count, (head + 1) * row_count)
            probs[rows, lanes] = chance.astype(low)
            grad_scores[rows, lanes] = (chance * (incoming - inner) * score_scale).astype(low)
    head_sums(grads.at[half, 0], grad_scores, k_ref, head_size)
    turned[0] = q_ref[...].T
    for head in range(heads):
        rows = slice(head * head_size, (head + 1) * head_size)
        lanes = slice(head * row_count, (head + 1) * row_count)
        grads[half, 1, rows] = dot_nn(turned[0, rows], grad_scores[:, lanes]).astype(low)
        grads[half, 2, rows] = dot_nn(turned[2, rows], probs[:, lanes]).astype(low)

    @pl.when(half == HALVES - 1)
    def _():
        parts = [(kind, half) for half in range(HALVES) for kind in range(3)]
        matrix = grads[...].reshape(3 * model_width, row_count)
        for part, copy in enumerate(w_copies):
            copy.wait()
            rows = slice(part * PART, (part + 1) * PART)
            columns = []
            for kind, side in parts:
                first = (kind * HALVES + side) * half_width
                columns.append(w_buf[rows, first : first + half_width])
            normed_ref[:, rows] = dot_nn(jnp.concatenate(columns, axis=1), matrix).T
        total = None
        for row in range(0, row_count, LANES):
            rows = slice(row, row + LANES)
            standard, _ = standardise(x_ref[rows].astype(wide))
            term = jnp.sum(normed_ref[rows] * standard, axis=0, keepdims=True)
            total = term if total is None else total + term
        share = gain_out_ref.shape[2]
        for number in range(model_width // share):
            term = total[:, number * share : (number + 1) * share]
            for copy in range(copies_each):
                gain_out_ref[number * copies_each + copy] = term


def attention_grad(
    shard_lengths, patch_rows, projected, lse, ga_t, w_qkv, relative, seq_count, dp_count
):
    row_count, model_width = patch_rows.shape
    half_width = model_width // HALVES
    head_size = model_width // HEADS
    heads = HEADS // HALVES
    part = lambda kind: pl.BlockSpec(
        (row_count, half_width), lambda half: (0, kind * HALVES + half)
    )
    shape = (HEADS, head_size, row_count)
    spread = (seq_count * dp_count, 1, model_width // seq_count)
    return pl.pallas_call(
        functools.partial(
            attention_grad_kernel, 1.0 / math.sqrt(head_size), head_size, relative, dp_count
        ),
        grid=(HALVES,),
        in_specs=[
            smem(),
            full(patch_rows.shape),
            part(0),
            part(1),
            part(2),
            pl.BlockSpec((1, row_count, LANES), lambda half: (half, 0, 0)),
            full(shape),
            pl.BlockSpec(memory_space=pl.ANY),
        ],
        out_specs=[full(patch_rows.shape), full(spread)],
        out_shape=[
            jax.ShapeDtypeStruct(patch_rows.shape, wide),
            jax.ShapeDtypeStruct(spread, wide),
        ],
        scratch_shapes=[
            pltpu.VMEM((row_count, half_width), low),
            pltpu.VMEM((3, half_width, row_count), low),
            pltpu.VMEM((row_count, row_count), wide),
            pltpu.VMEM((heads, row_count, row_count), wide),
            pltpu.VMEM((heads, row_count, row_count), wide),
            pltpu.VMEM((row_count, heads * row_count), low),
            pltpu.VMEM((row_count, heads * row_count), low),
            pltpu.VMEM((HALVES, 3, half_width, row_count), low),
            pltpu.VMEM(w_qkv.shape, low),
            pltpu.SemaphoreType.DMA((model_width // PART,)),
        ],
        compiler_params=params(2 * VMEM_LIMIT - VMEM_LIMIT // 8),
        cost_estimate=cost(1, 0),
        name="attention_grad",
    )(
        shard_lengths, patch_rows, projected, projected, projected, lse,
        ga_t.reshape(shape), w_qkv,
    )


def patch_grad_kernel(
    x_ref, gain_ref, grad_ref, bg_own_ref, bg_away_ref, merged_ref, patch_ref, merged_out_ref
):
    row_count, model_width = x_ref.shape
    half_width = model_width // HALVES
    core = position()[0]
    merged_out_ref[...] = merged_ref[...]
    for row in range(0, row_count, LANES):
        rows = slice(row, row + LANES)
        standard, inv_spread = standardise(x_ref[rows].astype(wide))
        grad = grad_ref[rows] * gain_ref[...]
        branch = inv_spread * (
            grad
            - jnp.mean(grad, axis=-1, keepdims=True)
            - standard * jnp.mean(grad * standard, axis=-1, keepdims=True)
        )
        for half in range(HALVES):
            cols = slice(half * half_width, (half + 1) * half_width)
            incoming = jnp.where(core == half, bg_own_ref[rows], bg_away_ref[rows])
            patch_ref[rows, cols] = (incoming.astype(wide) + branch[:, cols]).astype(low)


def patch_grads(patch_rows, gain, grad_normed, bg_own, bg_away, merged):
    args = (patch_rows, gain, grad_normed, bg_own, bg_away, merged)
    return pl.pallas_call(
        patch_grad_kernel,
        grid=(1,),
        in_specs=[full(arg.shape) for arg in args],
        out_specs=[full(patch_rows.shape), full(merged.shape)],
        out_shape=[
            jax.ShapeDtypeStruct(patch_rows.shape, low),
            jax.ShapeDtypeStruct(merged.shape, low),
        ],
        compiler_params=params(),
        cost_estimate=cost(1, 0),
        name="patch_grads",
    )(*args)


def placing_matrix(dest_ref, row_count):
    token_count = row_count // GROUP
    peer_count = token_count // lax.axis_size("seq")
    token_bits = token_count.bit_length() - 1
    dest = dest_ref[...]
    shard = lax.shift_right_logical(dest, jnp.full_like(dest, token_bits))
    slot = shard * peer_count + (dest & (peer_count - 1))
    square = (token_count, token_count)
    chosen = (lax.broadcasted_iota(jnp.int32, square, 0) == slot).astype(low)
    shape = (token_count, row_count)
    token = lax.broadcasted_iota(jnp.int32, shape, 0) * GROUP
    row = lax.broadcasted_iota(jnp.int32, shape, 1)
    parts = []
    for member in range(GROUP):
        spread = (row == token + member).astype(low)
        parts.append(dot_nn(chosen, spread).astype(low))
    return jnp.concatenate(parts, axis=0)


def place_kernel(dest_ref, returned_ref, own_ref, away_ref, stacked):
    token_count = returned_ref.shape[0]
    row_count, model_width = stacked.shape
    half_width = model_width // HALVES
    for member in range(GROUP):
        stacked[member * token_count : (member + 1) * token_count] = returned_ref[
            :, member * model_width : (member + 1) * model_width
        ]
    placing = placing_matrix(dest_ref, row_count)
    core = position()[0]
    for side, out_ref in enumerate((own_ref, away_ref)):
        cols = pl.ds(pl.multiple_of((core ^ side) * half_width, LANES), half_width)
        out_ref[...] = dot_tn(placing, stacked[:, cols]).astype(low)


def place_rows(token_dest, returned):
    token_count, merged_width = returned.shape
    row_count, model_width = token_count * GROUP, merged_width // GROUP
    half_width = model_width // HALVES
    return pl.pallas_call(
        place_kernel,
        grid=(1,),
        in_specs=[full(token_dest.shape), full(returned.shape)],
        out_specs=[full((row_count, half_width))] * 2,
        out_shape=[jax.ShapeDtypeStruct((row_count, half_width), low)] * 2,
        scratch_shapes=[pltpu.VMEM((row_count, model_width), low)],
        compiler_params=params(),
        cost_estimate=cost(1, 0),
        name="place_rows",
    )(token_dest, returned)


def project_kernel(dest_ref, x_ref, att_t_ref, bg_own_ref, bg_away_ref, *refs):
    own, away, (out_ref, ga_t_ref, attended) = refs[:4], refs[4:8], refs[8:]
    row_count, model_width = x_ref.shape
    half_width = model_width // HALVES
    token_count = row_count // GROUP
    placing = placing_matrix(dest_ref, row_count)
    core = position()[0]
    attended[...] = att_t_ref[...].T
    grad = None
    for side, (pieces, bg_ref) in enumerate(((own, bg_own_ref), (away, bg_away_ref))):
        matrix = jnp.concatenate([piece[...] for piece in pieces], axis=0)
        first = pl.multiple_of((core ^ side) * half_width, LANES)
        branch = dot_nn(attended[...], matrix)
        block = x_ref[:, pl.ds(first, half_width)].astype(wide) + branch
        tokens = dot_nn(placing, block.astype(low)).astype(low)
        for member in range(GROUP):
            place = pl.multiple_of(member * model_width + first, LANES)
            rows = slice(member * token_count, (member + 1) * token_count)
            out_ref[:, pl.ds(place, half_width)] = tokens[rows]
        term = dot_nt(matrix, bg_ref[...])
        grad = term if grad is None else grad + term
    ga_t_ref[...] = grad.astype(low)


def project(token_dest, patch_rows, att_t, bg_own, bg_away, own, away):
    row_count, model_width = patch_rows.shape
    args = (token_dest, patch_rows, att_t, bg_own, bg_away, *own, *away)
    shapes = [(row_count // GROUP, GROUP * model_width), (model_width, row_count)]
    return pl.pallas_call(
        project_kernel,
        grid=(1,),
        in_specs=[full(arg.shape) for arg in args],
        out_specs=[full(shape) for shape in shapes],
        out_shape=[jax.ShapeDtypeStruct(shape, low) for shape in shapes],
        scratch_shapes=[pltpu.VMEM((row_count, model_width), low)],
        compiler_params=params(),
        cost_estimate=cost(1, 0),
        name="project",
    )(*args)


def finish_kernel(
    norm_scale, own_ref, core_ref, x_ref, both_ref, gain_ref, out_ref, gain_out_ref
):
    core, x_bit, _, _ = position()
    rows, cols = own_ref.shape
    for x_off, pair in enumerate(((own_ref, core_ref), (x_ref, both_ref))):
        for core_off, piece in enumerate(pair):
            to_rows = pl.ds(pl.multiple_of((x_bit ^ x_off) * rows, rows), rows)
            to_cols = pl.ds(pl.multiple_of((core ^ core_off) * cols, LANES), cols)
            out_ref[to_rows, to_cols] = piece[...].astype(wide) * norm_scale
    gain_out_ref[...] = jnp.sum(gain_ref[...], axis=0) * norm_scale


def finish(held, gain_terms, norm_scale):
    rows, cols = held[0].shape
    share = gain_terms.shape[2]
    return pl.pallas_call(
        functools.partial(finish_kernel, norm_scale),
        grid=(1,),
        in_specs=[full(piece.shape) for piece in held] + [full(gain_terms.shape)],
        out_specs=[full((2 * rows, 2 * cols)), full((1, share))],
        out_shape=[
            jax.ShapeDtypeStruct((2 * rows, 2 * cols), wide),
            jax.ShapeDtypeStruct((1, share), wide),
        ],
        compiler_params=params(),
        cost_estimate=cost(1, 0),
        name="finish",
    )(*held, gain_terms)


def joint_permute(value, seq_count, dp_count, target):
    pairs = []
    for s in range(seq_count):
        for d in range(dp_count):
            to_s, to_d = target(s, d)
            pairs.append((s * dp_count + d, to_s * dp_count + to_d))
    return lax.ppermute(value, ("seq", "dp"), pairs)


def core_target(s, d):
    return s, d ^ 1


def first_target(s, d):
    return (s, d ^ 2) if d % 2 == 0 else (s ^ 1, d)


def second_target(s, d):
    return (s ^ 1, d) if d % 2 == 0 else (s, d ^ 2)


def both_target(s, d):
    return s ^ 1, d ^ 2


def far_target(step):
    return lambda s, d: (s ^ (2 * step), d)


def gather_far(place, w_out, seq_count, send):
    share, model_width = w_out.shape
    rows, cols = share // 2, model_width // 2
    core, x_bit = place[0], place[1]
    own = lax.dynamic_slice(w_out, (x_bit * rows, core * cols), (rows, cols))
    return [own] + [send(own, target=far_target(step)) for step in range(1, seq_count // 2)]


def to_relative(place, blocks, far_count):
    core, x_bit, y_bit, z_index = place
    width = blocks.shape[-1]
    blocks = blocks.reshape(far_count, 2, 2, -1, width)[jnp.arange(far_count) ^ z_index]
    blocks = jnp.where(y_bit == 0, blocks, blocks[:, ::-1])
    blocks = jnp.where(x_bit == 0, blocks, blocks[:, :, ::-1])
    x_first, y_first = blocks.transpose(2, 1, 0, 3, 4), blocks.transpose(1, 2, 0, 3, 4)
    return jnp.where(core == 0, x_first, y_first).reshape((4, far_count) + x_first.shape[3:])


def from_relative(place, blocks):
    core, x_bit, y_bit, z_index = place
    _, far_count, rows, width = blocks.shape
    blocks = blocks.reshape(2, 2, far_count, rows, width)
    y_first = blocks.transpose(2, 0, 1, 3, 4)
    blocks = jnp.where(core == 0, blocks.transpose(2, 1, 0, 3, 4), y_first)
    blocks = jnp.where(y_bit == 0, blocks, blocks[:, ::-1])
    blocks = jnp.where(x_bit == 0, blocks, blocks[:, :, ::-1])
    return blocks[jnp.arange(far_count) ^ z_index]


def together(*values):
    return lax.optimization_barrier(values)


def per_device(patches, lengths, token_dest, gain, w_qkv, w_out, cotangent):
    seq_count = lax.axis_size("seq")
    dp_count = lax.axis_size("dp")
    far_count = seq_count // 2
    send = functools.partial(joint_permute, seq_count=seq_count, dp_count=dp_count)
    place = position()
    patch_rows, shard_lengths = patches[0], lengths[0, 0]
    row_count, model_width = patch_rows.shape
    half_width = model_width // HALVES
    token_count = row_count // GROUP
    direct = 4 * far_count == HEADS

    far = gather_far(place, w_out, seq_count, send)
    projected = project_rows(patch_rows, gain, w_qkv)
    projected, cotangent, far = together(projected, cotangent, far)
    level = jnp.stack(far)
    returned = lax.all_to_all(cotangent[0], "seq", split_axis=0, concat_axis=0, tiled=True)
    att_t, lse = attention(shard_lengths, projected, far_count)
    if not direct:
        att_t = to_relative(place, att_t, far_count)
    near = send(level, target=second_target)
    beyond = send(level, target=first_target)
    corner = send(level, target=both_target)
    att_other = send(att_t, target=core_target)
    bg_own, bg_away = place_rows(token_dest, returned)
    bg_other = send(bg_away, target=core_target)
    bg_other, att_other, near, beyond, corner = together(
        bg_other, att_other, near, beyond, corner
    )
    level_core = send(level, target=core_target)
    near_core = send(near, target=core_target)
    beyond_core = send(beyond, target=core_target)
    corner_core = send(corner, target=core_target)

    merge = lambda piece: piece.reshape(-1, piece.shape[-1])
    terms = []
    for first in (1, 0):
        mine = merge(att_t[2 * first : 2 * first + 2])
        other = jnp.concatenate([merge(att_other[first]), merge(att_other[first + 2])])
        term = dot_nn(mine, bg_own) + dot_nn(other, bg_other)
        terms.append(term.astype(low).reshape(2, far_count, -1, half_width))
    arrived = [
        send(terms[1][1], target=second_target),
        send(terms[0][0], target=first_target),
        send(terms[0][1], target=both_target),
    ]
    kept = terms[1][0]
    own = [merge(piece) for piece in (level, near, beyond, corner)]
    away = [merge(piece) for piece in (level_core, beyond_core, near_core, corner_core)]
    outgoing, ga_t = project(
        token_dest, patch_rows, merge(att_t), bg_own, bg_away, own, away
    )
    merged = lax.all_to_all(
        outgoing.reshape(seq_count, token_count // seq_count, GROUP * model_width),
        "seq", split_axis=0, concat_axis=0, tiled=True,
    ).reshape(token_count, GROUP * model_width)
    if not direct:
        ga_t = from_relative(place, ga_t.reshape(4, far_count, -1, row_count))
    grad_normed, gain_terms = attention_grad(
        shard_lengths, patch_rows, projected, lse, ga_t, w_qkv, direct, seq_count, dp_count
    )
    grad_normed, gain_terms, arrived = together(grad_normed, gain_terms, arrived)
    level = sum(term.astype(wide) for term in [kept, *arrived]).astype(low)
    weight_terms = [level[0]] + [
        send(level[step], target=far_target(step)) for step in range(1, far_count)
    ]
    gain_arrived = lax.all_to_all(
        gain_terms, ("seq", "dp"), split_axis=0, concat_axis=0, tiled=True
    )
    patch_grad, merged = patch_grads(patch_rows, gain, grad_normed, bg_own, bg_away, merged)
    total = sum(term.astype(wide) for term in weight_terms).astype(low)
    held = [total, send(total, target=core_target)]
    held += [send(total, target=lambda s, d, flip=flip: (s, d ^ flip)) for flip in (2, 3)]
    norm_scale = 1.0 / math.sqrt(row_count * seq_count * dp_count)
    if direct:
        own_weight, own_gain = finish(held, gain_arrived, norm_scale)
        own_gain = own_gain[0]
    else:
        rows = total.shape[0]
        held = jnp.stack(held).reshape(2, 2, rows, half_width)
        held = jnp.where(place[1] == 0, held, held[::-1])
        held = jnp.where(place[0] == 0, held, held[:, ::-1])
        held = held.astype(wide).transpose(0, 2, 1, 3)
        own_weight = held.reshape(2 * rows, model_width) * norm_scale
        own_gain = jnp.sum(gain_arrived, axis=(0, 1)) * norm_scale
    return (merged[None], patch_grad[None], own_weight, own_gain)


def solution(mesh):
    placed = (
        P("dp", "seq", None),
        P("dp", "seq", None),
        P("dp", "seq"),
        P(),
        P(),
        P("seq", None),
        P("dp", "seq", None),
    )
    return jax.shard_map(
        per_device,
        mesh=mesh,
        in_specs=placed,
        out_specs=(P("dp", "seq", None), P("dp", "seq", None), P("seq", None), P("seq")),
        check_vma=False,
    )
```
